256 devices in a mesh: span: 32 (over x, z), plane: 8 (over y, core).
Axes of the slice: x: 4, y: 4, z: 8, core: 2. Of those that a mesh axis runs over, the one named last changes fastest.
Arguments:
- rhs: float32 [80, 8192], P(None, ('span', 'plane')), may hold values from -6 to 6
- blocks: float32 [8192, 70400], P(('span', 'plane')), as said below
- columns: int32 [11, 8192], P(None, ('span', 'plane')), may hold values from 0 to 8191, as said below
- line_slot: int32 [256, 32], P(('span', 'plane')), may hold values from 0 to 31, each once within a row
- line_lower: float32 [8192, 6400], P(('span', 'plane')), may hold values from -0.2 to 0.2
- line_upper: float32 [8192, 6400], P(('span', 'plane')), may hold values from -0.2 to 0.2
- pivot_inv: float32 [8192, 6400], P(('span', 'plane')), as said below
Outputs:
- solution: float32 [80, 8192], P(None, ('span', 'plane'))
- residual: float32 [80, 8192], P(None, ('span', 'plane'))
The draws below stay inside these ranges and needn't reach their ends.
Inputs may be any that keep to these rules, and one draw needn't show every extreme that they name: columns[0, i] = i; the other columns name faces on the device itself, on the devices one step along span (wrapping) or one step along plane (not wrapping). Blocks 1 to 4 name faces on the span devices after and before and the plane devices after and before, or on the device itself where no such plane device exists. pivot_inv is a diagonal with entries between about 0.5 and 2.0 plus a full-rank off-diagonal part of small entries. `blocks`: block 0 of every row has an added diagonal of 1 to about 4.06.
All inputs are finite; a program needn't handle non-finite values.
Results may differ from the reference program's by a relative error of at most 0.0065.
Values sent between devices are 32-bit elements; how exact they have to be, the bound alone decides.
A program may use at most 128 MiB of HBM per device.

```python
import jax
import jax.numpy as jnp
from jax import lax

B = 80
NBLK = 11
ITERS = 3
P_SIZE = 2
LPD = 2
F = 32
LEN = 16
NFACES = 8192
LINES = 512
N_SPAN = 32
N_PLANE = 8
DEVICES = 256


def draw_blocks(key, part):
    key = jax.random.fold_in(key, 11)
    key_noise, key_diag = jax.random.split(key, 2)
    noise = jax.random.normal(key_noise, (NFACES, NBLK, B, B), jnp.float32)
    noise = noise * (0.35 / (B * NBLK) ** 0.5)
    diag = jnp.exp(jax.random.uniform(key_diag, (NFACES, B), jnp.float32, 0.0, 1.4))
    eye = jnp.eye(B, dtype=jnp.float32)[None, :, :] * diag[:, :, None]
    return noise.at[:, 0].add(eye).reshape(NFACES, NBLK * B * B)


def draw_columns(key, part):
    key = jax.random.fold_in(key, 23)
    key_dir, key_loc = jax.random.split(key)
    faces = jnp.arange(NFACES, dtype=jnp.int32)
    device = faces // F
    span_idx = device // N_PLANE
    plane_idx = device % N_PLANE
    fixed_dir = jnp.array([0, 1, 2, 3, 4, 0, 0, 0, 0, 0, 0], jnp.int32)[:NBLK]
    rand_dir = jax.random.randint(key_dir, (NBLK, NFACES), 0, 5)
    slot_k = jnp.arange(NBLK, dtype=jnp.int32)[:, None]
    direction = jnp.where(slot_k < 5, fixed_dir[:, None], rand_dir)
    dspan = jnp.where(direction == 1, 1, jnp.where(direction == 2, -1, 0))
    dplane = jnp.where(direction == 3, 1, jnp.where(direction == 4, -1, 0))
    span_new = (span_idx[None, :] + dspan + N_SPAN) % N_SPAN
    plane_new = plane_idx[None, :] + dplane
    plane_new = jnp.where((plane_new < 0) | (plane_new >= N_PLANE), plane_idx[None, :], plane_new)
    local = jax.random.randint(key_loc, (NBLK, NFACES), 0, F)
    target = (span_new * N_PLANE + plane_new) * F + local
    return jnp.where(slot_k == 0, faces[None, :], target).astype(jnp.int32)


def draw_pivot_inv(key, part):
    key = jax.random.fold_in(key, 37)
    key_noise, key_diag = jax.random.split(key)
    count = LINES * LEN
    noise = jax.random.normal(key_noise, (count, B, B), jnp.float32)
    noise = noise * (0.3 / B ** 0.5)
    diag = jnp.exp(jax.random.uniform(key_diag, (count, B), jnp.float32, -0.7, 0.7))
    eye = jnp.eye(B, dtype=jnp.float32)[None, :, :] * diag[:, :, None]
    return (noise + eye).reshape(count, B * B)


def levels(own_key, shape, cuts, least, high):
    def one(axis_at, shards_of):
        steps = jax.random.uniform(jax.random.fold_in(jax.random.fold_in(own_key, 6), axis_at), (shards_of,), jnp.float32, least / len(cuts), high / len(cuts))
        return jnp.repeat(jnp.exp(steps), shape[axis_at] // shards_of).reshape((-1,) + (1,) * (len(shape) - axis_at - 1))

    loudness = one(*cuts[0])
    for cut in cuts[1:]:
        loudness = loudness * one(*cut)
    return loudness


def bell_draw(key, dims, deviation, limit, cuts=(), kind=jnp.bfloat16):
    loudness = levels(key, dims, cuts, -0.22, 0.18) if cuts else 1.0
    values = jax.random.normal(key, dims, jnp.float32) * deviation * loudness
    return jnp.minimum(jnp.maximum(values, -limit), limit).astype(kind)


def setup_inputs(seed: int = 0) -> dict:
    seeds = jax.random.split(jax.random.key(seed), 8)
    rhs = bell_draw(seeds[0], (B, NFACES), 1.0, 6.0, ((1, 256),), jnp.float32)
    blocks = draw_blocks(jax.random.fold_in(seeds[7], 71), 0)
    columns = draw_columns(jax.random.fold_in(seeds[7], 71), 0)
    line_slot = jax.vmap(lambda own: jax.random.permutation(own, F))(jax.random.split(seeds[3], DEVICES)).reshape((DEVICES, F)).astype(jnp.int32)
    line_lower = bell_draw(seeds[4], (LINES * LEN, B * B), 0.03, 0.2, ((0, 256),), jnp.float32)
    line_upper = bell_draw(seeds[5], (LINES * LEN, B * B), 0.03, 0.2, ((0, 256),), jnp.float32)
    pivot_inv = draw_pivot_inv(jax.random.fold_in(seeds[7], 71), 0)
    return dict(rhs=rhs, blocks=blocks, columns=columns, line_slot=line_slot, line_lower=line_lower, line_upper=line_upper, pivot_inv=pivot_inv)


HIGH = lax.Precision.HIGHEST

def small_solve(factor, target):
    extent = target.shape[0]
    forward_vals = []
    for row in range(extent):
        running = target[row]
        for inner in range(row):
            running = running - factor[row, inner] * forward_vals[inner]
        forward_vals.append(running / factor[row, row])
    backward_vals = [None] * extent
    for row in reversed(range(extent)):
        running = forward_vals[row]
        for inner in range(row + 1, extent):
            running = running - factor[inner, row] * backward_vals[inner]
        backward_vals[row] = running / factor[row, row]
    return jnp.stack(backward_vals)

def to_sequence(factor_rows, nlines, length, width):
    return jnp.swapaxes(factor_rows.reshape(nlines, length, width, width), 0, 1)

def line_solve(rhs_lines, lseq, useq, pseq):
    rseq = jnp.moveaxis(rhs_lines, 2, 0)

    def forward(prev, items):
        right, low = items
        cur = right - jnp.einsum('mab,bm->am', low, prev, precision=HIGH)
        return (cur, cur)
    start = jnp.zeros(rseq.shape[1:], jnp.float32)
    _, yseq = lax.scan(forward, start, (rseq, lseq))

    def backward(nxt, items):
        yval, upp, piv = items
        inner = yval - jnp.einsum('mab,bm->am', upp, nxt, precision=HIGH)
        cur = jnp.einsum('mab,bm->am', piv, inner, precision=HIGH)
        return (cur, cur)
    _, zseq = lax.scan(backward, start, (yseq, useq, pseq), reverse=True)
    return jnp.moveaxis(zseq, 0, 2)

def reference(rhs, blocks, columns, line_slot, line_lower, line_upper, pivot_inv):
    nlines_group = LPD * N_PLANE
    devs = jnp.arange(DEVICES, dtype=jnp.int32)[:, None]
    slots = jnp.arange(F, dtype=jnp.int32)[None, :]
    span_idx = devs // N_PLANE
    plane_idx = devs % N_PLANE
    gline = span_idx * nlines_group + slots // P_SIZE + 0 * plane_idx
    gpos = plane_idx * P_SIZE + slots % P_SIZE
    faces = devs * F + line_slot
    face_of = jnp.zeros((LINES, LEN), jnp.int32).at[gline.ravel(), gpos.ravel()].set(faces.ravel())
    lower = to_sequence(line_lower, LINES, LEN, B)
    upper = to_sequence(line_upper, LINES, LEN, B)
    pivot = to_sequence(pivot_inv, LINES, LEN, B)
    shaped_blocks = blocks.reshape(NFACES, NBLK, B, B)

    def apply_a(vec):
        picked = vec[:, columns]
        return jnp.einsum('ikab,bki->ai', shaped_blocks, picked, precision=HIGH)

    def apply_m(vec):
        sol = line_solve(vec[:, face_of], lower, upper, pivot)
        return jnp.zeros_like(vec).at[:, face_of].set(sol)
    beta = jnp.sqrt(jnp.sum(rhs * rhs) + 1e-06)
    basis = [rhs / beta]
    hcols = []
    for step in range(ITERS):
        wvec = apply_a(apply_m(basis[step]))
        stacked = jnp.stack(basis)
        hvals = jnp.einsum('jai,ai->j', stacked, wvec, precision=HIGH)
        wvec = wvec - jnp.einsum('j,jai->ai', hvals, stacked, precision=HIGH)
        hnext = jnp.sqrt(jnp.sum(wvec * wvec) + 1e-06)
        basis.append(wvec / hnext)
        hcols.append(jnp.concatenate([hvals, hnext[None], jnp.zeros((ITERS - step - 1,), jnp.float32)]))
    hmat = jnp.stack(hcols, axis=1)
    gram_mat = jnp.dot(hmat.T, hmat, precision=HIGH)
    target = beta * hmat[0]
    factor = jnp.linalg.cholesky(gram_mat)
    coef = small_solve(factor, target)
    update = jnp.einsum('j,jai->ai', coef, jnp.stack(basis[:ITERS]), precision=HIGH)
    solution = apply_m(update)
    residual = rhs - apply_a(solution)
    return (solution, residual)
```

```python
import functools

import jax
import jax.numpy as jnp
from jax import lax
from jax.experimental import pallas as pl
from jax.experimental.pallas import tpu as pltpu
from jax.sharding import PartitionSpec as P

MESH = pl.DeviceIdType.MESH
F32 = jnp.float32
BF16 = jnp.bfloat16

B = 80
NBLK = 11
ITERS = 3
F = 32
W = 128
SEG = 640
NGRP = 10
PAIRS = [(i, j) for i in range(4) for j in range(i, 4)]


def iota(shape, axis):
    return lax.broadcasted_iota(jnp.int32, shape, axis)


def split(x):
    hi = x.astype(BF16)
    lo = (x - hi.astype(F32)).astype(BF16)
    return hi, lo


def bdot(a, b):
    return jnp.dot(a, b, preferred_element_type=F32)


def pad_lanes(x):
    return jnp.concatenate([x, jnp.zeros((x.shape[0], W - x.shape[1]), x.dtype)], axis=1)


def small_solve(factor, target):
    extent = len(target)
    forward_vals = []
    for row in range(extent):
        running = target[row]
        for inner in range(row):
            running = running - factor[row][inner] * forward_vals[inner]
        forward_vals.append(running / factor[row][row])
    backward_vals = [None] * extent
    for row in reversed(range(extent)):
        running = forward_vals[row]
        for inner in range(row + 1, extent):
            running = running - factor[inner][row] * backward_vals[inner]
        backward_vals[row] = running / factor[row][row]
    return backward_vals


def coefficients(gram):
    def inner(c, d):
        out = None
        for i in range(len(c)):
            for j in range(len(d)):
                term = c[i] * d[j] * gram[min(i, j), max(i, j)]
                out = term if out is None else out + term
        return out

    beta = jnp.sqrt(gram[0, 0] + 1e-6)
    zero = jnp.zeros_like(beta)
    basis = [[1.0 / beta]]
    h = [[zero] * ITERS for _ in range(ITERS + 1)]
    for step in range(ITERS):
        w = [zero] + basis[step]
        for i in range(step + 1):
            h[i][step] = inner(basis[i], w)
        for i in range(step + 1):
            for n, c in enumerate(basis[i]):
                w[n] = w[n] - h[i][step] * c
        h[step + 1][step] = jnp.sqrt(jnp.maximum(inner(w, w), 0.0) + 1e-6)
        basis.append([c / h[step + 1][step] for c in w])
    normal = [
        [sum(h[n][i] * h[n][j] for n in range(min(i, j) + 2)) for j in range(ITERS)]
        for i in range(ITERS)
    ]
    target = [beta * h[0][j] for j in range(ITERS)]
    factor = [[None] * ITERS for _ in range(ITERS)]
    for j in range(ITERS):
        diag = normal[j][j]
        for n in range(j):
            diag = diag - factor[j][n] * factor[j][n]
        factor[j][j] = jnp.sqrt(diag)
        for i in range(j + 1, ITERS):
            below = normal[i][j]
            for n in range(j):
                below = below - factor[i][n] * factor[j][n]
            factor[i][j] = below / factor[j][j]
    y = small_solve(factor, target)
    out = []
    for n in range(ITERS):
        out.append(sum(y[j] * basis[j][n] for j in range(n, ITERS)))
    return out


def kernel(
    rhs_ref, blocks_hbm, columns_ref, slot_ref, slot_smem, low_hbm, upp_hbm, piv_hbm,
    sol_ref, res_ref,
    blk, flat, tall, lm, pm, pum, kf, zf, rsend, rrecv, zsend, trecv, gid, onehot,
    thi, tlo, smat, square, ga, gb,
    load_sem, rsend_sem, rrecv_sem, zsend_sem, tplane_sem, tspan_sem, gsend_sem, grecv_sem,
    gas_sem, gar_sem, gbs_sem, gbr_sem,
):
    nspan, nplane = 32, 8
    s = lax.axis_index("span")
    p = lax.axis_index("plane")
    x, z = s // 8, s % 8
    s_next, s_prev = lax.rem(s + 1, nspan), lax.rem(s + nspan - 1, nspan)
    p_next, p_prev = lax.rem(p + 1, nplane), lax.rem(p + nplane - 1, nplane)

    def plane_at(i):
        return lax.rem(p + i, nplane)

    loads = []
    for n, src in enumerate((low_hbm, piv_hbm, upp_hbm)):
        loads.append(pltpu.make_async_copy(src, flat.at[n], load_sem.at[n]))
    for n in range(4):
        loads.append(
            pltpu.make_async_copy(
                blocks_hbm.at[pl.ds(8 * n, 8)], blk.at[pl.ds(8 * n, 8)], load_sem.at[3 + n]
            )
        )
    for load in loads:
        load.start()

    barrier = pltpu.get_barrier_semaphore()

    def span_partner(i):
        xx = lax.rem(x + i // 4, 4)
        zz = lax.rem(z + 2 * (i % 4), 8)
        return xx * 8 + zz

    def greet(device):
        pl.semaphore_signal(barrier, inc=1, device_id=device, device_id_type=MESH)

    for i in range(1, nplane):
        greet((s, plane_at(i)))
    for i in range(nplane):
        greet((s_next, plane_at(i)))
        greet((s_prev, plane_at(i)))
    for i in range(1, 16):
        greet((span_partner(i), p))

    k0 = pad_lanes(jnp.transpose(rhs_ref[...]))
    kf[0] = k0

    lane = iota((1, W), 1)
    def to_slots(it):
        for t in range(F):
            rsend[it, t // 4, pl.ds(t % 4, 1), :] = kf[it, pl.ds(slot_smem[0, t], 1), :]

    to_slots(0)
    mine = pad_lanes(slot_ref[...].astype(F32)) + ((s * nplane + p) * F).astype(F32)
    gid[0] = jnp.broadcast_to(mine, (8, W))

    pl.semaphore_wait(barrier, 7 + 16 + 15)

    def send_pieces(it):
        for i in range(1, nplane):
            to = plane_at(i)
            pltpu.make_async_remote_copy(
                src_ref=rsend.at[it, to], dst_ref=rrecv.at[it, p],
                send_sem=rsend_sem.at[it], recv_sem=rrecv_sem.at[it],
                device_id=(s, to), device_id_type=MESH,
            ).start()
        pltpu.make_async_copy(rsend.at[it, p], rrecv.at[it, p], rrecv_sem.at[it]).start()

    send_pieces(0)
    gid_copies = []
    for n, to in enumerate(((s, p_next), (s, p_prev), (s_next, p), (s_prev, p))):
        copy = pltpu.make_async_remote_copy(
            src_ref=gid.at[0], dst_ref=gid.at[n + 1],
            send_sem=gsend_sem.at[n], recv_sem=grecv_sem.at[n],
            device_id=to, device_id_type=MESH,
        )
        copy.start()
        gid_copies.append(copy)

    for n in range(3):
        loads[n].wait()

    def relayout(g, _):
        for n in range(3):
            chunk = flat[n, :, pl.ds(pl.multiple_of(g * SEG, W), SEG)]
            for a in range(8):
                tall[n, pl.ds(pl.multiple_of((g * 8 + a) * F, F), F), :] = pad_lanes(
                    chunk[:, a * B : (a + 1) * B]
                )
        return 0

    lax.fori_loop(0, NGRP, relayout, 0)

    zeros48 = jnp.zeros((W - B, W), F32)

    def flip(m):
        return jnp.transpose(jnp.concatenate([m, zeros48], axis=0))[:B]

    def prepare(c, _):
        for q in range(2):
            row = 2 * c + q

            def matrix(n):
                return tall[n, pl.ds(row, B, stride=F), :]

            low, piv, upp = matrix(0), matrix(1), matrix(2)
            ph, pl_ = split(piv[:, :B])
            uh, ul = split(upp)
            both = bdot(ph, uh) + (bdot(ph, ul) + bdot(pl_, uh))
            if q == 0:
                lm[row], pm[row], pum[row] = flip(low), piv, both
            else:
                lm[row], pm[row], pum[row] = low, flip(piv), flip(both)
        return 0

    lax.fori_loop(0, F // 2, prepare, 0)

    square[...] = jnp.zeros_like(square)
    for it in range(ITERS):
        zsend[it, 0] = jnp.zeros((4, W), F32)
        zsend[it, nplane + 1] = jnp.zeros((4, W), F32)
    thi[...] = jnp.zeros_like(thi)
    tlo[...] = jnp.zeros_like(tlo)
    smat[...] = (iota((SEG, W), 0) // B == iota((SEG, W), 1)).astype(F32).astype(BF16)

    for copy in gid_copies:
        copy.wait()
    below = jnp.where(p == 0, -1.0, gid[1])
    above = jnp.where(p == nplane - 1, -1.0, gid[2])
    rows = [below[0:1], gid[0][0:1], above[0:1], gid[3][0:1], gid[4][0:1]]
    stacked = jnp.concatenate(rows + [jnp.zeros((W - 5, W), F32)], axis=0)
    by_slot = jnp.transpose(stacked)[:F]
    n_at = iota((F, 2 * W), 1)
    blk_at = n_at // 4
    span_part = n_at >= 96
    dir_at = jnp.where(span_part, 3 + (blk_at - 24) // 8, blk_at % 3)
    slot_at = jnp.where(span_part, (n_at - 96) % F, (blk_at // 3) * 4 + n_at % 4)
    want = iota((F, 2 * W), 0) == slot_at
    numbers = jnp.zeros((F, 2 * W), F32)
    for d in range(5):
        numbers = numbers + jnp.where(want & (dir_at == d), by_slot[:, d : d + 1], 0.0)
    numbers = jnp.sum(numbers, axis=0, keepdims=True)
    numbers = jnp.where(iota((1, 2 * W), 1) < 160, numbers, -2.0)
    cols = jnp.transpose(
        jnp.concatenate(
            [pad_lanes(columns_ref[...].astype(F32)), jnp.zeros((W - NBLK, W), F32)], axis=0
        )
    )[:F]
    for g in range(4):
        for k in range(NBLK):
            onehot[pl.ds(g * 88 + k * 8, 8), :] = (
                cols[g * 8 : g * 8 + 8, k : k + 1] == numbers
            ).astype(F32)

    def one(it, _):
        pltpu.make_async_copy(rrecv.at[it], rrecv.at[it], rrecv_sem.at[it]).wait()
        for m in range(2):
            for c in range(8):
                square[pl.ds(m * 8 + c, 1), :] = rrecv[it, c, pl.ds(2 * m + 1, 1), :]
        odd = jnp.transpose(square[...])[:B]
        ys = [[], []]
        for j in range(16):
            for m in range(2):
                row = m * 16 + j
                if j == 0:
                    ys[m].append(rrecv[it, 0, pl.ds(2 * m, 1), :])
                elif j % 2:
                    idx = m * 8 + j // 2
                    base = jnp.where(lane == idx, odd, 0.0)
                    ys[m].append(
                        jnp.sum(base - lm[row] * ys[m][j - 1], axis=1, keepdims=True)
                    )
                else:
                    r = rrecv[it, j // 2, pl.ds(2 * m, 1), :]
                    ys[m].append(r - jnp.sum(lm[row] * ys[m][j - 1], axis=0, keepdims=True))
        zs = [None, None]
        even = jnp.zeros((B, W), F32)
        for j in reversed(range(16)):
            for m in range(2):
                row = m * 16 + j
                term = pm[row] * ys[m][j]
                if j < 15:
                    term = term - pum[row] * zs[m]
                zs[m] = jnp.sum(term, axis=j % 2 == 0 and 1 or 0, keepdims=True)
                if j % 2:
                    zsend[it, j // 2 + 1, pl.ds(2 * m + 1, 1), :] = zs[m]
                else:
                    even = jnp.where(lane == m * 8 + j // 2, zs[m], even)
        even = jnp.transpose(jnp.concatenate([even, zeros48], axis=0))
        for m in range(2):
            for c in range(8):
                zsend[it, c + 1, pl.ds(2 * m, 1), :] = even[m * 8 + c : m * 8 + c + 1]

        for i in range(nplane):
            to = plane_at(i)
            for n, there in enumerate((s_next, s_prev)):
                pltpu.make_async_remote_copy(
                    src_ref=zsend.at[it, to + 1], dst_ref=trecv.at[it, 24 + 8 * n + p],
                    send_sem=zsend_sem.at[it], recv_sem=tspan_sem.at[it],
                    device_id=(there, to), device_id_type=MESH,
                ).start()
        for i in range(1, nplane):
            to = plane_at(i)
            pltpu.make_async_remote_copy(
                src_ref=zsend.at[it, pl.ds(to, 3)], dst_ref=trecv.at[it, pl.ds(3 * p, 3)],
                send_sem=zsend_sem.at[it], recv_sem=tplane_sem.at[it],
                device_id=(s, to), device_id_type=MESH,
            ).start()
        pltpu.make_async_copy(
            zsend.at[it, pl.ds(p, 3)], trecv.at[it, pl.ds(3 * p, 3)], tplane_sem.at[it]
        ).start()

        part = trecv.at[it, pl.ds(0, 24)]
        pltpu.make_async_copy(part, part, tplane_sem.at[it]).wait()
        part = trecv.at[it, pl.ds(24, 16)]
        pltpu.make_async_copy(part, part, tspan_sem.at[it]).wait()

        got = trecv[it].reshape(160, W)[:, :B]
        wide = jnp.concatenate([got] * 8, axis=1)
        hi, lo = split(wide)
        thi[pl.ds(0, 160), :] = hi
        tlo[pl.ds(0, 160), :] = lo

        def faces(g, _):
            @pl.when(it == 0)
            def _():
                part = blk.at[pl.ds(pl.multiple_of(8 * g, 8), 8)]
                pltpu.make_async_copy(part, part, load_sem.at[3 + g]).wait()

            at = pl.ds(pl.multiple_of(8 * g, 8), 8)
            oh = onehot[pl.ds(pl.multiple_of(88 * g, 8), 88), :].astype(BF16)
            picked = bdot(oh, thi[...]) + bdot(oh, tlo[...])
            zf[it, at, :] = picked[:8, :W]
            sums = []
            for half in range(2):
                acc = None
                for k in range(NBLK):
                    term = blk[at, pl.ds(k * 6400 + half * 3200, 3200)] * jnp.concatenate(
                        [picked[8 * k : 8 * k + 8]] * 5, axis=1
                    )
                    acc = term if acc is None else acc + term
                sums += [acc[:, n * SEG : (n + 1) * SEG] for n in range(5)]
            hi, lo = split(jnp.concatenate(sums, axis=0))
            out = bdot(hi, smat[...]) + bdot(lo, smat[...])
            total = out[:8]
            for n in range(1, NGRP):
                total = total + pltpu.roll(out[8 * n : 8 * n + 8], 8 * n, 1)
            kf[it + 1, at, :] = total
            return 0

        lax.fori_loop(0, 4, faces, 0)

        @pl.when(it < ITERS - 1)
        def _():
            for t in range(F):
                rsend[it + 1, t // 4, pl.ds(t % 4, 1), :] = kf[
                    it + 1, pl.ds(slot_smem[0, t], 1), :
                ]
            send_pieces(it + 1)

        return 0

    lax.fori_loop(0, ITERS, one, 0)

    ks = [kf[i] for i in range(4)]
    place = iota((16, W), 0)
    tile = jnp.zeros((16, W), F32)
    for n, (i, j) in enumerate(PAIRS):
        prod = jnp.sum(jnp.sum(ks[i] * ks[j], axis=0, keepdims=True), axis=1, keepdims=True)
        tile = jnp.where(place == n, prod, tile)
    ga[0] = tile
    z_pair = z + 1 - 2 * lax.rem(z, 2)
    s_pair = x * 8 + z_pair
    for i in range(1, 16):
        to = (s, plane_at(i)) if i < 8 else (s_pair, plane_at(i - 8))
        pltpu.make_async_remote_copy(
            src_ref=ga.at[0], dst_ref=ga.at[i],
            send_sem=gas_sem.at[0], recv_sem=gar_sem.at[0],
            device_id=to, device_id_type=MESH,
        ).start()
    arrived = ga.at[pl.ds(1, 15)]
    pltpu.make_async_copy(arrived, arrived, gar_sem.at[0]).wait()
    gb[0] = jnp.sum(ga[...], axis=0)
    for i in range(1, 16):
        pltpu.make_async_remote_copy(
            src_ref=gb.at[0], dst_ref=gb.at[i],
            send_sem=gbs_sem.at[0], recv_sem=gbr_sem.at[0],
            device_id=(span_partner(i), p), device_id_type=MESH,
        ).start()
    arrived_b = gb.at[pl.ds(1, 15)]
    pltpu.make_async_copy(arrived_b, arrived_b, gbr_sem.at[0]).wait()
    whole = jnp.sum(gb[...], axis=0)
    gram = {pair: whole[n : n + 1] for n, pair in enumerate(PAIRS)}
    coef = coefficients(gram)
    solved = sum(coef[i] * zf[i] for i in range(ITERS))
    left = ks[0] - sum(coef[i] * ks[i + 1] for i in range(ITERS))
    sol_ref[...] = jnp.transpose(solved)[:B]
    res_ref[...] = jnp.transpose(left)[:B]

    pltpu.make_async_copy(arrived, arrived, gas_sem.at[0]).wait()
    pltpu.make_async_copy(arrived_b, arrived_b, gbs_sem.at[0]).wait()
    for it in range(ITERS):
        out = rsend.at[it, pl.ds(0, 7)]
        pltpu.make_async_copy(out, out, rsend_sem.at[it]).wait()
        out = trecv.at[it, pl.ds(0, 37)]
        pltpu.make_async_copy(out, out, zsend_sem.at[it]).wait()


def on_device(rhs, blocks, columns, line_slot, line_lower, line_upper, pivot_inv):
    vmem = pl.BlockSpec(memory_space=pltpu.VMEM)
    hbm = pl.BlockSpec(memory_space=pl.ANY)
    out = jax.ShapeDtypeStruct((B, F), F32)
    dma = pltpu.SemaphoreType.DMA
    return pl.pallas_call(
        kernel,
        out_shape=(out, out),
        in_specs=[vmem, hbm, vmem, vmem, pl.BlockSpec(memory_space=pltpu.SMEM), hbm, hbm, hbm],
        out_specs=(vmem, vmem),
        scratch_shapes=[
            pltpu.VMEM((F, NBLK * B * B), F32),
            pltpu.VMEM((3, F, B * B), F32),
            pltpu.VMEM((3, B * F, W), F32),
            pltpu.VMEM((F, B, W), F32),
            pltpu.VMEM((F, B, W), F32),
            pltpu.VMEM((F, B, W), F32),
            pltpu.VMEM((ITERS + 1, F, W), F32),
            pltpu.VMEM((ITERS, F, W), F32),
            pltpu.VMEM((ITERS, 8, 4, W), F32),
            pltpu.VMEM((ITERS, 8, 4, W), F32),
            pltpu.VMEM((ITERS, 10, 4, W), F32),
            pltpu.VMEM((ITERS, 40, 4, W), F32),
            pltpu.VMEM((5, 8, W), F32),
            pltpu.VMEM((4 * 88, 2 * W), F32),
            pltpu.VMEM((2 * W, SEG), BF16),
            pltpu.VMEM((2 * W, SEG), BF16),
            pltpu.VMEM((SEG, W), BF16),
            pltpu.VMEM((W, W), F32),
            pltpu.VMEM((16, 16, W), F32),
            pltpu.VMEM((16, 16, W), F32),
            dma((7,)),
            dma((ITERS,)),
            dma((ITERS,)),
            dma((ITERS,)),
            dma((ITERS,)),
            dma((ITERS,)),
            dma((4,)),
            dma((4,)),
            dma((1,)),
            dma((1,)),
            dma((1,)),
            dma((1,)),
        ],
        compiler_params=pltpu.CompilerParams(
            collective_id=0, has_side_effects=True, vmem_limit_bytes=48 * 1024 * 1024
        ),
    )(rhs, blocks, columns, line_slot, line_slot, line_lower, line_upper, pivot_inv)


def solution(mesh):
    return jax.shard_map(
        on_device,
        mesh=mesh,
        in_specs=(
            P(None, ("span", "plane")),
            P(("span", "plane"), None),
            P(None, ("span", "plane")),
            P(("span", "plane"), None),
            P(("span", "plane"), None),
            P(("span", "plane"), None),
            P(("span", "plane"), None),
        ),
        out_specs=(P(None, ("span", "plane")), P(None, ("span", "plane"))),
        check_vma=False,
    )
```

```python
import functools

import jax
import jax.numpy as jnp
from jax import lax
from jax.experimental import pallas as pl
from jax.experimental.pallas import tpu as pltpu
from jax.sharding import PartitionSpec as P

MESH = pl.DeviceIdType.MESH
F32 = jnp.float32
BF16 = jnp.bfloat16

B = 80
NBLK = 11
ITERS = 3
F = 32
W = 128
SEG = 640
NGRP = 10
EARLY = (0, 3, 4)
LATE = (1, 2, 5, 6, 7, 8, 9, 10)
PAIRS = [(i, j) for i in range(4) for j in range(i, 4)]


def iota(shape, axis):
    return lax.broadcasted_iota(jnp.int32, shape, axis)


def split(x):
    hi = x.astype(BF16)
    lo = (x - hi.astype(F32)).astype(BF16)
    return hi, lo


def bdot(a, b):
    return jnp.dot(a, b, preferred_element_type=F32)


def pad_lanes(x):
    return jnp.concatenate([x, jnp.zeros((x.shape[0], W - x.shape[1]), x.dtype)], axis=1)


def small_solve(factor, target):
    extent = len(target)
    forward_vals = []
    for row in range(extent):
        running = target[row]
        for inner in range(row):
            running = running - factor[row][inner] * forward_vals[inner]
        forward_vals.append(running / factor[row][row])
    backward_vals = [None] * extent
    for row in reversed(range(extent)):
        running = forward_vals[row]
        for inner in range(row + 1, extent):
            running = running - factor[inner][row] * backward_vals[inner]
        backward_vals[row] = running / factor[row][row]
    return backward_vals


def coefficients(gram):
    def inner(c, d):
        out = None
        for i in range(len(c)):
            for j in range(len(d)):
                term = c[i] * d[j] * gram[min(i, j), max(i, j)]
                out = term if out is None else out + term
        return out

    beta = jnp.sqrt(gram[0, 0] + 1e-6)
    zero = jnp.zeros_like(beta)
    basis = [[1.0 / beta]]
    h = [[zero] * ITERS for _ in range(ITERS + 1)]
    for step in range(ITERS):
        w = [zero] + basis[step]
        for i in range(step + 1):
            h[i][step] = inner(basis[i], w)
        for i in range(step + 1):
            for n, c in enumerate(basis[i]):
                w[n] = w[n] - h[i][step] * c
        h[step + 1][step] = jnp.sqrt(jnp.maximum(inner(w, w), 0.0) + 1e-6)
        basis.append([c / h[step + 1][step] for c in w])
    normal = [
        [sum(h[n][i] * h[n][j] for n in range(min(i, j) + 2)) for j in range(ITERS)]
        for i in range(ITERS)
    ]
    target = [beta * h[0][j] for j in range(ITERS)]
    factor = [[None] * ITERS for _ in range(ITERS)]
    for j in range(ITERS):
        diag = normal[j][j]
        for n in range(j):
            diag = diag - factor[j][n] * factor[j][n]
        factor[j][j] = jnp.sqrt(diag)
        for i in range(j + 1, ITERS):
            below = normal[i][j]
            for n in range(j):
                below = below - factor[i][n] * factor[j][n]
            factor[i][j] = below / factor[j][j]
    y = small_solve(factor, target)
    out = []
    for n in range(ITERS):
        out.append(sum(y[j] * basis[j][n] for j in range(n, ITERS)))
    return out


def kernel(
    rhs_hbm, blocks_hbm, columns_hbm, slot_hbm, low_hbm, upp_hbm, piv_hbm,
    sol_ref, res_ref,
    rhs_ref, columns_ref, slot_ref, slot_smem, blk, flat, tall, lm, pm, pum, kf, zf, rsend, rrecv, zsend, trecv, gid, early_hot, late_hot, xe, xl, acc,
    thi, tlo, smat, square, ga, gb,
    load_sem, rsend_sem, rrecv_sem, zsend_sem, tplane_sem, tspan_sem, gsend_sem, grecv_sem,
    gas_sem, gar_sem, gbs_sem, gbr_sem,
):
    nspan, nplane = 32, 8
    s = lax.axis_index("span")
    p = lax.axis_index("plane")
    x, z = s // 8, s % 8
    s_next, s_prev = lax.rem(s + 1, nspan), lax.rem(s + nspan - 1, nspan)
    p_next, p_prev = lax.rem(p + 1, nplane), lax.rem(p + nplane - 1, nplane)

    def plane_at(i):
        return lax.rem(p + i, nplane)

    small = []
    for n, (src, dst) in enumerate(
        (
            (rhs_hbm, rhs_ref), (slot_hbm, slot_smem), (slot_hbm, slot_ref),
            (columns_hbm, columns_ref),
        )
    ):
        small.append(pltpu.make_async_copy(src, dst, load_sem.at[7 + n]))
        small[-1].start()
    loads = []
    for n, src in enumerate((low_hbm, piv_hbm, upp_hbm)):
        loads.append(pltpu.make_async_copy(src, flat.at[n], load_sem.at[n]))
    for n in range(4):
        loads.append(
            pltpu.make_async_copy(
                blocks_hbm.at[pl.ds(8 * n, 8)], blk.at[pl.ds(8 * n, 8)], load_sem.at[3 + n]
            )
        )
    for load in loads:
        load.start()

    barrier = pltpu.get_barrier_semaphore()

    def near(dx, dz):
        return lax.rem(x + dx, 4) * 8 + lax.rem(z + dz, 8)

    def greet(device):
        pl.semaphore_signal(barrier, inc=1, device_id=device, device_id_type=MESH)

    first = [(near(i // 8, 0), plane_at(i % 8)) for i in range(1, 32)]
    second = [(near(0, i), p) for i in range(1, 8)]
    for i in range(nplane):
        greet((s_next, plane_at(i)))
        greet((s_prev, plane_at(i)))
    for device in first + second:
        greet(device)

    for n in range(3):
        small[n].wait()
    k0 = pad_lanes(rhs_ref[...])
    kf[0] = k0

    lane = iota((1, W), 1)
    def to_slots(it):
        for t in range(F):
            rsend[it, t // 4, pl.ds(t % 4, 1), :] = kf[it, pl.ds(slot_smem[0, t], 1), :]

    to_slots(0)
    mine = pad_lanes(slot_ref[...].astype(F32)) + ((s * nplane + p) * F).astype(F32)
    gid[0] = jnp.broadcast_to(mine, (8, W))

    def send_pieces(it):
        for i in range(1, nplane):
            to = plane_at(i)
            pltpu.make_async_remote_copy(
                src_ref=rsend.at[it, to], dst_ref=rrecv.at[it, p],
                send_sem=rsend_sem.at[it], recv_sem=rrecv_sem.at[it],
                device_id=(s, to), device_id_type=MESH,
            ).start()
        pltpu.make_async_copy(rsend.at[it, p], rrecv.at[it, p], rrecv_sem.at[it]).start()

    for n in range(3):
        loads[n].wait()

    def relayout(g, _):
        for n in range(3):
            chunk = flat[n, :, pl.ds(pl.multiple_of(g * SEG, W), SEG)]
            for a in range(8):
                tall[n, pl.ds(pl.multiple_of((g * 8 + a) * F, F), F), :] = pad_lanes(
                    chunk[:, a * B : (a + 1) * B]
                )
        return 0

    lax.fori_loop(0, NGRP, relayout, 0)

    pl.semaphore_wait(barrier, 16 + 31 + 7)
    send_pieces(0)
    gid_copies = []
    for n, to in enumerate(((s, p_next), (s, p_prev), (s_next, p), (s_prev, p))):
        copy = pltpu.make_async_remote_copy(
            src_ref=gid.at[0], dst_ref=gid.at[n + 1],
            send_sem=gsend_sem.at[n], recv_sem=grecv_sem.at[n],
            device_id=to, device_id_type=MESH,
        )
        copy.start()
        gid_copies.append(copy)

    zeros48 = jnp.zeros((W - B, W), F32)

    def flip(m):
        return jnp.transpose(jnp.concatenate([m, zeros48], axis=0))[:B]

    def prepare(c, _):
        for n in range(8):
            row = 8 * c + n

            def matrix(which):
                return tall[which, pl.ds(row, B, stride=F), :]

            low, piv, upp = matrix(0), matrix(1), matrix(2)
            ph, pl_ = split(piv[:, :B])
            uh, ul = split(upp)
            both = bdot(ph, uh) + (bdot(ph, ul) + bdot(pl_, uh))
            if n % 2 == 0:
                lm[row], pm[row], pum[row] = flip(low), piv, both
            else:
                lm[row], pm[row], pum[row] = low, flip(piv), flip(both)
        return 0

    lax.fori_loop(0, F // 8, prepare, 0)

    square[...] = jnp.zeros_like(square)
    for it in range(ITERS):
        zsend[it, 0] = jnp.zeros((4, W), F32)
        zsend[it, nplane + 1] = jnp.zeros((4, W), F32)
    thi[...] = jnp.zeros_like(thi)
    tlo[...] = jnp.zeros_like(tlo)
    smat[...] = (iota((SEG, W), 0) // B == iota((SEG, W), 1)).astype(F32).astype(BF16)

    for copy in gid_copies:
        copy.wait()
    below = jnp.where(p == 0, -1.0, gid[1])
    above = jnp.where(p == nplane - 1, -1.0, gid[2])
    rows = [below[0:1], gid[0][0:1], above[0:1], gid[3][0:1], gid[4][0:1]]
    stacked = jnp.concatenate(rows + [jnp.zeros((W - 5, W), F32)], axis=0)
    by_slot = jnp.transpose(stacked)[:F]
    n_at = iota((F, 2 * W), 1)
    blk_at = n_at // 4
    span_part = n_at >= 96
    dir_at = jnp.where(span_part, 3 + (blk_at - 24) // 8, blk_at % 3)
    slot_at = jnp.where(span_part, (n_at - 96) % F, (blk_at // 3) * 4 + n_at % 4)
    want = iota((F, 2 * W), 0) == slot_at
    numbers = jnp.zeros((F, 2 * W), F32)
    for d in range(5):
        numbers = numbers + jnp.where(want & (dir_at == d), by_slot[:, d : d + 1], 0.0)
    numbers = jnp.sum(numbers, axis=0, keepdims=True)
    numbers = jnp.where(iota((1, 2 * W), 1) < 160, numbers, -2.0)
    small[3].wait()
    cols = jnp.transpose(
        jnp.concatenate(
            [pad_lanes(columns_ref[...].astype(F32)), jnp.zeros((W - NBLK, W), F32)], axis=0
        )
    )[:F]
    for n, k in enumerate(EARLY):
        early_hot[pl.ds(n * F, F), :] = (cols[:, k : k + 1] == numbers[:, :W]).astype(BF16)
    for n, k in enumerate(LATE):
        late_hot[pl.ds(n * F, F), :] = (cols[:, k : k + 1] == numbers).astype(BF16)
    for n in range(4):
        loads[3 + n].wait()

    def widen(it, start, count):
        got = trecv[it, pl.ds(start, count)].reshape(4 * count, W)[:, :B]
        hi, lo = split(jnp.concatenate([got] * 8, axis=1))
        thi[pl.ds(4 * start, 4 * count), :] = hi
        tlo[pl.ds(4 * start, 4 * count), :] = lo

    def weigh(g, half, which, picked, total):
        at = pl.ds(pl.multiple_of(8 * g, 8), 8)
        for n, k in enumerate(which):
            wide = picked[pl.ds(pl.multiple_of(n * F + 8 * g, 8), 8), :]
            term = blk[at, pl.ds(k * 6400 + half * 3200, 3200)] * jnp.concatenate(
                [wide] * 5, axis=1
            )
            total = term if total is None else total + term
        return total

    def one(it, _):
        pltpu.make_async_copy(rrecv.at[it], rrecv.at[it], rrecv_sem.at[it]).wait()
        for m in range(2):
            for c in range(8):
                square[pl.ds(m * 8 + c, 1), :] = rrecv[it, c, pl.ds(2 * m + 1, 1), :]
        odd = jnp.transpose(square[...])[:B]
        ys = [[], []]
        for j in range(16):
            for m in range(2):
                row = m * 16 + j
                if j == 0:
                    ys[m].append(rrecv[it, 0, pl.ds(2 * m, 1), :])
                elif j % 2:
                    idx = m * 8 + j // 2
                    base = jnp.where(lane == idx, odd, 0.0)
                    ys[m].append(
                        jnp.sum(base - lm[row] * ys[m][j - 1], axis=1, keepdims=True)
                    )
                else:
                    r = rrecv[it, j // 2, pl.ds(2 * m, 1), :]
                    ys[m].append(r - jnp.sum(lm[row] * ys[m][j - 1], axis=0, keepdims=True))
        zs = [None, None]
        even = jnp.zeros((B, W), F32)
        for j in reversed(range(16)):
            for m in range(2):
                row = m * 16 + j
                term = pm[row] * ys[m][j]
                if j < 15:
                    term = term - pum[row] * zs[m]
                zs[m] = jnp.sum(term, axis=j % 2 == 0 and 1 or 0, keepdims=True)
                if j % 2:
                    zsend[it, j // 2 + 1, pl.ds(2 * m + 1, 1), :] = zs[m]
                else:
                    even = jnp.where(lane == m * 8 + j // 2, zs[m], even)
        even = jnp.transpose(jnp.concatenate([even, zeros48], axis=0))
        for m in range(2):
            for c in range(8):
                zsend[it, c + 1, pl.ds(2 * m, 1), :] = even[m * 8 + c : m * 8 + c + 1]

        for i in range(nplane):
            to = plane_at(i)
            for n, there in enumerate((s_next, s_prev)):
                pltpu.make_async_remote_copy(
                    src_ref=zsend.at[it, to + 1], dst_ref=trecv.at[it, 24 + 8 * n + p],
                    send_sem=zsend_sem.at[it], recv_sem=tspan_sem.at[it],
                    device_id=(there, to), device_id_type=MESH,
                ).start()
        for i in range(1, nplane):
            to = plane_at(i)
            pltpu.make_async_remote_copy(
                src_ref=zsend.at[it, pl.ds(to, 3)], dst_ref=trecv.at[it, pl.ds(3 * p, 3)],
                send_sem=zsend_sem.at[it], recv_sem=tplane_sem.at[it],
                device_id=(s, to), device_id_type=MESH,
            ).start()
        pltpu.make_async_copy(
            zsend.at[it, pl.ds(p, 3)], trecv.at[it, pl.ds(3 * p, 3)], tplane_sem.at[it]
        ).start()

        part = trecv.at[it, pl.ds(0, 24)]
        pltpu.make_async_copy(part, part, tplane_sem.at[it]).wait()
        widen(it, 0, 24)
        hot = early_hot[...]
        xe[...] = bdot(hot, thi[pl.ds(0, W), :]) + bdot(hot, tlo[pl.ds(0, W), :])
        zf[it] = xe[pl.ds(0, F), pl.ds(0, W)]

        def early(g, _):
            at = pl.ds(pl.multiple_of(8 * g, 8), 8)
            for half in range(2):
                acc[at, pl.ds(half * 3200, 3200)] = weigh(g, half, EARLY, xe, None)
            return 0

        lax.fori_loop(0, 4, early, 0)

        part = trecv.at[it, pl.ds(24, 16)]
        pltpu.make_async_copy(part, part, tspan_sem.at[it]).wait()
        widen(it, 24, 16)
        hot = late_hot[...]
        xl[...] = bdot(hot, thi[...]) + bdot(hot, tlo[...])

        def late(g, _):
            at = pl.ds(pl.multiple_of(8 * g, 8), 8)
            sums = []
            for half in range(2):
                total = weigh(g, half, LATE, xl, acc[at, pl.ds(half * 3200, 3200)])
                sums += [total[:, n * SEG : (n + 1) * SEG] for n in range(5)]
            hi, lo = split(jnp.concatenate(sums, axis=0))
            out = bdot(hi, smat[...]) + bdot(lo, smat[...])
            total = out[:8]
            for n in range(1, NGRP):
                total = total + pltpu.roll(out[8 * n : 8 * n + 8], 8 * n, 1)
            kf[it + 1, at, :] = total
            return 0

        lax.fori_loop(0, 4, late, 0)

        @pl.when(it < ITERS - 1)
        def _():
            for t in range(F):
                rsend[it + 1, t // 4, pl.ds(t % 4, 1), :] = kf[
                    it + 1, pl.ds(slot_smem[0, t], 1), :
                ]
            send_pieces(it + 1)

        return 0

    lax.fori_loop(0, ITERS, one, 0)

    ks = [kf[i] for i in range(4)]
    tile = jnp.concatenate(
        [jnp.sum(ks[i] * ks[j], axis=0, keepdims=True) for i, j in PAIRS]
        + [jnp.zeros((6, W), F32)],
        axis=0,
    )
    tile = jnp.sum(tile, axis=1, keepdims=True)
    tile = jnp.where(iota((16, W), 0) == iota((16, W), 1), tile, 0.0)
    ga[0] = jnp.sum(tile, axis=0, keepdims=True)
    for i, to in enumerate(first):
        pltpu.make_async_remote_copy(
            src_ref=ga.at[0], dst_ref=ga.at[i + 1],
            send_sem=gas_sem.at[0], recv_sem=gar_sem.at[0],
            device_id=to, device_id_type=MESH,
        ).start()
    arrived = ga.at[pl.ds(1, 31)]
    pltpu.make_async_copy(arrived, arrived, gar_sem.at[0]).wait()
    gb[0] = jnp.sum(ga[...], axis=0)
    for i, to in enumerate(second):
        pltpu.make_async_remote_copy(
            src_ref=gb.at[0], dst_ref=gb.at[i + 1],
            send_sem=gbs_sem.at[0], recv_sem=gbr_sem.at[0],
            device_id=to, device_id_type=MESH,
        ).start()
    arrived_b = gb.at[pl.ds(1, 7)]
    pltpu.make_async_copy(arrived_b, arrived_b, gbr_sem.at[0]).wait()
    whole = jnp.sum(gb[...], axis=0)
    gram = {
        pair: jnp.broadcast_to(whole[:, n : n + 1], (1, W)) for n, pair in enumerate(PAIRS)
    }
    coef = coefficients(gram)
    solved = sum(coef[i] * zf[i] for i in range(ITERS))
    left = ks[0] - sum(coef[i] * ks[i + 1] for i in range(ITERS))
    sol_ref[...] = solved[:, :B]
    res_ref[...] = left[:, :B]

    pltpu.make_async_copy(arrived, arrived, gas_sem.at[0]).wait()
    pltpu.make_async_copy(arrived_b, arrived_b, gbs_sem.at[0]).wait()
    for it in range(ITERS):
        out = rsend.at[it, pl.ds(0, 7)]
        pltpu.make_async_copy(out, out, rsend_sem.at[it]).wait()
        out = trecv.at[it, pl.ds(0, 37)]
        pltpu.make_async_copy(out, out, zsend_sem.at[it]).wait()


def on_device(rhs, blocks, columns, line_slot, line_lower, line_upper, pivot_inv):
    vmem = pl.BlockSpec(memory_space=pltpu.VMEM)
    hbm = pl.BlockSpec(memory_space=pl.ANY)
    out = jax.ShapeDtypeStruct((F, B), F32)
    dma = pltpu.SemaphoreType.DMA
    solved, left = pl.pallas_call(
        kernel,
        out_shape=(out, out),
        in_specs=[hbm] * 7,
        out_specs=(vmem, vmem),
        scratch_shapes=[
            pltpu.VMEM((F, B), F32),
            pltpu.VMEM((NBLK, F), jnp.int32),
            pltpu.VMEM((1, F), jnp.int32),
            pltpu.SMEM((1, F), jnp.int32),
            pltpu.VMEM((F, NBLK * B * B), F32),
            pltpu.VMEM((3, F, B * B), F32),
            pltpu.VMEM((3, B * F, W), F32),
            pltpu.VMEM((F, B, W), F32),
            pltpu.VMEM((F, B, W), F32),
            pltpu.VMEM((F, B, W), F32),
            pltpu.VMEM((ITERS + 1, F, W), F32),
            pltpu.VMEM((ITERS, F, W), F32),
            pltpu.VMEM((ITERS, 8, 4, W), F32),
            pltpu.VMEM((ITERS, 8, 4, W), F32),
            pltpu.VMEM((ITERS, 10, 4, W), F32),
            pltpu.VMEM((ITERS, 40, 4, W), F32),
            pltpu.VMEM((5, 8, W), F32),
            pltpu.VMEM((3 * F, W), BF16),
            pltpu.VMEM((8 * F, 2 * W), BF16),
            pltpu.VMEM((3 * F, SEG), F32),
            pltpu.VMEM((8 * F, SEG), F32),
            pltpu.VMEM((F, B * B), F32),
            pltpu.VMEM((2 * W, SEG), BF16),
            pltpu.VMEM((2 * W, SEG), BF16),
            pltpu.VMEM((SEG, W), BF16),
            pltpu.VMEM((W, W), F32),
            pltpu.VMEM((32, 1, W), F32),
            pltpu.VMEM((8, 1, W), F32),
            dma((11,)),
            dma((ITERS,)),
            dma((ITERS,)),
            dma((ITERS,)),
            dma((ITERS,)),
            dma((ITERS,)),
            dma((4,)),
            dma((4,)),
            dma((1,)),
            dma((1,)),
            dma((1,)),
            dma((1,)),
        ],
        compiler_params=pltpu.CompilerParams(
            collective_id=0, has_side_effects=True, vmem_limit_bytes=60 * 1024 * 1024
        ),
    )(rhs.T, blocks, columns, line_slot, line_lower, line_upper, pivot_inv)
    return solved.T, left.T


def solution(mesh):
    return jax.shard_map(
        on_device,
        mesh=mesh,
        in_specs=(
            P(None, ("span", "plane")),
            P(("span", "plane"), None),
            P(None, ("span", "plane")),
            P(("span", "plane"), None),
            P(("span", "plane"), None),
            P(("span", "plane"), None),
            P(("span", "plane"), None),
        ),
        out_specs=(P(None, ("span", "plane")), P(None, ("span", "plane"))),
        check_vma=False,
    )
```

```python
import functools

import jax
import jax.numpy as jnp
from jax import lax
from jax.experimental import pallas as pl
from jax.experimental.pallas import tpu as pltpu
from jax.sharding import PartitionSpec as P

MESH = pl.DeviceIdType.MESH
F32 = jnp.float32
BF16 = jnp.bfloat16

B = 80
NBLK = 11
ITERS = 3
F = 32
W = 128
SEG = 640
NGRP = 10
EARLY = (0, 3, 4)
LATE = (1, 2, 5, 6, 7, 8, 9, 10)
PAIRS = [(i, j) for i in range(4) for j in range(i, 4)]


def iota(shape, axis):
    return lax.broadcasted_iota(jnp.int32, shape, axis)


def split(x):
    hi = x.astype(BF16)
    lo = (x - hi.astype(F32)).astype(BF16)
    return hi, lo


def bdot(a, b):
    return jnp.dot(a, b, preferred_element_type=F32)


def pad_lanes(x):
    return jnp.concatenate([x, jnp.zeros((x.shape[0], W - x.shape[1]), x.dtype)], axis=1)


def small_solve(factor, target):
    extent = len(target)
    forward_vals = []
    for row in range(extent):
        running = target[row]
        for inner in range(row):
            running = running - factor[row][inner] * forward_vals[inner]
        forward_vals.append(running / factor[row][row])
    backward_vals = [None] * extent
    for row in reversed(range(extent)):
        running = forward_vals[row]
        for inner in range(row + 1, extent):
            running = running - factor[inner][row] * backward_vals[inner]
        backward_vals[row] = running / factor[row][row]
    return backward_vals


def coefficients(gram):
    def inner(c, d):
        out = None
        for i in range(len(c)):
            for j in range(len(d)):
                term = c[i] * d[j] * gram[min(i, j), max(i, j)]
                out = term if out is None else out + term
        return out

    beta = jnp.sqrt(gram[0, 0] + 1e-6)
    zero = jnp.zeros_like(beta)
    basis = [[1.0 / beta]]
    h = [[zero] * ITERS for _ in range(ITERS + 1)]
    for step in range(ITERS):
        w = [zero] + basis[step]
        for i in range(step + 1):
            h[i][step] = inner(basis[i], w)
        for i in range(step + 1):
            for n, c in enumerate(basis[i]):
                w[n] = w[n] - h[i][step] * c
        h[step + 1][step] = jnp.sqrt(jnp.maximum(inner(w, w), 0.0) + 1e-6)
        basis.append([c / h[step + 1][step] for c in w])
    normal = [
        [sum(h[n][i] * h[n][j] for n in range(min(i, j) + 2)) for j in range(ITERS)]
        for i in range(ITERS)
    ]
    target = [beta * h[0][j] for j in range(ITERS)]
    factor = [[None] * ITERS for _ in range(ITERS)]
    for j in range(ITERS):
        diag = normal[j][j]
        for n in range(j):
            diag = diag - factor[j][n] * factor[j][n]
        factor[j][j] = jnp.sqrt(diag)
        for i in range(j + 1, ITERS):
            below = normal[i][j]
            for n in range(j):
                below = below - factor[i][n] * factor[j][n]
            factor[i][j] = below / factor[j][j]
    y = small_solve(factor, target)
    out = []
    for n in range(ITERS):
        out.append(sum(y[j] * basis[j][n] for j in range(n, ITERS)))
    return out


def kernel(
    rhs_hbm, blocks_hbm, columns_hbm, slot_hbm, low_hbm, upp_hbm, piv_hbm,
    both_ref,
    rhs_ref, columns_ref, slot_ref, slot_smem, blk, flat, tall, lm, pm, pum, kf, zf, rsend, rrecv, zsend, trecv, gid, early_hot, late_hot, xe, xl, acc, acc2, sfull,
    thi, tlo, smat, square, ga, gb,
    load_sem, rsend_sem, rrecv_sem, zsend_sem, tplane_sem, tspan_sem, gsend_sem, grecv_sem,
    gas_sem, gar_sem, gbs_sem, gbr_sem,
):
    nspan, nplane = 32, 8
    s = lax.axis_index("span")
    p = lax.axis_index("plane")
    x, z = s // 8, s % 8
    s_next, s_prev = lax.rem(s + 1, nspan), lax.rem(s + nspan - 1, nspan)
    p_next, p_prev = lax.rem(p + 1, nplane), lax.rem(p + nplane - 1, nplane)

    def plane_at(i):
        return lax.rem(p + i, nplane)

    small = []
    for n, (src, dst) in enumerate(
        (
            (rhs_hbm, rhs_ref), (slot_hbm, slot_smem), (slot_hbm, slot_ref),
            (columns_hbm, columns_ref),
        )
    ):
        small.append(pltpu.make_async_copy(src, dst, load_sem.at[7 + n]))
        small[-1].start()
    loads = []
    for n, src in enumerate((low_hbm, piv_hbm, upp_hbm)):
        loads.append(pltpu.make_async_copy(src, flat.at[n], load_sem.at[n]))
    for n in range(4):
        loads.append(
            pltpu.make_async_copy(
                blocks_hbm.at[pl.ds(8 * n, 8)], blk.at[pl.ds(8 * n, 8)], load_sem.at[3 + n]
            )
        )
    for load in loads:
        load.start()

    barrier = pltpu.get_barrier_semaphore()

    def near(dx, dz):
        return lax.rem(x + dx, 4) * 8 + lax.rem(z + dz, 8)

    def greet(device):
        pl.semaphore_signal(barrier, inc=1, device_id=device, device_id_type=MESH)

    first = [(near(i // 8, 0), plane_at(i % 8)) for i in range(1, 32)]
    second = [(near(0, i), p) for i in range(1, 8)]
    for i in range(nplane):
        greet((s_next, plane_at(i)))
        greet((s_prev, plane_at(i)))
    for device in first + second:
        greet(device)

    for n in range(3):
        small[n].wait()
    k0 = pad_lanes(rhs_ref[...])
    kf[0] = k0

    lane = iota((1, W), 1)
    def to_slots(it):
        for t in range(F):
            rsend[it, t // 4, pl.ds(t % 4, 1), :] = kf[it, pl.ds(slot_smem[0, t], 1), :]

    to_slots(0)
    mine = pad_lanes(slot_ref[...].astype(F32)) + ((s * nplane + p) * F).astype(F32)
    gid[0] = jnp.broadcast_to(mine, (8, W))

    def send_pieces(it):
        for i in range(1, nplane):
            to = plane_at(i)
            pltpu.make_async_remote_copy(
                src_ref=rsend.at[it, to], dst_ref=rrecv.at[it, p],
                send_sem=rsend_sem.at[it], recv_sem=rrecv_sem.at[it],
                device_id=(s, to), device_id_type=MESH,
            ).start()
        pltpu.make_async_copy(rsend.at[it, p], rrecv.at[it, p], rrecv_sem.at[it]).start()

    for n in range(3):
        loads[n].wait()

    def relayout(g, _):
        for n in range(3):
            chunk = flat[n, :, pl.ds(pl.multiple_of(g * SEG, W), SEG)]
            for a in range(8):
                tall[n, pl.ds(pl.multiple_of((g * 8 + a) * F, F), F), :] = pad_lanes(
                    chunk[:, a * B : (a + 1) * B]
                )
        return 0

    lax.fori_loop(0, NGRP, relayout, 0)

    pl.semaphore_wait(barrier, 16 + 31 + 7)
    send_pieces(0)
    gid_copies = []
    for n, to in enumerate(((s, p_next), (s, p_prev), (s_next, p), (s_prev, p))):
        copy = pltpu.make_async_remote_copy(
            src_ref=gid.at[0], dst_ref=gid.at[n + 1],
            send_sem=gsend_sem.at[n], recv_sem=grecv_sem.at[n],
            device_id=to, device_id_type=MESH,
        )
        copy.start()
        gid_copies.append(copy)

    zeros48 = jnp.zeros((W - B, W), F32)

    def flip(m):
        return jnp.transpose(jnp.concatenate([m, zeros48], axis=0))[:B]

    def prepare(c, _):
        for n in range(8):
            row = 8 * c + n

            def matrix(which):
                return tall[which, pl.ds(row, B, stride=F), :]

            low, piv, upp = matrix(0), matrix(1), matrix(2)
            ph, pl_ = split(piv[:, :B])
            uh, ul = split(upp)
            both = bdot(ph, uh) + (bdot(ph, ul) + bdot(pl_, uh))
            if n % 2 == 0:
                lm[row], pm[row], pum[row] = flip(low), piv, both
            else:
                lm[row], pm[row], pum[row] = low, flip(piv), flip(both)
        return 0

    lax.fori_loop(0, F // 8, prepare, 0)

    square[...] = jnp.zeros_like(square)
    for it in range(ITERS):
        zsend[it, 0] = jnp.zeros((4, W), F32)
        zsend[it, nplane + 1] = jnp.zeros((4, W), F32)
    thi[...] = jnp.zeros_like(thi)
    tlo[...] = jnp.zeros_like(tlo)
    def ones(n, _):
        at = pl.ds(pl.multiple_of(n * SEG, SEG), SEG)
        match = (n * SEG + iota((SEG, W), 0)) // B == iota((SEG, W), 1)
        sfull[at, :] = match.astype(F32).astype(BF16)
        return 0

    lax.fori_loop(0, NGRP, ones, 0)

    for copy in gid_copies:
        copy.wait()
    below = jnp.where(p == 0, -1.0, gid[1])
    above = jnp.where(p == nplane - 1, -1.0, gid[2])
    rows = [below[0:1], gid[0][0:1], above[0:1], gid[3][0:1], gid[4][0:1]]
    stacked = jnp.concatenate(rows + [jnp.zeros((W - 5, W), F32)], axis=0)
    by_slot = jnp.transpose(stacked)[:F]
    n_at = iota((F, 2 * W), 1)
    blk_at = n_at // 4
    span_part = n_at >= 96
    dir_at = jnp.where(span_part, 3 + (blk_at - 24) // 8, blk_at % 3)
    slot_at = jnp.where(span_part, (n_at - 96) % F, (blk_at // 3) * 4 + n_at % 4)
    want = iota((F, 2 * W), 0) == slot_at
    numbers = jnp.zeros((F, 2 * W), F32)
    for d in range(5):
        numbers = numbers + jnp.where(want & (dir_at == d), by_slot[:, d : d + 1], 0.0)
    numbers = jnp.sum(numbers, axis=0, keepdims=True)
    numbers = jnp.where(iota((1, 2 * W), 1) < 160, numbers, -2.0)
    small[3].wait()
    cols = jnp.transpose(
        jnp.concatenate(
            [pad_lanes(columns_ref[...].astype(F32)), jnp.zeros((W - NBLK, W), F32)], axis=0
        )
    )[:F]
    for n, k in enumerate(EARLY):
        early_hot[pl.ds(n * F, F), :] = (cols[:, k : k + 1] == numbers[:, :W]).astype(BF16)
    for n, k in enumerate(LATE):
        late_hot[pl.ds(n * F, F), :] = (cols[:, k : k + 1] == numbers).astype(BF16)
    for n in range(4):
        loads[3 + n].wait()

    def widen(it, start, count):
        got = trecv[it, pl.ds(start, count)].reshape(4 * count, W)[:, :B]
        hi, lo = split(jnp.concatenate([got] * 8, axis=1))
        thi[pl.ds(4 * start, 4 * count), :] = hi
        tlo[pl.ds(4 * start, 4 * count), :] = lo

    def weigh(row, half, which, picked, total):
        at = pl.ds(row, 8)
        for n, k in enumerate(which):
            term = blk[at, pl.ds(k * 6400 + half * 3200, 3200)] * jnp.concatenate(
                [picked[pl.ds(n * F + row, 8), :]] * 5, axis=1
            )
            total = term if total is None else total + term
        return total

    def one(it, _):
        pltpu.make_async_copy(rrecv.at[it], rrecv.at[it], rrecv_sem.at[it]).wait()
        for m in range(2):
            for c in range(8):
                square[pl.ds(m * 8 + c, 1), :] = rrecv[it, c, pl.ds(2 * m + 1, 1), :]
        odd = jnp.transpose(square[...])[:B]
        ys = [[], []]
        for j in range(16):
            for m in range(2):
                row = m * 16 + j
                if j == 0:
                    ys[m].append(rrecv[it, 0, pl.ds(2 * m, 1), :])
                elif j % 2:
                    idx = m * 8 + j // 2
                    base = jnp.where(lane == idx, odd, 0.0)
                    ys[m].append(
                        jnp.sum(base - lm[row] * ys[m][j - 1], axis=1, keepdims=True)
                    )
                else:
                    r = rrecv[it, j // 2, pl.ds(2 * m, 1), :]
                    ys[m].append(r - jnp.sum(lm[row] * ys[m][j - 1], axis=0, keepdims=True))
        zs = [None, None]
        even = jnp.zeros((B, W), F32)
        for j in reversed(range(16)):
            for m in range(2):
                row = m * 16 + j
                term = pm[row] * ys[m][j]
                if j < 15:
                    term = term - pum[row] * zs[m]
                zs[m] = jnp.sum(term, axis=j % 2 == 0 and 1 or 0, keepdims=True)
                if j % 2:
                    zsend[it, j // 2 + 1, pl.ds(2 * m + 1, 1), :] = zs[m]
                else:
                    even = jnp.where(lane == m * 8 + j // 2, zs[m], even)
        even = jnp.transpose(jnp.concatenate([even, zeros48], axis=0))
        for m in range(2):
            for c in range(8):
                zsend[it, c + 1, pl.ds(2 * m, 1), :] = even[m * 8 + c : m * 8 + c + 1]

        for i in range(nplane):
            to = plane_at(i)
            for n, there in enumerate((s_next, s_prev)):
                pltpu.make_async_remote_copy(
                    src_ref=zsend.at[it, to + 1], dst_ref=trecv.at[it, 24 + 8 * n + p],
                    send_sem=zsend_sem.at[it], recv_sem=tspan_sem.at[it],
                    device_id=(there, to), device_id_type=MESH,
                ).start()
        for i in range(1, nplane):
            to = plane_at(i)
            pltpu.make_async_remote_copy(
                src_ref=zsend.at[it, pl.ds(to, 3)], dst_ref=trecv.at[it, pl.ds(3 * p, 3)],
                send_sem=zsend_sem.at[it], recv_sem=tplane_sem.at[it],
                device_id=(s, to), device_id_type=MESH,
            ).start()
        pltpu.make_async_copy(
            zsend.at[it, pl.ds(p, 3)], trecv.at[it, pl.ds(3 * p, 3)], tplane_sem.at[it]
        ).start()

        part = trecv.at[it, pl.ds(0, 24)]
        pltpu.make_async_copy(part, part, tplane_sem.at[it]).wait()
        widen(it, 0, 24)
        hot = early_hot[...]
        xe[...] = bdot(hot, thi[pl.ds(0, W), :]) + bdot(hot, tlo[pl.ds(0, W), :])
        zf[it] = xe[pl.ds(0, F), pl.ds(0, W)]

        for row in range(0, F, 8):
            for half in range(2):
                acc[pl.ds(row, 8), pl.ds(half * 3200, 3200)] = weigh(row, half, EARLY, xe, None)

        part = trecv.at[it, pl.ds(24, 16)]
        pltpu.make_async_copy(part, part, tspan_sem.at[it]).wait()
        widen(it, 24, 16)
        hot = late_hot[...]
        xl[...] = bdot(hot, thi[...]) + bdot(hot, tlo[...])

        out = None
        for half in range(2):
            lanes = pl.ds(half * 3200, 3200)
            for row in range(0, F, 16):
                total = jnp.concatenate(
                    [weigh(n, half, LATE, xl, acc[pl.ds(n, 8), lanes]) for n in (row, row + 8)],
                    axis=0,
                )
                hi, lo = split(total)
                acc2[pl.ds(row, 16), lanes] = hi
                acc2[pl.ds(F + row, 16), lanes] = lo
            part = bdot(acc2[:, lanes], sfull[lanes, :])
            out = part if out is None else out + part
        kf[it + 1] = out[:F] + out[F:]

        @pl.when(it < ITERS - 1)
        def _():
            for t in range(F):
                rsend[it + 1, t // 4, pl.ds(t % 4, 1), :] = kf[
                    it + 1, pl.ds(slot_smem[0, t], 1), :
                ]
            send_pieces(it + 1)

        return 0

    lax.fori_loop(0, ITERS, one, 0)

    ks = [kf[i] for i in range(4)]
    tile = jnp.concatenate(
        [jnp.sum(ks[i] * ks[j], axis=0, keepdims=True) for i, j in PAIRS]
        + [jnp.zeros((6, W), F32)],
        axis=0,
    )
    tile = jnp.sum(tile, axis=1, keepdims=True)
    tile = jnp.where(iota((16, W), 0) == iota((16, W), 1), tile, 0.0)
    ga[0] = jnp.sum(tile, axis=0, keepdims=True)
    for i, to in enumerate(first):
        pltpu.make_async_remote_copy(
            src_ref=ga.at[0], dst_ref=ga.at[i + 1],
            send_sem=gas_sem.at[0], recv_sem=gar_sem.at[0],
            device_id=to, device_id_type=MESH,
        ).start()
    arrived = ga.at[pl.ds(1, 31)]
    pltpu.make_async_copy(arrived, arrived, gar_sem.at[0]).wait()
    gb[0] = jnp.sum(ga[...], axis=0)
    for i, to in enumerate(second):
        pltpu.make_async_remote_copy(
            src_ref=gb.at[0], dst_ref=gb.at[i + 1],
            send_sem=gbs_sem.at[0], recv_sem=gbr_sem.at[0],
            device_id=to, device_id_type=MESH,
        ).start()
    arrived_b = gb.at[pl.ds(1, 7)]
    pltpu.make_async_copy(arrived_b, arrived_b, gbr_sem.at[0]).wait()
    whole = jnp.sum(gb[...], axis=0)
    gram = {
        pair: jnp.broadcast_to(whole[:, n : n + 1], (1, W)) for n, pair in enumerate(PAIRS)
    }
    coef = coefficients(gram)
    solved = sum(coef[i] * zf[i] for i in range(ITERS))
    left = ks[0] - sum(coef[i] * ks[i + 1] for i in range(ITERS))
    both_ref[0] = solved[:, :B]
    both_ref[1] = left[:, :B]

    pltpu.make_async_copy(arrived, arrived, gas_sem.at[0]).wait()
    pltpu.make_async_copy(arrived_b, arrived_b, gbs_sem.at[0]).wait()
    for it in range(ITERS):
        out = rsend.at[it, pl.ds(0, 7)]
        pltpu.make_async_copy(out, out, rsend_sem.at[it]).wait()
        out = trecv.at[it, pl.ds(0, 37)]
        pltpu.make_async_copy(out, out, zsend_sem.at[it]).wait()


def on_device(rhs, blocks, columns, line_slot, line_lower, line_upper, pivot_inv):
    vmem = pl.BlockSpec(memory_space=pltpu.VMEM)
    hbm = pl.BlockSpec(memory_space=pl.ANY)
    out = jax.ShapeDtypeStruct((F, B), F32)
    dma = pltpu.SemaphoreType.DMA
    both = pl.pallas_call(
        kernel,
        out_shape=jax.ShapeDtypeStruct((2, F, B), F32),
        in_specs=[hbm] * 7,
        out_specs=vmem,
        scratch_shapes=[
            pltpu.VMEM((F, B), F32),
            pltpu.VMEM((NBLK, F), jnp.int32),
            pltpu.VMEM((1, F), jnp.int32),
            pltpu.SMEM((1, F), jnp.int32),
            pltpu.VMEM((F, NBLK * B * B), F32),
            pltpu.VMEM((3, F, B * B), F32),
            pltpu.VMEM((3, B * F, W), F32),
            pltpu.VMEM((F, B, W), F32),
            pltpu.VMEM((F, B, W), F32),
            pltpu.VMEM((F, B, W), F32),
            pltpu.VMEM((ITERS + 1, F, W), F32),
            pltpu.VMEM((ITERS, F, W), F32),
            pltpu.VMEM((ITERS, 8, 4, W), F32),
            pltpu.VMEM((ITERS, 8, 4, W), F32),
            pltpu.VMEM((ITERS, 10, 4, W), F32),
            pltpu.VMEM((ITERS, 40, 4, W), F32),
            pltpu.VMEM((5, 8, W), F32),
            pltpu.VMEM((3 * F, W), BF16),
            pltpu.VMEM((8 * F, 2 * W), BF16),
            pltpu.VMEM((3 * F, SEG), F32),
            pltpu.VMEM((8 * F, SEG), F32),
            pltpu.VMEM((F, B * B), F32),
            pltpu.VMEM((2 * F, B * B), BF16),
            pltpu.VMEM((B * B, W), BF16),
            pltpu.VMEM((2 * W, SEG), BF16),
            pltpu.VMEM((2 * W, SEG), BF16),
            pltpu.VMEM((SEG, W), BF16),
            pltpu.VMEM((W, W), F32),
            pltpu.VMEM((32, 1, W), F32),
            pltpu.VMEM((8, 1, W), F32),
            dma((11,)),
            dma((ITERS,)),
            dma((ITERS,)),
            dma((ITERS,)),
            dma((ITERS,)),
            dma((ITERS,)),
            dma((4,)),
            dma((4,)),
            dma((1,)),
            dma((1,)),
            dma((1,)),
            dma((1,)),
        ],
        compiler_params=pltpu.CompilerParams(
            collective_id=0, has_side_effects=True, vmem_limit_bytes=60 * 1024 * 1024
        ),
    )(rhs.T, blocks, columns, line_slot, line_lower, line_upper, pivot_inv)
    return both[0].T, both[1].T


def solution(mesh):
    return jax.shard_map(
        on_device,
        mesh=mesh,
        in_specs=(
            P(None, ("span", "plane")),
            P(("span", "plane"), None),
            P(None, ("span", "plane")),
            P(("span", "plane"), None),
            P(("span", "plane"), None),
            P(("span", "plane"), None),
            P(("span", "plane"), None),
        ),
        out_specs=(P(None, ("span", "plane")), P(None, ("span", "plane"))),
        check_vma=False,
    )
```

```python
import functools

import jax
import jax.numpy as jnp
from jax import lax
from jax.experimental import pallas as pl
from jax.experimental.pallas import tpu as pltpu
from jax.sharding import PartitionSpec as P

MESH = pl.DeviceIdType.MESH
F32 = jnp.float32
BF16 = jnp.bfloat16

B = 80
NBLK = 11
ITERS = 3
F = 32
W = 128
SEG = 640
NGRP = 10
EARLY = (0, 3, 4)
LATE = (1, 2, 5, 6, 7, 8, 9, 10)
PAIRS = [(i, j) for i in range(4) for j in range(i, 4)]


def iota(shape, axis):
    return lax.broadcasted_iota(jnp.int32, shape, axis)


def split(x):
    hi = x.astype(BF16)
    lo = (x - hi.astype(F32)).astype(BF16)
    return hi, lo


def bdot(a, b):
    return jnp.dot(a, b, preferred_element_type=F32)


def pad_lanes(x):
    return jnp.concatenate([x, jnp.zeros((x.shape[0], W - x.shape[1]), x.dtype)], axis=1)


def small_solve(factor, target):
    extent = len(target)
    forward_vals = []
    for row in range(extent):
        running = target[row]
        for inner in range(row):
            running = running - factor[row][inner] * forward_vals[inner]
        forward_vals.append(running / factor[row][row])
    backward_vals = [None] * extent
    for row in reversed(range(extent)):
        running = forward_vals[row]
        for inner in range(row + 1, extent):
            running = running - factor[inner][row] * backward_vals[inner]
        backward_vals[row] = running / factor[row][row]
    return backward_vals


def coefficients(gram):
    def inner(c, d):
        out = None
        for i in range(len(c)):
            for j in range(len(d)):
                term = c[i] * d[j] * gram[min(i, j), max(i, j)]
                out = term if out is None else out + term
        return out

    beta = jnp.sqrt(gram[0, 0] + 1e-6)
    zero = jnp.zeros_like(beta)
    basis = [[1.0 / beta]]
    h = [[zero] * ITERS for _ in range(ITERS + 1)]
    for step in range(ITERS):
        w = [zero] + basis[step]
        for i in range(step + 1):
            h[i][step] = inner(basis[i], w)
        for i in range(step + 1):
            for n, c in enumerate(basis[i]):
                w[n] = w[n] - h[i][step] * c
        h[step + 1][step] = jnp.sqrt(jnp.maximum(inner(w, w), 0.0) + 1e-6)
        basis.append([c / h[step + 1][step] for c in w])
    normal = [
        [sum(h[n][i] * h[n][j] for n in range(min(i, j) + 2)) for j in range(ITERS)]
        for i in range(ITERS)
    ]
    target = [beta * h[0][j] for j in range(ITERS)]
    factor = [[None] * ITERS for _ in range(ITERS)]
    for j in range(ITERS):
        diag = normal[j][j]
        for n in range(j):
            diag = diag - factor[j][n] * factor[j][n]
        factor[j][j] = jnp.sqrt(diag)
        for i in range(j + 1, ITERS):
            below = normal[i][j]
            for n in range(j):
                below = below - factor[i][n] * factor[j][n]
            factor[i][j] = below / factor[j][j]
    y = small_solve(factor, target)
    out = []
    for n in range(ITERS):
        out.append(sum(y[j] * basis[j][n] for j in range(n, ITERS)))
    return out


def kernel(
    rhs_hbm, blocks_hbm, columns_hbm, slot_hbm, low_hbm, upp_hbm, piv_hbm,
    both_ref,
    rhs_ref, columns_ref, slot_ref, slot_smem, blk, flat, tall, lm, pm, pum, kf, zf, rsend, rrecv, zsend, trecv, gid, early_hot, late_hot, xe, xl, acc, acc2, sfull,
    thi, tlo, smat, square, ga, gb,
    load_sem, rsend_sem, rrecv_sem, zsend_sem, tplane_sem, tspan_sem, gsend_sem, grecv_sem,
    gas_sem, gar_sem, gbs_sem, gbr_sem,
):
    nspan, nplane = 32, 8
    s = lax.axis_index("span")
    p = lax.axis_index("plane")
    x, z = s // 8, s % 8
    s_next, s_prev = lax.rem(s + 1, nspan), lax.rem(s + nspan - 1, nspan)
    p_next, p_prev = lax.rem(p + 1, nplane), lax.rem(p + nplane - 1, nplane)

    def plane_at(i):
        return lax.rem(p + i, nplane)

    small = []
    for n, (src, dst) in enumerate(
        (
            (rhs_hbm, rhs_ref), (slot_hbm, slot_smem), (slot_hbm, slot_ref),
            (columns_hbm, columns_ref),
        )
    ):
        small.append(pltpu.make_async_copy(src, dst, load_sem.at[7 + n]))
        small[-1].start()
    loads = []
    for n, src in enumerate((low_hbm, piv_hbm, upp_hbm)):
        loads.append(pltpu.make_async_copy(src, flat.at[n], load_sem.at[n]))
    for n in range(4):
        loads.append(
            pltpu.make_async_copy(
                blocks_hbm.at[pl.ds(8 * n, 8)], blk.at[pl.ds(8 * n, 8)], load_sem.at[3 + n]
            )
        )
    for load in loads:
        load.start()

    barrier = pltpu.get_barrier_semaphore()

    def near(dx, dz):
        return lax.rem(x + dx, 4) * 8 + lax.rem(z + dz, 8)

    def greet(device):
        pl.semaphore_signal(barrier, inc=1, device_id=device, device_id_type=MESH)

    first = [(near(i // 8, 0), plane_at(i % 8)) for i in range(1, 32)]
    second = [(near(0, i), p) for i in range(1, 8)]
    for i in range(nplane):
        greet((s_next, plane_at(i)))
        greet((s_prev, plane_at(i)))
    for device in first + second:
        greet(device)

    for n in range(3):
        small[n].wait()
    k0 = pad_lanes(rhs_ref[...])
    kf[0] = k0

    lane = iota((1, W), 1)
    def to_slots(it):
        for t in range(F):
            rsend[it, t // 4, pl.ds(t % 4, 1), :] = kf[it, pl.ds(slot_smem[0, t], 1), :]

    to_slots(0)
    mine = pad_lanes(slot_ref[...].astype(F32)) + ((s * nplane + p) * F).astype(F32)
    gid[0] = jnp.broadcast_to(mine, (8, W))

    def send_pieces(it):
        for i in range(1, nplane):
            to = plane_at(i)
            pltpu.make_async_remote_copy(
                src_ref=rsend.at[it, to], dst_ref=rrecv.at[it, p],
                send_sem=rsend_sem.at[it], recv_sem=rrecv_sem.at[it],
                device_id=(s, to), device_id_type=MESH,
            ).start()
        pltpu.make_async_copy(rsend.at[it, p], rrecv.at[it, p], rrecv_sem.at[it]).start()

    for n in range(3):
        loads[n].wait()

    def relayout(g, _):
        for n in range(3):
            chunk = flat[n, :, pl.ds(pl.multiple_of(g * SEG, W), SEG)]
            for a in range(8):
                tall[n, pl.ds(pl.multiple_of((g * 8 + a) * F, F), F), :] = pad_lanes(
                    chunk[:, a * B : (a + 1) * B]
                )
        return 0

    lax.fori_loop(0, NGRP, relayout, 0)

    pl.semaphore_wait(barrier, 16 + 31 + 7)
    send_pieces(0)
    gid_copies = []
    for n, to in enumerate(((s, p_next), (s, p_prev), (s_next, p), (s_prev, p))):
        copy = pltpu.make_async_remote_copy(
            src_ref=gid.at[0], dst_ref=gid.at[n + 1],
            send_sem=gsend_sem.at[n], recv_sem=grecv_sem.at[n],
            device_id=to, device_id_type=MESH,
        )
        copy.start()
        gid_copies.append(copy)

    zeros48 = jnp.zeros((W - B, W), F32)

    def flip(m):
        return jnp.transpose(jnp.concatenate([m, zeros48], axis=0))[:B]

    def prepare(c, _):
        for n in range(8):
            row = 8 * c + n

            def matrix(which):
                return tall[which, pl.ds(row, B, stride=F), :]

            low, piv, upp = matrix(0), matrix(1), matrix(2)
            ph, pl_ = split(piv[:, :B])
            uh, ul = split(upp)
            both = bdot(ph, uh) + (bdot(ph, ul) + bdot(pl_, uh))
            if n % 2 == 0:
                lm[row], pm[row], pum[row] = flip(low), piv, both
            else:
                lm[row], pm[row], pum[row] = low, flip(piv), flip(both)
        return 0

    lax.fori_loop(0, F // 8, prepare, 0)

    square[...] = jnp.zeros_like(square)
    for it in range(ITERS):
        zsend[it, 0] = jnp.zeros((4, W), F32)
        zsend[it, nplane + 1] = jnp.zeros((4, W), F32)
    thi[...] = jnp.zeros_like(thi)
    tlo[...] = jnp.zeros_like(tlo)

    def set_up():
        for copy in gid_copies:
            copy.wait()
        below = jnp.where(p == 0, -1.0, gid[1])
        above = jnp.where(p == nplane - 1, -1.0, gid[2])
        rows = [below[0:1], gid[0][0:1], above[0:1], gid[3][0:1], gid[4][0:1]]
        stacked = jnp.concatenate(rows + [jnp.zeros((W - 5, W), F32)], axis=0)
        by_slot = jnp.transpose(stacked)[:F]
        n_at = iota((1, 2 * W), 1)
        blk_at = n_at // 4
        span_part = n_at >= 96
        dir_at = jnp.where(span_part, 3 + (blk_at - 24) // 8, blk_at % 3)
        slot_at = jnp.where(span_part, (n_at - 96) % F, (blk_at // 3) * 4 + n_at % 4)
        want = iota((F, 2 * W), 0) == slot_at
        numbers = jnp.zeros((F, 2 * W), F32)
        for d in range(5):
            numbers = numbers + jnp.where(want & (dir_at == d), by_slot[:, d : d + 1], 0.0)
        numbers = jnp.sum(numbers, axis=0, keepdims=True)
        numbers = jnp.where(iota((1, 2 * W), 1) < 160, numbers, -2.0)
        small[3].wait()
        cols = jnp.transpose(
            jnp.concatenate(
                [pad_lanes(columns_ref[...].astype(F32)), jnp.zeros((W - NBLK, W), F32)], axis=0
            )
        )[:F]
        for n, k in enumerate(EARLY):
            early_hot[pl.ds(n * F, F), :] = (cols[:, k : k + 1] == numbers[:, :W]).astype(BF16)
        for n, k in enumerate(LATE):
            late_hot[pl.ds(n * F, F), :] = (cols[:, k : k + 1] == numbers).astype(BF16)
        for n in range(4):
            loads[3 + n].wait()
        start = iota((SEG, W), 1) * B - iota((SEG, W), 0)

        def ones(n, _):
            ahead = start - n * SEG
            sfull[pl.ds(pl.multiple_of(n * SEG, SEG), SEG), :] = jnp.where(
                (ahead <= 0) & (ahead > -B), 1.0, 0.0
            ).astype(BF16)
            return 0

        lax.fori_loop(0, NGRP, ones, 0)

    def widen(it, start, count):
        got = trecv[it, pl.ds(start, count)].reshape(4 * count, W)[:, :B]
        hi, lo = split(jnp.concatenate([got] * 8, axis=1))
        thi[pl.ds(4 * start, 4 * count), :] = hi
        tlo[pl.ds(4 * start, 4 * count), :] = lo

    def weigh(row, half, which, picked, total):
        at = pl.ds(row, 8)
        for n, k in enumerate(which):
            term = blk[at, pl.ds(k * 6400 + half * 3200, 3200)] * jnp.concatenate(
                [picked[pl.ds(n * F + row, 8), :]] * 5, axis=1
            )
            total = term if total is None else total + term
        return total

    def one(it, _):
        pltpu.make_async_copy(rrecv.at[it], rrecv.at[it], rrecv_sem.at[it]).wait()
        for m in range(2):
            for c in range(8):
                square[pl.ds(m * 8 + c, 1), :] = rrecv[it, c, pl.ds(2 * m + 1, 1), :]
        odd = jnp.transpose(square[...])[:B]
        ys = [[], []]
        for j in range(16):
            for m in range(2):
                row = m * 16 + j
                if j == 0:
                    ys[m].append(rrecv[it, 0, pl.ds(2 * m, 1), :])
                elif j % 2:
                    idx = m * 8 + j // 2
                    base = jnp.where(lane == idx, odd, 0.0)
                    ys[m].append(
                        jnp.sum(base - lm[row] * ys[m][j - 1], axis=1, keepdims=True)
                    )
                else:
                    r = rrecv[it, j // 2, pl.ds(2 * m, 1), :]
                    ys[m].append(r - jnp.sum(lm[row] * ys[m][j - 1], axis=0, keepdims=True))
        zs = [None, None]
        even = jnp.zeros((B, W), F32)
        for j in reversed(range(16)):
            for m in range(2):
                row = m * 16 + j
                term = pm[row] * ys[m][j]
                if j < 15:
                    term = term - pum[row] * zs[m]
                zs[m] = jnp.sum(term, axis=j % 2 == 0 and 1 or 0, keepdims=True)
                if j % 2:
                    zsend[it, j // 2 + 1, pl.ds(2 * m + 1, 1), :] = zs[m]
                else:
                    even = jnp.where(lane == m * 8 + j // 2, zs[m], even)
        even = jnp.transpose(jnp.concatenate([even, zeros48], axis=0))
        for m in range(2):
            for c in range(8):
                zsend[it, c + 1, pl.ds(2 * m, 1), :] = even[m * 8 + c : m * 8 + c + 1]

        for i in range(nplane):
            to = plane_at(i)
            for n, there in enumerate((s_next, s_prev)):
                pltpu.make_async_remote_copy(
                    src_ref=zsend.at[it, to + 1], dst_ref=trecv.at[it, 24 + 8 * n + p],
                    send_sem=zsend_sem.at[it], recv_sem=tspan_sem.at[it],
                    device_id=(there, to), device_id_type=MESH,
                ).start()
        for i in range(1, nplane):
            to = plane_at(i)
            pltpu.make_async_remote_copy(
                src_ref=zsend.at[it, pl.ds(to, 3)], dst_ref=trecv.at[it, pl.ds(3 * p, 3)],
                send_sem=zsend_sem.at[it], recv_sem=tplane_sem.at[it],
                device_id=(s, to), device_id_type=MESH,
            ).start()
        pltpu.make_async_copy(
            zsend.at[it, pl.ds(p, 3)], trecv.at[it, pl.ds(3 * p, 3)], tplane_sem.at[it]
        ).start()

        @pl.when(it == 0)
        def _():
            set_up()

        part = trecv.at[it, pl.ds(0, 24)]
        pltpu.make_async_copy(part, part, tplane_sem.at[it]).wait()
        widen(it, 0, 24)
        hot = early_hot[...]
        xe[...] = bdot(hot, thi[pl.ds(0, W), :]) + bdot(hot, tlo[pl.ds(0, W), :])
        zf[it] = xe[pl.ds(0, F), pl.ds(0, W)]

        for row in range(0, F, 8):
            for half in range(2):
                acc[pl.ds(row, 8), pl.ds(half * 3200, 3200)] = weigh(row, half, EARLY, xe, None)

        part = trecv.at[it, pl.ds(24, 16)]
        pltpu.make_async_copy(part, part, tspan_sem.at[it]).wait()
        widen(it, 24, 16)
        hot = late_hot[...]
        xl[...] = bdot(hot, thi[...]) + bdot(hot, tlo[...])

        out = None
        for half in range(2):
            lanes = pl.ds(half * 3200, 3200)
            for row in range(0, F, 16):
                total = jnp.concatenate(
                    [weigh(n, half, LATE, xl, acc[pl.ds(n, 8), lanes]) for n in (row, row + 8)],
                    axis=0,
                )
                hi, lo = split(total)
                acc2[pl.ds(row, 16), lanes] = hi
                acc2[pl.ds(F + row, 16), lanes] = lo
            part = bdot(acc2[:, lanes], sfull[lanes, :])
            out = part if out is None else out + part
        kf[it + 1] = out[:F] + out[F:]

        @pl.when(it < ITERS - 1)
        def _():
            for t in range(F):
                rsend[it + 1, t // 4, pl.ds(t % 4, 1), :] = kf[
                    it + 1, pl.ds(slot_smem[0, t], 1), :
                ]
            send_pieces(it + 1)

        return 0

    lax.fori_loop(0, ITERS, one, 0)

    ks = [kf[i] for i in range(4)]
    tile = jnp.concatenate(
        [jnp.sum(ks[i] * ks[j], axis=0, keepdims=True) for i, j in PAIRS]
        + [jnp.zeros((6, W), F32)],
        axis=0,
    )
    tile = jnp.sum(tile, axis=1, keepdims=True)
    tile = jnp.where(iota((16, W), 0) == iota((16, W), 1), tile, 0.0)
    ga[0] = jnp.sum(tile, axis=0, keepdims=True)
    for i, to in enumerate(first):
        pltpu.make_async_remote_copy(
            src_ref=ga.at[0], dst_ref=ga.at[i + 1],
            send_sem=gas_sem.at[0], recv_sem=gar_sem.at[0],
            device_id=to, device_id_type=MESH,
        ).start()
    arrived = ga.at[pl.ds(1, 31)]
    pltpu.make_async_copy(arrived, arrived, gar_sem.at[0]).wait()
    gb[0] = jnp.sum(ga[...], axis=0)
    for i, to in enumerate(second):
        pltpu.make_async_remote_copy(
            src_ref=gb.at[0], dst_ref=gb.at[i + 1],
            send_sem=gbs_sem.at[0], recv_sem=gbr_sem.at[0],
            device_id=to, device_id_type=MESH,
        ).start()
    arrived_b = gb.at[pl.ds(1, 7)]
    pltpu.make_async_copy(arrived_b, arrived_b, gbr_sem.at[0]).wait()
    whole = jnp.sum(gb[...], axis=0)
    gram = {
        pair: jnp.broadcast_to(whole[:, n : n + 1], (1, W)) for n, pair in enumerate(PAIRS)
    }
    coef = coefficients(gram)
    solved = sum(coef[i] * zf[i] for i in range(ITERS))
    left = ks[0] - sum(coef[i] * ks[i + 1] for i in range(ITERS))
    both_ref[0] = solved[:, :B]
    both_ref[1] = left[:, :B]

    pltpu.make_async_copy(arrived, arrived, gas_sem.at[0]).wait()
    pltpu.make_async_copy(arrived_b, arrived_b, gbs_sem.at[0]).wait()
    for it in range(ITERS):
        out = rsend.at[it, pl.ds(0, 7)]
        pltpu.make_async_copy(out, out, rsend_sem.at[it]).wait()
        out = trecv.at[it, pl.ds(0, 37)]
        pltpu.make_async_copy(out, out, zsend_sem.at[it]).wait()


def on_device(rhs, blocks, columns, line_slot, line_lower, line_upper, pivot_inv):
    vmem = pl.BlockSpec(memory_space=pltpu.VMEM)
    hbm = pl.BlockSpec(memory_space=pl.ANY)
    out = jax.ShapeDtypeStruct((F, B), F32)
    dma = pltpu.SemaphoreType.DMA
    both = pl.pallas_call(
        kernel,
        out_shape=jax.ShapeDtypeStruct((2, F, B), F32),
        in_specs=[hbm] * 7,
        out_specs=vmem,
        scratch_shapes=[
            pltpu.VMEM((F, B), F32),
            pltpu.VMEM((NBLK, F), jnp.int32),
            pltpu.VMEM((1, F), jnp.int32),
            pltpu.SMEM((1, F), jnp.int32),
            pltpu.VMEM((F, NBLK * B * B), F32),
            pltpu.VMEM((3, F, B * B), F32),
            pltpu.VMEM((3, B * F, W), F32),
            pltpu.VMEM((F, B, W), F32),
            pltpu.VMEM((F, B, W), F32),
            pltpu.VMEM((F, B, W), F32),
            pltpu.VMEM((ITERS + 1, F, W), F32),
            pltpu.VMEM((ITERS, F, W), F32),
            pltpu.VMEM((ITERS, 8, 4, W), F32),
            pltpu.VMEM((ITERS, 8, 4, W), F32),
            pltpu.VMEM((ITERS, 10, 4, W), F32),
            pltpu.VMEM((ITERS, 40, 4, W), F32),
            pltpu.VMEM((5, 8, W), F32),
            pltpu.VMEM((3 * F, W), BF16),
            pltpu.VMEM((8 * F, 2 * W), BF16),
            pltpu.VMEM((3 * F, SEG), F32),
            pltpu.VMEM((8 * F, SEG), F32),
            pltpu.VMEM((F, B * B), F32),
            pltpu.VMEM((2 * F, B * B), BF16),
            pltpu.VMEM((B * B, W), BF16),
            pltpu.VMEM((2 * W, SEG), BF16),
            pltpu.VMEM((2 * W, SEG), BF16),
            pltpu.VMEM((SEG, W), BF16),
            pltpu.VMEM((W, W), F32),
            pltpu.VMEM((32, 1, W), F32),
            pltpu.VMEM((8, 1, W), F32),
            dma((11,)),
            dma((ITERS,)),
            dma((ITERS,)),
            dma((ITERS,)),
            dma((ITERS,)),
            dma((ITERS,)),
            dma((4,)),
            dma((4,)),
            dma((1,)),
            dma((1,)),
            dma((1,)),
            dma((1,)),
        ],
        compiler_params=pltpu.CompilerParams(
            collective_id=0, has_side_effects=True, vmem_limit_bytes=60 * 1024 * 1024
        ),
    )(rhs.T, blocks, columns, line_slot, line_lower, line_upper, pivot_inv)
    return both[0].T, both[1].T


def solution(mesh):
    return jax.shard_map(
        on_device,
        mesh=mesh,
        in_specs=(
            P(None, ("span", "plane")),
            P(("span", "plane"), None),
            P(None, ("span", "plane")),
            P(("span", "plane"), None),
            P(("span", "plane"), None),
            P(("span", "plane"), None),
            P(("span", "plane"), None),
        ),
        out_specs=(P(None, ("span", "plane")), P(None, ("span", "plane"))),
        check_vma=False,
    )
```

```python
import functools

import jax
import jax.numpy as jnp
from jax import lax
from jax.experimental import pallas as pl
from jax.experimental.pallas import tpu as pltpu
from jax.sharding import PartitionSpec as P

MESH = pl.DeviceIdType.MESH
F32 = jnp.float32
BF16 = jnp.bfloat16

B = 80
NBLK = 11
ITERS = 3
F = 32
W = 128
SEG = 640
NGRP = 10
EARLY = (0, 3, 4)
LATE = (1, 2, 5, 6, 7, 8, 9, 10)
PAIRS = [(i, j) for i in range(4) for j in range(i, 4)]


def iota(shape, axis):
    return lax.broadcasted_iota(jnp.int32, shape, axis)


def split(x):
    hi = x.astype(BF16)
    lo = (x - hi.astype(F32)).astype(BF16)
    return hi, lo


def bdot(a, b):
    return jnp.dot(a, b, preferred_element_type=F32)


def pad_lanes(x):
    return jnp.concatenate([x, jnp.zeros((x.shape[0], W - x.shape[1]), x.dtype)], axis=1)


def small_solve(factor, target):
    extent = len(target)
    forward_vals = []
    for row in range(extent):
        running = target[row]
        for inner in range(row):
            running = running - factor[row][inner] * forward_vals[inner]
        forward_vals.append(running / factor[row][row])
    backward_vals = [None] * extent
    for row in reversed(range(extent)):
        running = forward_vals[row]
        for inner in range(row + 1, extent):
            running = running - factor[inner][row] * backward_vals[inner]
        backward_vals[row] = running / factor[row][row]
    return backward_vals


def coefficients(gram):
    def inner(c, d):
        out = None
        for i in range(len(c)):
            for j in range(len(d)):
                term = c[i] * d[j] * gram[min(i, j), max(i, j)]
                out = term if out is None else out + term
        return out

    beta = jnp.sqrt(gram[0, 0] + 1e-6)
    zero = jnp.zeros_like(beta)
    basis = [[1.0 / beta]]
    h = [[zero] * ITERS for _ in range(ITERS + 1)]
    for step in range(ITERS):
        w = [zero] + basis[step]
        for i in range(step + 1):
            h[i][step] = inner(basis[i], w)
        for i in range(step + 1):
            for n, c in enumerate(basis[i]):
                w[n] = w[n] - h[i][step] * c
        h[step + 1][step] = jnp.sqrt(jnp.maximum(inner(w, w), 0.0) + 1e-6)
        basis.append([c / h[step + 1][step] for c in w])
    normal = [
        [sum(h[n][i] * h[n][j] for n in range(min(i, j) + 2)) for j in range(ITERS)]
        for i in range(ITERS)
    ]
    target = [beta * h[0][j] for j in range(ITERS)]
    factor = [[None] * ITERS for _ in range(ITERS)]
    for j in range(ITERS):
        diag = normal[j][j]
        for n in range(j):
            diag = diag - factor[j][n] * factor[j][n]
        factor[j][j] = jnp.sqrt(diag)
        for i in range(j + 1, ITERS):
            below = normal[i][j]
            for n in range(j):
                below = below - factor[i][n] * factor[j][n]
            factor[i][j] = below / factor[j][j]
    y = small_solve(factor, target)
    out = []
    for n in range(ITERS):
        out.append(sum(y[j] * basis[j][n] for j in range(n, ITERS)))
    return out


def kernel(
    rhs_hbm, blocks_hbm, columns_hbm, slot_hbm, low_hbm, upp_hbm, piv_hbm,
    both_ref,
    rhs_ref, columns_ref, slot_ref, slot_smem, blk, flat, tall, lm, pm, pum, kf, zf, rsend, rrecv, zsend, trecv, gid, early_hot, late_hot, xe, xl, acc, acc2, sfull,
    thi, tlo, smat, square, ga, gb,
    load_sem, rsend_sem, rrecv_sem, zsend_sem, tplane_sem, tspan_sem, gsend_sem, grecv_sem,
    gas_sem, gar_sem, gbs_sem, gbr_sem,
):
    nspan, nplane = 32, 8
    s = lax.axis_index("span")
    p = lax.axis_index("plane")
    x, z = s // 8, s % 8
    s_next, s_prev = lax.rem(s + 1, nspan), lax.rem(s + nspan - 1, nspan)
    p_next, p_prev = lax.rem(p + 1, nplane), lax.rem(p + nplane - 1, nplane)

    def plane_at(i):
        return lax.rem(p + i, nplane)

    small = []
    for n, (src, dst) in enumerate(
        (
            (rhs_hbm, rhs_ref), (slot_hbm, slot_smem), (slot_hbm, slot_ref),
            (columns_hbm, columns_ref),
        )
    ):
        small.append(pltpu.make_async_copy(src, dst, load_sem.at[7 + n]))
        small[-1].start()
    loads = []
    for n, src in enumerate((low_hbm, piv_hbm, upp_hbm)):
        loads.append(pltpu.make_async_copy(src, flat.at[n], load_sem.at[n]))
    for n in range(4):
        loads.append(
            pltpu.make_async_copy(
                blocks_hbm.at[pl.ds(8 * n, 8)], blk.at[pl.ds(8 * n, 8)], load_sem.at[3 + n]
            )
        )
    for load in loads:
        load.start()

    barrier = pltpu.get_barrier_semaphore()

    def near(dx, dz):
        return lax.rem(x + dx, 4) * 8 + lax.rem(z + dz, 8)

    def greet(device):
        pl.semaphore_signal(barrier, inc=1, device_id=device, device_id_type=MESH)

    first = [(near(i // 8, 0), plane_at(i % 8)) for i in range(1, 32)]
    second = [(near(0, i), p) for i in range(1, 8)]
    for device in first[:7] + first[7::8] + second + [(s_next, p), (s_prev, p)]:
        greet(device)

    for n in range(3):
        small[n].wait()
    k0 = pad_lanes(rhs_ref[...])
    kf[0] = k0

    lane = iota((1, W), 1)
    def to_slots(it):
        for t in range(F):
            rsend[it, t // 4, pl.ds(t % 4, 1), :] = kf[it, pl.ds(slot_smem[0, t], 1), :]

    to_slots(0)
    mine = pad_lanes(slot_ref[...].astype(F32)) + ((s * nplane + p) * F).astype(F32)
    gid[0] = jnp.broadcast_to(mine, (8, W))

    def send_pieces(it):
        for i in range(1, nplane):
            to = plane_at(i)
            pltpu.make_async_remote_copy(
                src_ref=rsend.at[it, to], dst_ref=rrecv.at[it, p],
                send_sem=rsend_sem.at[it], recv_sem=rrecv_sem.at[it],
                device_id=(s, to), device_id_type=MESH,
            ).start()
        pltpu.make_async_copy(rsend.at[it, p], rrecv.at[it, p], rrecv_sem.at[it]).start()

    for n in range(3):
        loads[n].wait()

    def relayout(g, _):
        for n in range(3):
            chunk = flat[n, :, pl.ds(pl.multiple_of(g * SEG, W), SEG)]
            for a in range(8):
                tall[n, pl.ds(pl.multiple_of((g * 8 + a) * F, F), F), :] = pad_lanes(
                    chunk[:, a * B : (a + 1) * B]
                )
        return 0

    lax.fori_loop(0, NGRP, relayout, 0)

    pl.semaphore_wait(barrier, 19)
    send_pieces(0)
    gid_copies = []
    for n, to in enumerate(((s, p_next), (s, p_prev), (s_next, p), (s_prev, p))):
        copy = pltpu.make_async_remote_copy(
            src_ref=gid.at[0], dst_ref=gid.at[n + 1],
            send_sem=gsend_sem.at[n], recv_sem=grecv_sem.at[n],
            device_id=to, device_id_type=MESH,
        )
        copy.start()
        gid_copies.append(copy)

    zeros48 = jnp.zeros((W - B, W), F32)

    def flip(m):
        return jnp.transpose(jnp.concatenate([m, zeros48], axis=0))[:B]

    def prepare(c, _):
        for n in range(8):
            row = 8 * c + n

            def matrix(which):
                return tall[which, pl.ds(row, B, stride=F), :]

            low, piv, upp = matrix(0), matrix(1), matrix(2)
            ph, pl_ = split(piv[:, :B])
            uh, ul = split(upp)
            both = bdot(ph, uh) + (bdot(ph, ul) + bdot(pl_, uh))
            if n % 2 == 0:
                lm[row], pm[row], pum[row] = flip(low), piv, both
            else:
                lm[row], pm[row], pum[row] = low, flip(piv), flip(both)
        return 0

    lax.fori_loop(0, F // 8, prepare, 0)

    square[...] = jnp.zeros_like(square)
    for it in range(ITERS):
        zsend[it, 0] = jnp.zeros((4, W), F32)
        zsend[it, nplane + 1] = jnp.zeros((4, W), F32)
    thi[...] = jnp.zeros_like(thi)
    tlo[...] = jnp.zeros_like(tlo)

    def set_up():
        for copy in gid_copies:
            copy.wait()
        below = jnp.where(p == 0, -1.0, gid[1])
        above = jnp.where(p == nplane - 1, -1.0, gid[2])
        rows = [below[0:1], gid[0][0:1], above[0:1], gid[3][0:1], gid[4][0:1]]
        stacked = jnp.concatenate(rows + [jnp.zeros((W - 5, W), F32)], axis=0)
        by_slot = jnp.transpose(stacked)[:F]
        n_at = iota((1, 2 * W), 1)
        blk_at = n_at // 4
        span_part = n_at >= 96
        dir_at = jnp.where(span_part, 3 + (blk_at - 24) // 8, blk_at % 3)
        slot_at = jnp.where(span_part, (n_at - 96) % F, (blk_at // 3) * 4 + n_at % 4)
        want = iota((F, 2 * W), 0) == slot_at
        numbers = jnp.zeros((F, 2 * W), F32)
        for d in range(5):
            numbers = numbers + jnp.where(want & (dir_at == d), by_slot[:, d : d + 1], 0.0)
        numbers = jnp.sum(numbers, axis=0, keepdims=True)
        numbers = jnp.where(iota((1, 2 * W), 1) < 160, numbers, -2.0)
        small[3].wait()
        cols = jnp.transpose(
            jnp.concatenate(
                [pad_lanes(columns_ref[...].astype(F32)), jnp.zeros((W - NBLK, W), F32)], axis=0
            )
        )[:F]
        for n, k in enumerate(EARLY):
            early_hot[pl.ds(n * F, F), :] = (cols[:, k : k + 1] == numbers[:, :W]).astype(BF16)
        for n, k in enumerate(LATE):
            late_hot[pl.ds(n * F, F), :] = (cols[:, k : k + 1] == numbers).astype(BF16)
        for n in range(4):
            loads[3 + n].wait()
        start = iota((SEG, W), 1) * B - iota((SEG, W), 0)

        def ones(n, _):
            ahead = start - n * SEG
            sfull[pl.ds(pl.multiple_of(n * SEG, SEG), SEG), :] = jnp.where(
                (ahead <= 0) & (ahead > -B), 1.0, 0.0
            ).astype(BF16)
            return 0

        lax.fori_loop(0, NGRP, ones, 0)

    def widen(it, start, count):
        got = trecv[it, pl.ds(start, count)].reshape(4 * count, W)[:, :B]
        hi, lo = split(jnp.concatenate([got] * 8, axis=1))
        thi[pl.ds(4 * start, 4 * count), :] = hi
        tlo[pl.ds(4 * start, 4 * count), :] = lo

    def weigh(row, half, which, picked, total):
        at = pl.ds(row, 8)
        for n, k in enumerate(which):
            term = blk[at, pl.ds(k * 6400 + half * 3200, 3200)] * jnp.concatenate(
                [picked[pl.ds(n * F + row, 8), :]] * 5, axis=1
            )
            total = term if total is None else total + term
        return total

    def one(it, _):
        pltpu.make_async_copy(rrecv.at[it], rrecv.at[it], rrecv_sem.at[it]).wait()
        for m in range(2):
            for c in range(8):
                square[pl.ds(m * 8 + c, 1), :] = rrecv[it, c, pl.ds(2 * m + 1, 1), :]
        odd = jnp.transpose(square[...])[:B]
        ys = [[], []]
        for j in range(16):
            for m in range(2):
                row = m * 16 + j
                if j == 0:
                    ys[m].append(rrecv[it, 0, pl.ds(2 * m, 1), :])
                elif j % 2:
                    idx = m * 8 + j // 2
                    base = jnp.where(lane == idx, odd, 0.0)
                    ys[m].append(
                        jnp.sum(base - lm[row] * ys[m][j - 1], axis=1, keepdims=True)
                    )
                else:
                    r = rrecv[it, j // 2, pl.ds(2 * m, 1), :]
                    ys[m].append(r - jnp.sum(lm[row] * ys[m][j - 1], axis=0, keepdims=True))
        zs = [None, None]
        even = jnp.zeros((B, W), F32)
        for j in reversed(range(16)):
            for m in range(2):
                row = m * 16 + j
                term = pm[row] * ys[m][j]
                if j < 15:
                    term = term - pum[row] * zs[m]
                zs[m] = jnp.sum(term, axis=j % 2 == 0 and 1 or 0, keepdims=True)
                if j % 2:
                    zsend[it, j // 2 + 1, pl.ds(2 * m + 1, 1), :] = zs[m]
                else:
                    even = jnp.where(lane == m * 8 + j // 2, zs[m], even)
        even = jnp.transpose(jnp.concatenate([even, zeros48], axis=0))
        for m in range(2):
            for c in range(8):
                zsend[it, c + 1, pl.ds(2 * m, 1), :] = even[m * 8 + c : m * 8 + c + 1]

        for i in range(nplane):
            to = plane_at(i)
            for n, there in enumerate((s_next, s_prev)):
                pltpu.make_async_remote_copy(
                    src_ref=zsend.at[it, to + 1], dst_ref=trecv.at[it, 24 + 8 * n + p],
                    send_sem=zsend_sem.at[it], recv_sem=tspan_sem.at[it],
                    device_id=(there, to), device_id_type=MESH,
                ).start()
        for i in range(1, nplane):
            to = plane_at(i)
            pltpu.make_async_remote_copy(
                src_ref=zsend.at[it, pl.ds(to, 3)], dst_ref=trecv.at[it, pl.ds(3 * p, 3)],
                send_sem=zsend_sem.at[it], recv_sem=tplane_sem.at[it],
                device_id=(s, to), device_id_type=MESH,
            ).start()
        pltpu.make_async_copy(
            zsend.at[it, pl.ds(p, 3)], trecv.at[it, pl.ds(3 * p, 3)], tplane_sem.at[it]
        ).start()

        @pl.when(it == 0)
        def _():
            set_up()

        part = trecv.at[it, pl.ds(0, 24)]
        pltpu.make_async_copy(part, part, tplane_sem.at[it]).wait()
        widen(it, 0, 24)
        hot = early_hot[...]
        xe[...] = bdot(hot, thi[pl.ds(0, W), :]) + bdot(hot, tlo[pl.ds(0, W), :])
        zf[it] = xe[pl.ds(0, F), pl.ds(0, W)]

        for row in range(0, F, 8):
            for half in range(2):
                acc[pl.ds(row, 8), pl.ds(half * 3200, 3200)] = weigh(row, half, EARLY, xe, None)

        part = trecv.at[it, pl.ds(24, 16)]
        pltpu.make_async_copy(part, part, tspan_sem.at[it]).wait()
        widen(it, 24, 16)
        hot = late_hot[...]
        xl[...] = bdot(hot, thi[...]) + bdot(hot, tlo[...])

        out = None
        for half in range(2):
            lanes = pl.ds(half * 3200, 3200)
            for row in range(0, F, 16):
                total = jnp.concatenate(
                    [weigh(n, half, LATE, xl, acc[pl.ds(n, 8), lanes]) for n in (row, row + 8)],
                    axis=0,
                )
                hi, lo = split(total)
                acc2[pl.ds(row, 16), lanes] = hi
                acc2[pl.ds(F + row, 16), lanes] = lo
            part = bdot(acc2[:, lanes], sfull[lanes, :])
            out = part if out is None else out + part
        kf[it + 1] = out[:F] + out[F:]

        @pl.when(it < ITERS - 1)
        def _():
            for t in range(F):
                rsend[it + 1, t // 4, pl.ds(t % 4, 1), :] = kf[
                    it + 1, pl.ds(slot_smem[0, t], 1), :
                ]
            send_pieces(it + 1)

        return 0

    lax.fori_loop(0, ITERS, one, 0)

    ks = [kf[i] for i in range(4)]
    tile = jnp.concatenate(
        [jnp.sum(ks[i] * ks[j], axis=0, keepdims=True) for i, j in PAIRS]
        + [jnp.zeros((6, W), F32)],
        axis=0,
    )
    tile = jnp.sum(tile, axis=1, keepdims=True)
    tile = jnp.where(iota((16, W), 0) == iota((16, W), 1), tile, 0.0)
    ga[0] = jnp.sum(tile, axis=0, keepdims=True)
    for i, to in enumerate(first):
        pltpu.make_async_remote_copy(
            src_ref=ga.at[0], dst_ref=ga.at[i + 1],
            send_sem=gas_sem.at[0], recv_sem=gar_sem.at[0],
            device_id=to, device_id_type=MESH,
        ).start()
    arrived = ga.at[pl.ds(1, 31)]
    pltpu.make_async_copy(arrived, arrived, gar_sem.at[0]).wait()
    gb[0] = jnp.sum(ga[...], axis=0)
    for i, to in enumerate(second):
        pltpu.make_async_remote_copy(
            src_ref=gb.at[0], dst_ref=gb.at[i + 1],
            send_sem=gbs_sem.at[0], recv_sem=gbr_sem.at[0],
            device_id=to, device_id_type=MESH,
        ).start()
    arrived_b = gb.at[pl.ds(1, 7)]
    pltpu.make_async_copy(arrived_b, arrived_b, gbr_sem.at[0]).wait()
    whole = jnp.sum(gb[...], axis=0)
    gram = {
        pair: jnp.broadcast_to(whole[:, n : n + 1], (1, W)) for n, pair in enumerate(PAIRS)
    }
    coef = coefficients(gram)
    solved = sum(coef[i] * zf[i] for i in range(ITERS))
    left = ks[0] - sum(coef[i] * ks[i + 1] for i in range(ITERS))
    both_ref[0] = solved[:, :B]
    both_ref[1] = left[:, :B]

    pltpu.make_async_copy(arrived, arrived, gas_sem.at[0]).wait()
    pltpu.make_async_copy(arrived_b, arrived_b, gbs_sem.at[0]).wait()
    for it in range(ITERS):
        out = rsend.at[it, pl.ds(0, 7)]
        pltpu.make_async_copy(out, out, rsend_sem.at[it]).wait()
        out = trecv.at[it, pl.ds(0, 37)]
        pltpu.make_async_copy(out, out, zsend_sem.at[it]).wait()


def on_device(rhs, blocks, columns, line_slot, line_lower, line_upper, pivot_inv):
    vmem = pl.BlockSpec(memory_space=pltpu.VMEM)
    hbm = pl.BlockSpec(memory_space=pl.ANY)
    out = jax.ShapeDtypeStruct((F, B), F32)
    dma = pltpu.SemaphoreType.DMA
    both = pl.pallas_call(
        kernel,
        out_shape=jax.ShapeDtypeStruct((2, F, B), F32),
        in_specs=[hbm] * 7,
        out_specs=vmem,
        scratch_shapes=[
            pltpu.VMEM((F, B), F32),
            pltpu.VMEM((NBLK, F), jnp.int32),
            pltpu.VMEM((1, F), jnp.int32),
            pltpu.SMEM((1, F), jnp.int32),
            pltpu.VMEM((F, NBLK * B * B), F32),
            pltpu.VMEM((3, F, B * B), F32),
            pltpu.VMEM((3, B * F, W), F32),
            pltpu.VMEM((F, B, W), F32),
            pltpu.VMEM((F, B, W), F32),
            pltpu.VMEM((F, B, W), F32),
            pltpu.VMEM((ITERS + 1, F, W), F32),
            pltpu.VMEM((ITERS, F, W), F32),
            pltpu.VMEM((ITERS, 8, 4, W), F32),
            pltpu.VMEM((ITERS, 8, 4, W), F32),
            pltpu.VMEM((ITERS, 10, 4, W), F32),
            pltpu.VMEM((ITERS, 40, 4, W), F32),
            pltpu.VMEM((5, 8, W), F32),
            pltpu.VMEM((3 * F, W), BF16),
            pltpu.VMEM((8 * F, 2 * W), BF16),
            pltpu.VMEM((3 * F, SEG), F32),
            pltpu.VMEM((8 * F, SEG), F32),
            pltpu.VMEM((F, B * B), F32),
            pltpu.VMEM((2 * F, B * B), BF16),
            pltpu.VMEM((B * B, W), BF16),
            pltpu.VMEM((2 * W, SEG), BF16),
            pltpu.VMEM((2 * W, SEG), BF16),
            pltpu.VMEM((SEG, W), BF16),
            pltpu.VMEM((W, W), F32),
            pltpu.VMEM((32, 1, W), F32),
            pltpu.VMEM((8, 1, W), F32),
            dma((11,)),
            dma((ITERS,)),
            dma((ITERS,)),
            dma((ITERS,)),
            dma((ITERS,)),
            dma((ITERS,)),
            dma((4,)),
            dma((4,)),
            dma((1,)),
            dma((1,)),
            dma((1,)),
            dma((1,)),
        ],
        compiler_params=pltpu.CompilerParams(
            collective_id=0, has_side_effects=True, vmem_limit_bytes=60 * 1024 * 1024
        ),
    )(rhs.T, blocks, columns, line_slot, line_lower, line_upper, pivot_inv)
    return both[0].T, both[1].T


def solution(mesh):
    return jax.shard_map(
        on_device,
        mesh=mesh,
        in_specs=(
            P(None, ("span", "plane")),
            P(("span", "plane"), None),
            P(None, ("span", "plane")),
            P(("span", "plane"), None),
            P(("span", "plane"), None),
            P(("span", "plane"), None),
            P(("span", "plane"), None),
        ),
        out_specs=(P(None, ("span", "plane")), P(None, ("span", "plane"))),
        check_vma=False,
    )
```

```python
import functools

import jax
import jax.numpy as jnp
from jax import lax
from jax.experimental import pallas as pl
from jax.experimental.pallas import tpu as pltpu
from jax.sharding import PartitionSpec as P

MESH = pl.DeviceIdType.MESH
F32 = jnp.float32
BF16 = jnp.bfloat16

B = 80
NBLK = 11
ITERS = 3
F = 32
W = 128
SEG = 640
NGRP = 10
EARLY = (0, 3, 4)
LATE = (1, 2, 5, 6, 7, 8, 9, 10)
PAIRS = [(i, j) for i in range(4) for j in range(i, 4)]


def iota(shape, axis):
    return lax.broadcasted_iota(jnp.int32, shape, axis)


def split(x):
    hi = x.astype(BF16)
    lo = (x - hi.astype(F32)).astype(BF16)
    return hi, lo


def bdot(a, b):
    return jnp.dot(a, b, preferred_element_type=F32)


def pad_lanes(x):
    return jnp.concatenate([x, jnp.zeros((x.shape[0], W - x.shape[1]), x.dtype)], axis=1)


def small_solve(factor, target):
    extent = len(target)
    forward_vals = []
    for row in range(extent):
        running = target[row]
        for inner in range(row):
            running = running - factor[row][inner] * forward_vals[inner]
        forward_vals.append(running / factor[row][row])
    backward_vals = [None] * extent
    for row in reversed(range(extent)):
        running = forward_vals[row]
        for inner in range(row + 1, extent):
            running = running - factor[inner][row] * backward_vals[inner]
        backward_vals[row] = running / factor[row][row]
    return backward_vals


def coefficients(gram):
    def inner(c, d):
        out = None
        for i in range(len(c)):
            for j in range(len(d)):
                term = c[i] * d[j] * gram[min(i, j), max(i, j)]
                out = term if out is None else out + term
        return out

    beta = jnp.sqrt(gram[0, 0] + 1e-6)
    zero = jnp.zeros_like(beta)
    basis = [[1.0 / beta]]
    h = [[zero] * ITERS for _ in range(ITERS + 1)]
    for step in range(ITERS):
        w = [zero] + basis[step]
        for i in range(step + 1):
            h[i][step] = inner(basis[i], w)
        for i in range(step + 1):
            for n, c in enumerate(basis[i]):
                w[n] = w[n] - h[i][step] * c
        h[step + 1][step] = jnp.sqrt(jnp.maximum(inner(w, w), 0.0) + 1e-6)
        basis.append([c / h[step + 1][step] for c in w])
    normal = [
        [sum(h[n][i] * h[n][j] for n in range(min(i, j) + 2)) for j in range(ITERS)]
        for i in range(ITERS)
    ]
    target = [beta * h[0][j] for j in range(ITERS)]
    factor = [[None] * ITERS for _ in range(ITERS)]
    for j in range(ITERS):
        diag = normal[j][j]
        for n in range(j):
            diag = diag - factor[j][n] * factor[j][n]
        factor[j][j] = jnp.sqrt(diag)
        for i in range(j + 1, ITERS):
            below = normal[i][j]
            for n in range(j):
                below = below - factor[i][n] * factor[j][n]
            factor[i][j] = below / factor[j][j]
    y = small_solve(factor, target)
    out = []
    for n in range(ITERS):
        out.append(sum(y[j] * basis[j][n] for j in range(n, ITERS)))
    return out


def kernel(
    rhs_hbm, blocks_hbm, columns_hbm, slot_hbm, low_hbm, upp_hbm, piv_hbm,
    both_ref,
    rhs_ref, columns_ref, slot_ref, slot_smem, blk, flat, tall, lm, pm, pum, kf, zf, rsend, rrecv, zsend, trecv, gid, early_hot, late_hot, xe, xl, acc, acc2, sfull,
    thi, tlo, smat, cm, dm, ga, gb,
    load_sem, rsend_sem, rrecv_sem, zsend_sem, tplane_sem, tspan_sem, gsend_sem, grecv_sem,
    gas_sem, gar_sem, gbs_sem, gbr_sem,
):
    nspan, nplane = 32, 8
    s = lax.axis_index("span")
    p = lax.axis_index("plane")
    x, z = s // 8, s % 8
    s_next, s_prev = lax.rem(s + 1, nspan), lax.rem(s + nspan - 1, nspan)
    p_next, p_prev = lax.rem(p + 1, nplane), lax.rem(p + nplane - 1, nplane)

    def plane_at(i):
        return lax.rem(p + i, nplane)

    small = []
    for n, (src, dst) in enumerate(
        (
            (rhs_hbm, rhs_ref), (slot_hbm, slot_smem), (slot_hbm, slot_ref),
            (columns_hbm, columns_ref),
        )
    ):
        small.append(pltpu.make_async_copy(src, dst, load_sem.at[7 + n]))
        small[-1].start()
    loads = []
    for n, src in enumerate((low_hbm, piv_hbm, upp_hbm)):
        loads.append(pltpu.make_async_copy(src, flat.at[n], load_sem.at[n]))
    for n in range(4):
        loads.append(
            pltpu.make_async_copy(
                blocks_hbm.at[pl.ds(8 * n, 8)], blk.at[pl.ds(8 * n, 8)], load_sem.at[3 + n]
            )
        )
    for load in loads[:3]:
        load.start()

    barrier = pltpu.get_barrier_semaphore()

    def near(dx, dz):
        return lax.rem(x + dx, 4) * 8 + lax.rem(z + dz, 8)

    def greet(device):
        pl.semaphore_signal(barrier, inc=1, device_id=device, device_id_type=MESH)

    first = [(near(i // 8, 0), plane_at(i % 8)) for i in range(1, 32)]
    second = [(near(0, i), p) for i in range(1, 8)]
    for device in first[:7] + first[7::8] + second + [(s_next, p), (s_prev, p)]:
        greet(device)

    for n in range(3):
        small[n].wait()
    k0 = pad_lanes(rhs_ref[...])
    kf[0] = k0

    lane = iota((1, W), 1)
    def to_slots(it):
        for t in range(F):
            rsend[it, t // 4, pl.ds(t % 4, 1), :] = kf[it, pl.ds(slot_smem[0, t], 1), :]

    to_slots(0)
    mine = pad_lanes(slot_ref[...].astype(F32)) + ((s * nplane + p) * F).astype(F32)
    gid[0] = jnp.broadcast_to(mine, (8, W))

    def send_pieces(it):
        for i in range(1, nplane):
            to = plane_at(i)
            pltpu.make_async_remote_copy(
                src_ref=rsend.at[it, to], dst_ref=rrecv.at[it, p],
                send_sem=rsend_sem.at[it], recv_sem=rrecv_sem.at[it],
                device_id=(s, to), device_id_type=MESH,
            ).start()
        pltpu.make_async_copy(rsend.at[it, p], rrecv.at[it, p], rrecv_sem.at[it]).start()

    for n in range(3):
        loads[n].wait()
    for load in loads[3:]:
        load.start()

    def relayout(g, _):
        for n in range(3):
            first_lane = pl.multiple_of(g * SEG, W)
            tiles = [flat[n, :, pl.ds(first_lane + v * W, W)] for v in range(5)]
            for a in range(8):
                tile, at = a * B // W, a * B % W
                row = tiles[tile]
                if at > W - B:
                    row = jnp.where(lane < at, tiles[tile + 1], row)
                if at:
                    row = pltpu.roll(row, W - at, 1)
                tall[n, pl.ds(pl.multiple_of((g * 8 + a) * F, F), F), :] = row
        return 0

    lax.fori_loop(0, NGRP, relayout, 0)

    pl.semaphore_wait(barrier, 19)
    send_pieces(0)
    gid_copies = []
    for n, to in enumerate(((s, p_next), (s, p_prev), (s_next, p), (s_prev, p))):
        copy = pltpu.make_async_remote_copy(
            src_ref=gid.at[0], dst_ref=gid.at[n + 1],
            send_sem=gsend_sem.at[n], recv_sem=grecv_sem.at[n],
            device_id=to, device_id_type=MESH,
        )
        copy.start()
        gid_copies.append(copy)

    zeros48 = jnp.zeros((W - B, W), F32)

    def flip(m):
        return jnp.transpose(jnp.concatenate([m, zeros48], axis=0))[:B]

    def product(a, b):
        ah, al = split(a[:, :B])
        bh, bl = split(b)
        part = bdot(jnp.concatenate([ah, al], axis=0), jnp.concatenate([bh, bl], axis=1))
        return part[:B, :W] + (part[:B, W:] + part[B:, :W])

    def prepare(c, _):
        for n in range(8):
            row = 8 * c + n

            def matrix(which):
                return tall[which, pl.ds(row, B, stride=F), :]

            low, piv, upp = matrix(0), matrix(1), matrix(2)
            both = product(piv, upp)
            if n % 2 == 0:
                lm[row], pm[row], pum[row] = flip(low), piv, both
            else:
                lm[row], pm[row], pum[row] = low, flip(piv), flip(both)
        return 0

    lax.fori_loop(0, F // 8, prepare, 0)

    for it in range(ITERS):
        zsend[it, 0] = jnp.zeros((4, W), F32)
        zsend[it, nplane + 1] = jnp.zeros((4, W), F32)
    thi[...] = jnp.zeros_like(thi)
    tlo[...] = jnp.zeros_like(tlo)

    def carried():
        def step(i, cs, ds, odd):
            new_c, new_d = [], []
            for m in range(2):
                low = tall[0, pl.ds(m * 16 + 8 + i, B, stride=F), :]
                c = -product(low, cs[m])
                upp = pum[m * 16 + 7 - i]
                d = -product(upp if odd else flip(upp), ds[m])
                cm[m * 8 + i] = c if odd else flip(c)
                dm[m * 8 + 7 - i] = d if odd else flip(d)
                new_c.append(c)
                new_d.append(d)
            return new_c, new_d

        def two(n, carry):
            cs, ds = step(2 * n + 1, *carry, True)
            return step(2 * n + 2, cs, ds, False)

        cs = [-tall[0, pl.ds(m * 16 + 8, B, stride=F), :] for m in range(2)]
        ds = [-flip(pum[m * 16 + 7]) for m in range(2)]
        cs, ds = lax.fori_loop(0, 3, two, (cs, ds))
        step(7, cs, ds, True)

    def set_up():
        for copy in gid_copies:
            copy.wait()
        below = jnp.where(p == 0, -1.0, gid[1])
        above = jnp.where(p == nplane - 1, -1.0, gid[2])
        rows = [below[0:1], gid[0][0:1], above[0:1], gid[3][0:1], gid[4][0:1]]
        stacked = jnp.concatenate(rows + [jnp.zeros((W - 5, W), F32)], axis=0)
        by_slot = jnp.transpose(stacked)[:F]
        n_at = iota((1, 2 * W), 1)
        blk_at = n_at // 4
        span_part = n_at >= 96
        dir_at = jnp.where(span_part, 3 + (blk_at - 24) // 8, blk_at % 3)
        slot_at = jnp.where(span_part, (n_at - 96) % F, (blk_at // 3) * 4 + n_at % 4)
        want = iota((F, 2 * W), 0) == slot_at
        numbers = jnp.zeros((F, 2 * W), F32)
        for d in range(5):
            numbers = numbers + jnp.where(want & (dir_at == d), by_slot[:, d : d + 1], 0.0)
        numbers = jnp.sum(numbers, axis=0, keepdims=True)
        numbers = jnp.where(iota((1, 2 * W), 1) < 160, numbers, -2.0)
        small[3].wait()
        cols = jnp.transpose(
            jnp.concatenate(
                [pad_lanes(columns_ref[...].astype(F32)), jnp.zeros((W - NBLK, W), F32)], axis=0
            )
        )[:F]
        for n, k in enumerate(EARLY):
            early_hot[pl.ds(n * F, F), :] = (cols[:, k : k + 1] == numbers[:, :W]).astype(BF16)
        for n, k in enumerate(LATE):
            late_hot[pl.ds(n * F, F), :] = (cols[:, k : k + 1] == numbers).astype(BF16)
        for n in range(4):
            loads[3 + n].wait()
        start = iota((SEG, W), 1) * B - iota((SEG, W), 0)

        def ones(n, _):
            ahead = start - n * SEG
            sfull[pl.ds(pl.multiple_of(n * SEG, SEG), SEG), :] = jnp.where(
                (ahead <= 0) & (ahead > -B), 1.0, 0.0
            ).astype(BF16)
            return 0

        lax.fori_loop(0, NGRP, ones, 0)

    def widen(it, start, count):
        got = trecv[it, pl.ds(start, count)].reshape(4 * count, W)[:, :B]
        hi, lo = split(jnp.concatenate([got] * 8, axis=1))
        thi[pl.ds(4 * start, 4 * count), :] = hi
        tlo[pl.ds(4 * start, 4 * count), :] = lo

    def weigh(row, half, which, picked, total):
        at = pl.ds(row, 8)
        for n, k in enumerate(which):
            term = blk[at, pl.ds(k * 6400 + half * 3200, 3200)] * jnp.concatenate(
                [picked[pl.ds(n * F + row, 8), :]] * 5, axis=1
            )
            total = term if total is None else total + term
        return total

    def one(it, _):
        pltpu.make_async_copy(rrecv.at[it], rrecv.at[it], rrecv_sem.at[it]).wait()
        diag = iota((B, W), 0) == iota((B, W), 1)

        def to_lanes(column):
            return jnp.sum(jnp.where(diag, column, 0.0), axis=0, keepdims=True)

        @pl.when(it == 0)
        def plain():
            ys = [[], []]
            for j in range(16):
                for m in range(2):
                    row = m * 16 + j
                    if j == 0:
                        ys[m].append(rrecv[it, 0, pl.ds(2 * m, 1), :])
                    elif j % 2:
                        base = jnp.where(diag, rrecv[it, j // 2, pl.ds(2 * m + 1, 1), :], 0.0)
                        ys[m].append(
                            jnp.sum(base - lm[row] * ys[m][j - 1], axis=1, keepdims=True)
                        )
                    else:
                        r = rrecv[it, j // 2, pl.ds(2 * m, 1), :]
                        ys[m].append(r - jnp.sum(lm[row] * ys[m][j - 1], axis=0, keepdims=True))
            zs = [None, None]
            for j in reversed(range(16)):
                for m in range(2):
                    row = m * 16 + j
                    term = pm[row] * ys[m][j]
                    if j < 15:
                        term = term - pum[row] * zs[m]
                    zs[m] = jnp.sum(term, axis=j % 2 == 0 and 1 or 0, keepdims=True)
                    if j % 2:
                        zsend[it, j // 2 + 1, pl.ds(2 * m + 1, 1), :] = zs[m]
                    else:
                        zsend[it, j // 2 + 1, pl.ds(2 * m, 1), :] = to_lanes(zs[m])

        @pl.when(it > 0)
        def halves():
            ys = [[None] * 16 for _ in range(2)]
            for i in range(8):
                for j in (i, 8 + i):
                    for m in range(2):
                        row = m * 16 + j
                        if j % 2:
                            base = jnp.where(diag, rrecv[it, j // 2, pl.ds(2 * m + 1, 1), :], 0.0)
                            ys[m][j] = jnp.sum(
                                base - lm[row] * ys[m][j - 1], axis=1, keepdims=True
                            )
                        else:
                            ys[m][j] = rrecv[it, j // 2, pl.ds(2 * m, 1), :]
                            if i:
                                ys[m][j] = ys[m][j] - jnp.sum(
                                    lm[row] * ys[m][j - 1], axis=0, keepdims=True
                                )
            for m in range(2):
                column = ys[m][7]
                across = to_lanes(column)
                ys[m][8] = ys[m][8] - jnp.sum(lm[m * 16 + 8] * column, axis=0, keepdims=True)
                for i in range(1, 8):
                    if i % 2:
                        more = jnp.sum(cm[m * 8 + i] * across, axis=1, keepdims=True)
                    else:
                        more = jnp.sum(cm[m * 8 + i] * column, axis=0, keepdims=True)
                    ys[m][8 + i] = ys[m][8 + i] + more
            zs = [[None] * 16 for _ in range(2)]
            for i in range(8):
                for j in (15 - i, 7 - i):
                    for m in range(2):
                        term = pm[m * 16 + j] * ys[m][j]
                        if i:
                            term = term - pum[m * 16 + j] * zs[m][j + 1]
                        zs[m][j] = jnp.sum(term, axis=j % 2 == 0 and 1 or 0, keepdims=True)
            for m in range(2):
                column = zs[m][8]
                across = to_lanes(column)
                for j in range(8):
                    if j == 7:
                        more = -jnp.sum(pum[m * 16 + 7] * column, axis=0, keepdims=True)
                    elif j % 2:
                        more = jnp.sum(dm[m * 8 + j] * column, axis=0, keepdims=True)
                    else:
                        more = jnp.sum(dm[m * 8 + j] * across, axis=1, keepdims=True)
                    zs[m][j] = zs[m][j] + more
                for j in range(16):
                    if j % 2:
                        zsend[it, j // 2 + 1, pl.ds(2 * m + 1, 1), :] = zs[m][j]
                    else:
                        zsend[it, j // 2 + 1, pl.ds(2 * m, 1), :] = to_lanes(zs[m][j])

        for i in range(nplane):
            to = plane_at(i)
            for n, there in enumerate((s_next, s_prev)):
                pltpu.make_async_remote_copy(
                    src_ref=zsend.at[it, to + 1], dst_ref=trecv.at[it, 24 + 8 * n + p],
                    send_sem=zsend_sem.at[it], recv_sem=tspan_sem.at[it],
                    device_id=(there, to), device_id_type=MESH,
                ).start()
        for i in range(1, nplane):
            to = plane_at(i)
            pltpu.make_async_remote_copy(
                src_ref=zsend.at[it, pl.ds(to, 3)], dst_ref=trecv.at[it, pl.ds(3 * p, 3)],
                send_sem=zsend_sem.at[it], recv_sem=tplane_sem.at[it],
                device_id=(s, to), device_id_type=MESH,
            ).start()
        pltpu.make_async_copy(
            zsend.at[it, pl.ds(p, 3)], trecv.at[it, pl.ds(3 * p, 3)], tplane_sem.at[it]
        ).start()

        @pl.when(it == 0)
        def _():
            set_up()
            carried()

        part = trecv.at[it, pl.ds(0, 24)]
        pltpu.make_async_copy(part, part, tplane_sem.at[it]).wait()
        widen(it, 0, 24)
        hot = early_hot[...]
        xe[...] = bdot(hot, thi[pl.ds(0, W), :]) + bdot(hot, tlo[pl.ds(0, W), :])
        zf[it] = xe[pl.ds(0, F), pl.ds(0, W)]

        for row in range(0, F, 8):
            for half in range(2):
                acc[pl.ds(row, 8), pl.ds(half * 3200, 3200)] = weigh(row, half, EARLY, xe, None)

        part = trecv.at[it, pl.ds(24, 16)]
        pltpu.make_async_copy(part, part, tspan_sem.at[it]).wait()
        widen(it, 24, 16)
        hot = late_hot[...]
        xl[...] = bdot(hot, thi[...]) + bdot(hot, tlo[...])

        out = None
        for half in range(2):
            lanes = pl.ds(half * 3200, 3200)
            for row in range(0, F, 16):
                total = jnp.concatenate(
                    [weigh(n, half, LATE, xl, acc[pl.ds(n, 8), lanes]) for n in (row, row + 8)],
                    axis=0,
                )
                hi, lo = split(total)
                acc2[pl.ds(row, 16), lanes] = hi
                acc2[pl.ds(F + row, 16), lanes] = lo
            part = bdot(acc2[:, lanes], sfull[lanes, :])
            out = part if out is None else out + part
        kf[it + 1] = out[:F] + out[F:]

        @pl.when(it < ITERS - 1)
        def _():
            for t in range(F):
                rsend[it + 1, t // 4, pl.ds(t % 4, 1), :] = kf[
                    it + 1, pl.ds(slot_smem[0, t], 1), :
                ]
            send_pieces(it + 1)

        return 0

    lax.fori_loop(0, ITERS, one, 0)

    ks = [kf[i] for i in range(4)]
    tile = jnp.concatenate(
        [jnp.sum(ks[i] * ks[j], axis=0, keepdims=True) for i, j in PAIRS]
        + [jnp.zeros((6, W), F32)],
        axis=0,
    )
    tile = jnp.sum(tile, axis=1, keepdims=True)
    tile = jnp.where(iota((16, W), 0) == iota((16, W), 1), tile, 0.0)
    ga[0] = jnp.sum(tile, axis=0, keepdims=True)
    for i, to in enumerate(first):
        pltpu.make_async_remote_copy(
            src_ref=ga.at[0], dst_ref=ga.at[i + 1],
            send_sem=gas_sem.at[0], recv_sem=gar_sem.at[0],
            device_id=to, device_id_type=MESH,
        ).start()
    arrived = ga.at[pl.ds(1, 31)]
    pltpu.make_async_copy(arrived, arrived, gar_sem.at[0]).wait()
    gb[0] = jnp.sum(ga[...], axis=0)
    for i, to in enumerate(second):
        pltpu.make_async_remote_copy(
            src_ref=gb.at[0], dst_ref=gb.at[i + 1],
            send_sem=gbs_sem.at[0], recv_sem=gbr_sem.at[0],
            device_id=to, device_id_type=MESH,
        ).start()
    arrived_b = gb.at[pl.ds(1, 7)]
    pltpu.make_async_copy(arrived_b, arrived_b, gbr_sem.at[0]).wait()
    whole = jnp.sum(gb[...], axis=0)
    gram = {
        pair: jnp.broadcast_to(whole[:, n : n + 1], (1, W)) for n, pair in enumerate(PAIRS)
    }
    coef = coefficients(gram)
    solved = sum(coef[i] * zf[i] for i in range(ITERS))
    left = ks[0] - sum(coef[i] * ks[i + 1] for i in range(ITERS))
    both_ref[0] = solved[:, :B]
    both_ref[1] = left[:, :B]

    pltpu.make_async_copy(arrived, arrived, gas_sem.at[0]).wait()
    pltpu.make_async_copy(arrived_b, arrived_b, gbs_sem.at[0]).wait()
    for it in range(ITERS):
        out = rsend.at[it, pl.ds(0, 7)]
        pltpu.make_async_copy(out, out, rsend_sem.at[it]).wait()
        out = trecv.at[it, pl.ds(0, 37)]
        pltpu.make_async_copy(out, out, zsend_sem.at[it]).wait()


def on_device(rhs, blocks, columns, line_slot, line_lower, line_upper, pivot_inv):
    vmem = pl.BlockSpec(memory_space=pltpu.VMEM)
    hbm = pl.BlockSpec(memory_space=pl.ANY)
    out = jax.ShapeDtypeStruct((F, B), F32)
    dma = pltpu.SemaphoreType.DMA
    both = pl.pallas_call(
        kernel,
        out_shape=jax.ShapeDtypeStruct((2, F, B), F32),
        in_specs=[hbm] * 7,
        out_specs=vmem,
        scratch_shapes=[
            pltpu.VMEM((F, B), F32),
            pltpu.VMEM((NBLK, F), jnp.int32),
            pltpu.VMEM((1, F), jnp.int32),
            pltpu.SMEM((1, F), jnp.int32),
            pltpu.VMEM((F, NBLK * B * B), F32),
            pltpu.VMEM((3, F, B * B), F32),
            pltpu.VMEM((3, B * F, W), F32),
            pltpu.VMEM((F, B, W), F32),
            pltpu.VMEM((F, B, W), F32),
            pltpu.VMEM((F, B, W), F32),
            pltpu.VMEM((ITERS + 1, F, W), F32),
            pltpu.VMEM((ITERS, F, W), F32),
            pltpu.VMEM((ITERS, 8, 4, W), F32),
            pltpu.VMEM((ITERS, 8, 4, W), F32),
            pltpu.VMEM((ITERS, 10, 4, W), F32),
            pltpu.VMEM((ITERS, 40, 4, W), F32),
            pltpu.VMEM((5, 8, W), F32),
            pltpu.VMEM((3 * F, W), BF16),
            pltpu.VMEM((8 * F, 2 * W), BF16),
            pltpu.VMEM((3 * F, SEG), F32),
            pltpu.VMEM((8 * F, SEG), F32),
            pltpu.VMEM((F, B * B), F32),
            pltpu.VMEM((2 * F, B * B), BF16),
            pltpu.VMEM((B * B, W), BF16),
            pltpu.VMEM((2 * W, SEG), BF16),
            pltpu.VMEM((2 * W, SEG), BF16),
            pltpu.VMEM((SEG, W), BF16),
            pltpu.VMEM((16, B, W), F32),
            pltpu.VMEM((16, B, W), F32),
            pltpu.VMEM((32, 1, W), F32),
            pltpu.VMEM((8, 1, W), F32),
            dma((11,)),
            dma((ITERS,)),
            dma((ITERS,)),
            dma((ITERS,)),
            dma((ITERS,)),
            dma((ITERS,)),
            dma((4,)),
            dma((4,)),
            dma((1,)),
            dma((1,)),
            dma((1,)),
            dma((1,)),
        ],
        compiler_params=pltpu.CompilerParams(
            collective_id=0, has_side_effects=True, vmem_limit_bytes=60 * 1024 * 1024
        ),
    )(rhs.T, blocks, columns, line_slot, line_lower, line_upper, pivot_inv)
    return both[0].T, both[1].T


def solution(mesh):
    return jax.shard_map(
        on_device,
        mesh=mesh,
        in_specs=(
            P(None, ("span", "plane")),
            P(("span", "plane"), None),
            P(None, ("span", "plane")),
            P(("span", "plane"), None),
            P(("span", "plane"), None),
            P(("span", "plane"), None),
            P(("span", "plane"), None),
        ),
        out_specs=(P(None, ("span", "plane")), P(None, ("span", "plane"))),
        check_vma=False,
    )
```

```python
import functools

import jax
import jax.numpy as jnp
from jax import lax
from jax.experimental import pallas as pl
from jax.experimental.pallas import tpu as pltpu
from jax.sharding import PartitionSpec as P

MESH = pl.DeviceIdType.MESH
F32 = jnp.float32
BF16 = jnp.bfloat16

B = 80
NBLK = 11
ITERS = 3
F = 32
W = 128
SEG = 640
NGRP = 10
EARLY = (0, 3, 4)
LATE = (1, 2, 5, 6, 7, 8, 9, 10)
PAIRS = [(i, j) for i in range(4) for j in range(i, 4)]


def iota(shape, axis):
    return lax.broadcasted_iota(jnp.int32, shape, axis)


def split(x):
    hi = x.astype(BF16)
    lo = (x - hi.astype(F32)).astype(BF16)
    return hi, lo


def bdot(a, b):
    return jnp.dot(a, b, preferred_element_type=F32)


def pad_lanes(x):
    return jnp.concatenate([x, jnp.zeros((x.shape[0], W - x.shape[1]), x.dtype)], axis=1)


def small_solve(factor, target):
    extent = len(target)
    forward_vals = []
    for row in range(extent):
        running = target[row]
        for inner in range(row):
            running = running - factor[row][inner] * forward_vals[inner]
        forward_vals.append(running / factor[row][row])
    backward_vals = [None] * extent
    for row in reversed(range(extent)):
        running = forward_vals[row]
        for inner in range(row + 1, extent):
            running = running - factor[inner][row] * backward_vals[inner]
        backward_vals[row] = running / factor[row][row]
    return backward_vals


def coefficients(gram):
    def inner(c, d):
        out = None
        for i in range(len(c)):
            for j in range(len(d)):
                term = c[i] * d[j] * gram[min(i, j), max(i, j)]
                out = term if out is None else out + term
        return out

    beta = jnp.sqrt(gram[0, 0] + 1e-6)
    zero = jnp.zeros_like(beta)
    basis = [[1.0 / beta]]
    h = [[zero] * ITERS for _ in range(ITERS + 1)]
    for step in range(ITERS):
        w = [zero] + basis[step]
        for i in range(step + 1):
            h[i][step] = inner(basis[i], w)
        for i in range(step + 1):
            for n, c in enumerate(basis[i]):
                w[n] = w[n] - h[i][step] * c
        h[step + 1][step] = jnp.sqrt(jnp.maximum(inner(w, w), 0.0) + 1e-6)
        basis.append([c / h[step + 1][step] for c in w])
    normal = [
        [sum(h[n][i] * h[n][j] for n in range(min(i, j) + 2)) for j in range(ITERS)]
        for i in range(ITERS)
    ]
    target = [beta * h[0][j] for j in range(ITERS)]
    factor = [[None] * ITERS for _ in range(ITERS)]
    for j in range(ITERS):
        diag = normal[j][j]
        for n in range(j):
            diag = diag - factor[j][n] * factor[j][n]
        factor[j][j] = jnp.sqrt(diag)
        for i in range(j + 1, ITERS):
            below = normal[i][j]
            for n in range(j):
                below = below - factor[i][n] * factor[j][n]
            factor[i][j] = below / factor[j][j]
    y = small_solve(factor, target)
    out = []
    for n in range(ITERS):
        out.append(sum(y[j] * basis[j][n] for j in range(n, ITERS)))
    return out


def kernel(
    rhs_hbm, blocks_hbm, columns_hbm, slot_hbm, low_hbm, upp_hbm, piv_hbm,
    both_ref,
    rhs_ref, columns_ref, slot_ref, slot_smem, blk, flat, tall, lm, pm, pum, kf, zf, rsend, rrecv, zsend, trecv, gid, early_hot, late_hot, xe, xl, acc, acc2, sfull,
    thi, tlo, smat, cm, dm, ga, gb,
    load_sem, rsend_sem, rrecv_sem, zsend_sem, tplane_sem, tspan_sem, gsend_sem, grecv_sem,
    gas_sem, gar_sem, gbs_sem, gbr_sem,
):
    nspan, nplane = 32, 8
    s = lax.axis_index("span")
    p = lax.axis_index("plane")
    x, z = s // 8, s % 8
    s_next, s_prev = lax.rem(s + 1, nspan), lax.rem(s + nspan - 1, nspan)
    p_next, p_prev = lax.rem(p + 1, nplane), lax.rem(p + nplane - 1, nplane)

    def plane_at(i):
        return lax.rem(p + i, nplane)

    small = []
    for n, (src, dst) in enumerate(
        (
            (rhs_hbm, rhs_ref), (slot_hbm, slot_smem), (slot_hbm, slot_ref),
            (columns_hbm, columns_ref),
        )
    ):
        small.append(pltpu.make_async_copy(src, dst, load_sem.at[7 + n]))
        small[-1].start()
    loads = []
    for n, src in enumerate((low_hbm, piv_hbm, upp_hbm)):
        loads.append(pltpu.make_async_copy(src, flat.at[n], load_sem.at[n]))
    for n in range(4):
        loads.append(
            pltpu.make_async_copy(
                blocks_hbm.at[pl.ds(8 * n, 8)], blk.at[pl.ds(8 * n, 8)], load_sem.at[3 + n]
            )
        )
    for load in loads[:3]:
        load.start()

    barrier = pltpu.get_barrier_semaphore()

    def near(dx, dz):
        return lax.rem(x + dx, 4) * 8 + lax.rem(z + dz, 8)

    def greet(device):
        pl.semaphore_signal(barrier, inc=1, device_id=device, device_id_type=MESH)

    first = [(near(i // 8, 0), plane_at(i % 8)) for i in range(1, 32)]
    second = [(near(0, i), p) for i in range(1, 8)]
    for device in first[:7] + first[7::8] + second + [(s_next, p), (s_prev, p)]:
        greet(device)

    for n in range(3):
        small[n].wait()
    k0 = pad_lanes(rhs_ref[...])
    kf[0] = k0

    lane = iota((1, W), 1)
    def to_slots(it):
        for t in range(F):
            rsend[it, t // 4, pl.ds(t % 4, 1), :] = kf[it, pl.ds(slot_smem[0, t], 1), :]

    to_slots(0)
    mine = pad_lanes(slot_ref[...].astype(F32)) + ((s * nplane + p) * F).astype(F32)
    gid[0] = jnp.broadcast_to(mine, (8, W))

    def send_pieces(it):
        for i in range(1, nplane):
            to = plane_at(i)
            pltpu.make_async_remote_copy(
                src_ref=rsend.at[it, to], dst_ref=rrecv.at[it, p],
                send_sem=rsend_sem.at[it], recv_sem=rrecv_sem.at[it],
                device_id=(s, to), device_id_type=MESH,
            ).start()
        pltpu.make_async_copy(rsend.at[it, p], rrecv.at[it, p], rrecv_sem.at[it]).start()

    for n in range(3):
        loads[n].wait()
    for load in loads[3:]:
        load.start()

    def relayout(g, _):
        for n in range(3):
            first_lane = pl.multiple_of(g * SEG, W)
            tiles = [flat[n, :, pl.ds(first_lane + v * W, W)] for v in range(5)]
            for a in range(8):
                tile, at = a * B // W, a * B % W
                row = tiles[tile]
                if at > W - B:
                    row = jnp.where(lane < at, tiles[tile + 1], row)
                if at:
                    row = pltpu.roll(row, W - at, 1)
                tall[n, pl.ds(pl.multiple_of((g * 8 + a) * F, F), F), :] = row
        return 0

    lax.fori_loop(0, NGRP, relayout, 0)

    pl.semaphore_wait(barrier, 19)
    send_pieces(0)
    gid_copies = []
    for n, to in enumerate(((s, p_next), (s, p_prev), (s_next, p), (s_prev, p))):
        copy = pltpu.make_async_remote_copy(
            src_ref=gid.at[0], dst_ref=gid.at[n + 1],
            send_sem=gsend_sem.at[n], recv_sem=grecv_sem.at[n],
            device_id=to, device_id_type=MESH,
        )
        copy.start()
        gid_copies.append(copy)

    zeros48 = jnp.zeros((W - B, W), F32)

    def flip(m):
        return jnp.transpose(jnp.concatenate([m, zeros48], axis=0))[:B]

    def product(a, b):
        ah, al = split(a[:, :B])
        bh, bl = split(b)
        part = bdot(jnp.concatenate([ah, al], axis=0), jnp.concatenate([bh, bl], axis=1))
        return part[:B, :W] + (part[:B, W:] + part[B:, :W])

    def prepare(c, _):
        for n in range(8):
            row = 8 * c + n

            def matrix(which):
                return tall[which, pl.ds(row, B, stride=F), :]

            low, piv, upp = matrix(0), matrix(1), matrix(2)
            both = product(piv, upp)
            if n % 2 == 0:
                lm[row], pm[row], pum[row] = flip(low), piv, both
            else:
                lm[row], pm[row], pum[row] = low, flip(piv), flip(both)
        return 0

    lax.fori_loop(0, F // 8, prepare, 0)

    for it in range(ITERS):
        zsend[it, 0] = jnp.zeros((4, W), F32)
        zsend[it, nplane + 1] = jnp.zeros((4, W), F32)
    thi[...] = jnp.zeros_like(thi)
    tlo[...] = jnp.zeros_like(tlo)

    def carried():
        def step(i, cs, ds, odd):
            new_c, new_d = [], []
            for m in range(2):
                low = tall[0, pl.ds(m * 16 + 8 + i, B, stride=F), :]
                c = -product(low, cs[m])
                upp = pum[m * 16 + 7 - i]
                d = -product(upp if odd else flip(upp), ds[m])
                cm[m * 8 + i] = c if odd else flip(c)
                dm[m * 8 + 7 - i] = d if odd else flip(d)
                new_c.append(c)
                new_d.append(d)
            return new_c, new_d

        def two(n, carry):
            cs, ds = step(2 * n + 1, *carry, True)
            return step(2 * n + 2, cs, ds, False)

        cs = [-tall[0, pl.ds(m * 16 + 8, B, stride=F), :] for m in range(2)]
        ds = [-flip(pum[m * 16 + 7]) for m in range(2)]
        cs, ds = lax.fori_loop(0, 3, two, (cs, ds))
        step(7, cs, ds, True)

    def set_up():
        for copy in gid_copies:
            copy.wait()
        below = jnp.where(p == 0, -1.0, gid[1])
        above = jnp.where(p == nplane - 1, -1.0, gid[2])
        rows = [below[0:1], gid[0][0:1], above[0:1], gid[3][0:1], gid[4][0:1]]
        stacked = jnp.concatenate(rows + [jnp.zeros((W - 5, W), F32)], axis=0)
        by_slot = jnp.transpose(stacked)[:F]
        n_at = iota((1, 2 * W), 1)
        blk_at = n_at // 4
        span_part = n_at >= 96
        dir_at = jnp.where(span_part, 3 + (blk_at - 24) // 8, blk_at % 3)
        slot_at = jnp.where(span_part, (n_at - 96) % F, (blk_at // 3) * 4 + n_at % 4)
        want = iota((F, 2 * W), 0) == slot_at
        numbers = jnp.zeros((F, 2 * W), F32)
        for d in range(5):
            numbers = numbers + jnp.where(want & (dir_at == d), by_slot[:, d : d + 1], 0.0)
        numbers = jnp.sum(numbers, axis=0, keepdims=True)
        numbers = jnp.where(iota((1, 2 * W), 1) < 160, numbers, -2.0)
        small[3].wait()
        cols = jnp.transpose(
            jnp.concatenate(
                [pad_lanes(columns_ref[...].astype(F32)), jnp.zeros((W - NBLK, W), F32)], axis=0
            )
        )[:F]
        for n, k in enumerate(EARLY):
            early_hot[pl.ds(n * F, F), :] = (cols[:, k : k + 1] == numbers[:, :W]).astype(BF16)
        for n, k in enumerate(LATE):
            late_hot[pl.ds(n * F, F), :] = (cols[:, k : k + 1] == numbers).astype(BF16)
        for n in range(4):
            loads[3 + n].wait()
        start = iota((SEG, W), 1) * B - iota((SEG, W), 0)

        def ones(n, _):
            ahead = start - n * SEG
            sfull[pl.ds(pl.multiple_of(n * SEG, SEG), SEG), :] = jnp.where(
                (ahead <= 0) & (ahead > -B), 1.0, 0.0
            ).astype(BF16)
            return 0

        lax.fori_loop(0, NGRP, ones, 0)

    def widen(it, start, count):
        got = trecv[it, pl.ds(start, count)].reshape(4 * count, W)[:, :B]
        hi, lo = split(jnp.concatenate([got] * 8, axis=1))
        thi[pl.ds(4 * start, 4 * count), :] = hi
        tlo[pl.ds(4 * start, 4 * count), :] = lo

    def weigh(row, half, which, picked, total):
        at = pl.ds(row, 8)
        for n, k in enumerate(which):
            term = blk[at, pl.ds(k * 6400 + half * 3200, 3200)] * jnp.concatenate(
                [picked[pl.ds(n * F + row, 8), :]] * 5, axis=1
            )
            total = term if total is None else total + term
        return total

    def one(it, _):
        pltpu.make_async_copy(rrecv.at[it], rrecv.at[it], rrecv_sem.at[it]).wait()
        diag = iota((B, W), 0) == iota((B, W), 1)

        def to_lanes(column):
            return jnp.sum(jnp.where(diag, column, 0.0), axis=0, keepdims=True)

        @pl.when(it == 0)
        def plain():
            ys = [[], []]
            for j in range(16):
                for m in range(2):
                    row = m * 16 + j
                    if j == 0:
                        ys[m].append(rrecv[it, 0, pl.ds(2 * m, 1), :])
                    elif j % 2:
                        base = jnp.where(diag, rrecv[it, j // 2, pl.ds(2 * m + 1, 1), :], 0.0)
                        ys[m].append(
                            jnp.sum(base - lm[row] * ys[m][j - 1], axis=1, keepdims=True)
                        )
                    else:
                        r = rrecv[it, j // 2, pl.ds(2 * m, 1), :]
                        ys[m].append(r - jnp.sum(lm[row] * ys[m][j - 1], axis=0, keepdims=True))
            zs = [None, None]
            for j in reversed(range(16)):
                for m in range(2):
                    row = m * 16 + j
                    term = pm[row] * ys[m][j]
                    if j < 15:
                        term = term - pum[row] * zs[m]
                    zs[m] = jnp.sum(term, axis=j % 2 == 0 and 1 or 0, keepdims=True)
                    if j % 2:
                        zsend[it, j // 2 + 1, pl.ds(2 * m + 1, 1), :] = zs[m]
                    else:
                        zsend[it, j // 2 + 1, pl.ds(2 * m, 1), :] = to_lanes(zs[m])

        @pl.when(it > 0)
        def halves():
            ys = [[None] * 16 for _ in range(2)]
            for i in range(8):
                for j in (i, 8 + i):
                    for m in range(2):
                        row = m * 16 + j
                        if j % 2:
                            base = jnp.where(diag, rrecv[it, j // 2, pl.ds(2 * m + 1, 1), :], 0.0)
                            ys[m][j] = jnp.sum(
                                base - lm[row] * ys[m][j - 1], axis=1, keepdims=True
                            )
                        else:
                            ys[m][j] = rrecv[it, j // 2, pl.ds(2 * m, 1), :]
                            if i:
                                ys[m][j] = ys[m][j] - jnp.sum(
                                    lm[row] * ys[m][j - 1], axis=0, keepdims=True
                                )
            for m in range(2):
                column = ys[m][7]
                across = to_lanes(column)
                ys[m][8] = ys[m][8] - jnp.sum(lm[m * 16 + 8] * column, axis=0, keepdims=True)
                for i in range(1, 8):
                    if i % 2:
                        more = jnp.sum(cm[m * 8 + i] * across, axis=1, keepdims=True)
                    else:
                        more = jnp.sum(cm[m * 8 + i] * column, axis=0, keepdims=True)
                    ys[m][8 + i] = ys[m][8 + i] + more
            zs = [[None] * 16 for _ in range(2)]
            for i in range(8):
                for j in (15 - i, 7 - i):
                    for m in range(2):
                        term = pm[m * 16 + j] * ys[m][j]
                        if i:
                            term = term - pum[m * 16 + j] * zs[m][j + 1]
                        zs[m][j] = jnp.sum(term, axis=j % 2 == 0 and 1 or 0, keepdims=True)
            for m in range(2):
                column = zs[m][8]
                across = to_lanes(column)
                for j in range(8):
                    if j == 7:
                        more = -jnp.sum(pum[m * 16 + 7] * column, axis=0, keepdims=True)
                    elif j % 2:
                        more = jnp.sum(dm[m * 8 + j] * column, axis=0, keepdims=True)
                    else:
                        more = jnp.sum(dm[m * 8 + j] * across, axis=1, keepdims=True)
                    zs[m][j] = zs[m][j] + more
                for j in range(16):
                    if j % 2:
                        zsend[it, j // 2 + 1, pl.ds(2 * m + 1, 1), :] = zs[m][j]
                    else:
                        zsend[it, j // 2 + 1, pl.ds(2 * m, 1), :] = to_lanes(zs[m][j])

        for i in range(nplane):
            to = plane_at(i)
            for n, there in enumerate((s_next, s_prev)):
                pltpu.make_async_remote_copy(
                    src_ref=zsend.at[it, to + 1], dst_ref=trecv.at[it, 24 + 8 * n + p],
                    send_sem=zsend_sem.at[it], recv_sem=tspan_sem.at[it],
                    device_id=(there, to), device_id_type=MESH,
                ).start()
        for i in range(1, nplane):
            to = plane_at(i)
            pltpu.make_async_remote_copy(
                src_ref=zsend.at[it, pl.ds(to, 3)], dst_ref=trecv.at[it, pl.ds(3 * p, 3)],
                send_sem=zsend_sem.at[it], recv_sem=tplane_sem.at[it],
                device_id=(s, to), device_id_type=MESH,
            ).start()
        pltpu.make_async_copy(
            zsend.at[it, pl.ds(p, 3)], trecv.at[it, pl.ds(3 * p, 3)], tplane_sem.at[it]
        ).start()

        @pl.when(it == 0)
        def _():
            set_up()
            carried()

        part = trecv.at[it, pl.ds(0, 24)]
        pltpu.make_async_copy(part, part, tplane_sem.at[it]).wait()
        widen(it, 0, 24)
        hot = early_hot[...]
        xe[...] = bdot(hot, thi[pl.ds(0, W), :]) + bdot(hot, tlo[pl.ds(0, W), :])
        zf[it] = xe[pl.ds(0, F), pl.ds(0, W)]

        for row in range(0, F, 8):
            for half in range(2):
                acc[pl.ds(row, 8), pl.ds(half * 3200, 3200)] = weigh(row, half, EARLY, xe, None)

        part = trecv.at[it, pl.ds(24, 16)]
        pltpu.make_async_copy(part, part, tspan_sem.at[it]).wait()
        widen(it, 24, 16)
        hot = late_hot[...]
        xl[...] = bdot(hot, thi[...]) + bdot(hot, tlo[...])

        out = None
        for half in range(2):
            lanes = pl.ds(half * 3200, 3200)
            for row in range(0, F, 16):
                total = jnp.concatenate(
                    [weigh(n, half, LATE, xl, acc[pl.ds(n, 8), lanes]) for n in (row, row + 8)],
                    axis=0,
                )
                hi, lo = split(total)
                acc2[pl.ds(row, 16), lanes] = hi
                acc2[pl.ds(F + row, 16), lanes] = lo
            part = bdot(acc2[:, lanes], sfull[lanes, :])
            out = part if out is None else out + part
        kf[it + 1] = out[:F] + out[F:]

        @pl.when(it < ITERS - 1)
        def _():
            for t in range(F):
                rsend[it + 1, t // 4, pl.ds(t % 4, 1), :] = kf[
                    it + 1, pl.ds(slot_smem[0, t], 1), :
                ]
            send_pieces(it + 1)

        return 0

    lax.fori_loop(0, ITERS, one, 0)

    ks = [kf[i] for i in range(4)]
    tile = jnp.concatenate(
        [jnp.sum(ks[i] * ks[j], axis=0, keepdims=True) for i, j in PAIRS]
        + [jnp.zeros((6, W), F32)],
        axis=0,
    )
    tile = jnp.sum(tile, axis=1, keepdims=True)
    tile = jnp.where(iota((16, W), 0) == iota((16, W), 1), tile, 0.0)
    ga[0] = jnp.sum(tile, axis=0, keepdims=True)
    for i, to in enumerate(first):
        pltpu.make_async_remote_copy(
            src_ref=ga.at[0], dst_ref=ga.at[i + 1],
            send_sem=gas_sem.at[0], recv_sem=gar_sem.at[0],
            device_id=to, device_id_type=MESH,
        ).start()
    arrived = ga.at[pl.ds(1, 31)]
    pltpu.make_async_copy(arrived, arrived, gar_sem.at[0]).wait()
    gb[0] = jnp.sum(ga[...], axis=0)
    for i, to in enumerate(second):
        pltpu.make_async_remote_copy(
            src_ref=gb.at[0], dst_ref=gb.at[i + 1],
            send_sem=gbs_sem.at[0], recv_sem=gbr_sem.at[0],
            device_id=to, device_id_type=MESH,
        ).start()
    arrived_b = gb.at[pl.ds(1, 7)]
    pltpu.make_async_copy(arrived_b, arrived_b, gbr_sem.at[0]).wait()
    whole = jnp.sum(gb[...], axis=0)
    gram = {
        pair: jnp.broadcast_to(whole[:, n : n + 1], (1, W)) for n, pair in enumerate(PAIRS)
    }
    coef = coefficients(gram)
    solved = sum(coef[i] * zf[i] for i in range(ITERS))
    left = ks[0] - sum(coef[i] * ks[i + 1] for i in range(ITERS))
    both_ref[0] = solved[:, :B]
    both_ref[1] = left[:, :B]

    pltpu.make_async_copy(arrived, arrived, gas_sem.at[0]).wait()
    pltpu.make_async_copy(arrived_b, arrived_b, gbs_sem.at[0]).wait()
    for it in range(ITERS):
        out = rsend.at[it, pl.ds(0, 7)]
        pltpu.make_async_copy(out, out, rsend_sem.at[it]).wait()
        out = trecv.at[it, pl.ds(0, 37)]
        pltpu.make_async_copy(out, out, zsend_sem.at[it]).wait()


def on_device(rhs, blocks, columns, line_slot, line_lower, line_upper, pivot_inv):
    vmem = pl.BlockSpec(memory_space=pltpu.VMEM)
    hbm = pl.BlockSpec(memory_space=pltpu.HBM)
    out = jax.ShapeDtypeStruct((F, B), F32)
    dma = pltpu.SemaphoreType.DMA
    both = pl.pallas_call(
        kernel,
        out_shape=jax.ShapeDtypeStruct((2, F, B), F32),
        in_specs=[hbm] * 7,
        out_specs=vmem,
        scratch_shapes=[
            pltpu.VMEM((F, B), F32),
            pltpu.VMEM((NBLK, F), jnp.int32),
            pltpu.VMEM((1, F), jnp.int32),
            pltpu.SMEM((1, F), jnp.int32),
            pltpu.VMEM((F, NBLK * B * B), F32),
            pltpu.VMEM((3, F, B * B), F32),
            pltpu.VMEM((3, B * F, W), F32),
            pltpu.VMEM((F, B, W), F32),
            pltpu.VMEM((F, B, W), F32),
            pltpu.VMEM((F, B, W), F32),
            pltpu.VMEM((ITERS + 1, F, W), F32),
            pltpu.VMEM((ITERS, F, W), F32),
            pltpu.VMEM((ITERS, 8, 4, W), F32),
            pltpu.VMEM((ITERS, 8, 4, W), F32),
            pltpu.VMEM((ITERS, 10, 4, W), F32),
            pltpu.VMEM((ITERS, 40, 4, W), F32),
            pltpu.VMEM((5, 8, W), F32),
            pltpu.VMEM((3 * F, W), BF16),
            pltpu.VMEM((8 * F, 2 * W), BF16),
            pltpu.VMEM((3 * F, SEG), F32),
            pltpu.VMEM((8 * F, SEG), F32),
            pltpu.VMEM((F, B * B), F32),
            pltpu.VMEM((2 * F, B * B), BF16),
            pltpu.VMEM((B * B, W), BF16),
            pltpu.VMEM((2 * W, SEG), BF16),
            pltpu.VMEM((2 * W, SEG), BF16),
            pltpu.VMEM((SEG, W), BF16),
            pltpu.VMEM((16, B, W), F32),
            pltpu.VMEM((16, B, W), F32),
            pltpu.VMEM((32, 1, W), F32),
            pltpu.VMEM((8, 1, W), F32),
            dma((11,)),
            dma((ITERS,)),
            dma((ITERS,)),
            dma((ITERS,)),
            dma((ITERS,)),
            dma((ITERS,)),
            dma((4,)),
            dma((4,)),
            dma((1,)),
            dma((1,)),
            dma((1,)),
            dma((1,)),
        ],
        compiler_params=pltpu.CompilerParams(
            collective_id=0, has_side_effects=True, vmem_limit_bytes=48 * 1024 * 1024
        ),
    )(
        *(
            pltpu.with_memory_space_constraint(given, pltpu.HBM)
            for given in (rhs.T, blocks, columns, line_slot, line_lower, line_upper, pivot_inv)
        )
    )
    return both[0].T, both[1].T


def solution(mesh):
    return jax.shard_map(
        on_device,
        mesh=mesh,
        in_specs=(
            P(None, ("span", "plane")),
            P(("span", "plane"), None),
            P(None, ("span", "plane")),
            P(("span", "plane"), None),
            P(("span", "plane"), None),
            P(("span", "plane"), None),
            P(("span", "plane"), None),
        ),
        out_specs=(P(None, ("span", "plane")), P(None, ("span", "plane"))),
        check_vma=False,
    )
```

```python
import functools

import jax
import jax.numpy as jnp
from jax import lax
from jax.experimental import pallas as pl
from jax.experimental.pallas import tpu as pltpu
from jax.sharding import PartitionSpec as P

MESH = pl.DeviceIdType.MESH
F32 = jnp.float32
BF16 = jnp.bfloat16

B = 80
NBLK = 11
ITERS = 3
F = 32
W = 128
SEG = 640
NGRP = 10
EARLY = (0, 3, 4)
LATE = (1, 2, 5, 6, 7, 8, 9, 10)
PAIRS = [(i, j) for i in range(4) for j in range(i, 4)]


def iota(shape, axis):
    return lax.broadcasted_iota(jnp.int32, shape, axis)


def split(x):
    hi = x.astype(BF16)
    lo = (x - hi.astype(F32)).astype(BF16)
    return hi, lo


def bdot(a, b):
    return jnp.dot(a, b, preferred_element_type=F32)


def pad_lanes(x):
    return jnp.concatenate([x, jnp.zeros((x.shape[0], W - x.shape[1]), x.dtype)], axis=1)


def add_rows(x):
    x = x[:40] + x[40:]
    last = x[32:]
    x = x[:16] + x[16:32]
    return jnp.sum((x[:8] + x[8:]) + last, axis=0, keepdims=True)


def add_lanes(x):
    return jnp.sum(x, axis=1, keepdims=True)


def small_solve(factor, target):
    extent = len(target)
    forward_vals = []
    for row in range(extent):
        running = target[row]
        for inner in range(row):
            running = running - factor[row][inner] * forward_vals[inner]
        forward_vals.append(running * factor[row][row])
    backward_vals = [None] * extent
    for row in reversed(range(extent)):
        running = forward_vals[row]
        for inner in range(row + 1, extent):
            running = running - factor[inner][row] * backward_vals[inner]
        backward_vals[row] = running * factor[row][row]
    return backward_vals


def coefficients(gram):
    def inner(c, d):
        out = None
        for i in range(len(c)):
            for j in range(len(d)):
                term = c[i] * d[j] * gram[min(i, j), max(i, j)]
                out = term if out is None else out + term
        return out

    square = gram[0, 0] + 1e-6
    scale = lax.rsqrt(square)
    beta = square * scale
    zero = jnp.zeros_like(beta)
    basis = [[scale]]
    h = [[zero] * ITERS for _ in range(ITERS + 1)]
    for step in range(ITERS):
        w = [zero] + basis[step]
        for i in range(step + 1):
            h[i][step] = inner(basis[i], w)
        for i in range(step + 1):
            for n, c in enumerate(basis[i]):
                w[n] = w[n] - h[i][step] * c
        square = jnp.maximum(inner(w, w), 0.0) + 1e-6
        scale = lax.rsqrt(square)
        h[step + 1][step] = square * scale
        basis.append([c * scale for c in w])
    normal = [
        [sum(h[n][i] * h[n][j] for n in range(min(i, j) + 2)) for j in range(ITERS)]
        for i in range(ITERS)
    ]
    target = [beta * h[0][j] for j in range(ITERS)]
    factor = [[None] * ITERS for _ in range(ITERS)]
    for j in range(ITERS):
        diag = normal[j][j]
        for n in range(j):
            diag = diag - factor[j][n] * factor[j][n]
        factor[j][j] = lax.rsqrt(diag)
        for i in range(j + 1, ITERS):
            below = normal[i][j]
            for n in range(j):
                below = below - factor[i][n] * factor[j][n]
            factor[i][j] = below * factor[j][j]
    y = small_solve(factor, target)
    out = []
    for n in range(ITERS):
        out.append(sum(y[j] * basis[j][n] for j in range(n, ITERS)))
    return out


def kernel(
    rhs_hbm, blocks_hbm, columns_hbm, slot_hbm, low_hbm, upp_hbm, piv_hbm,
    both_ref,
    rhs_ref, columns_ref, slot_ref, slot_smem, blk, flat, tall, lm, pm, pum, kf, zf, rsend, rrecv, zsend, trecv, gid, early_hot, late_hot, xe, xl, acc, acc2, sfull,
    thi, tlo, smat, cm, dm, ga, gb,
    load_sem, rsend_sem, rrecv_sem, zsend_sem, tplane_sem, tspan_sem, gsend_sem, grecv_sem,
    gas_sem, gar_sem, gbs_sem, gbr_sem,
):
    nspan, nplane = 32, 8
    s = lax.axis_index("span")
    p = lax.axis_index("plane")
    x, z = s // 8, s % 8
    s_next, s_prev = lax.rem(s + 1, nspan), lax.rem(s + nspan - 1, nspan)
    p_next, p_prev = lax.rem(p + 1, nplane), lax.rem(p + nplane - 1, nplane)

    peers = [lax.rem(p + i, nplane) for i in range(nplane)]

    def plane_at(i):
        return peers[i]

    small = []
    for n, (src, dst) in enumerate(
        (
            (rhs_hbm, rhs_ref), (slot_hbm, slot_smem), (slot_hbm, slot_ref),
            (columns_hbm, columns_ref),
        )
    ):
        small.append(pltpu.make_async_copy(src, dst, load_sem.at[7 + n]))
        small[-1].start()
    loads = []
    for n, src in enumerate((low_hbm, piv_hbm, upp_hbm)):
        loads.append(pltpu.make_async_copy(src, flat.at[n], load_sem.at[n]))
    for n in range(4):
        loads.append(
            pltpu.make_async_copy(
                blocks_hbm.at[pl.ds(8 * n, 8)], blk.at[pl.ds(8 * n, 8)], load_sem.at[3 + n]
            )
        )
    for load in loads[:3]:
        load.start()

    barrier = pltpu.get_barrier_semaphore()

    def near(dx, dz):
        return lax.rem(x + dx, 4) * 8 + lax.rem(z + dz, 8)

    def greet(device):
        pl.semaphore_signal(barrier, inc=1, device_id=device, device_id_type=MESH)

    far = (4, 3, 5, 2, 6, 1, 7, 0)
    first = [(near(i, 0), plane_at(n)) for i in (2, 1, 3, 0) for n in far if i or n]
    second = [(near(0, i), p) for i in far[:7]]
    for device in first[24:] + first[7:24:8] + second + [(s_next, p), (s_prev, p)]:
        greet(device)

    for n in range(3):
        small[n].wait()
    k0 = pad_lanes(rhs_ref[...])
    kf[0] = k0

    lane = iota((1, W), 1)
    def to_slots(it):
        for t in range(F):
            rsend[it, t // 4, pl.ds(t % 4, 1), :] = kf[it, pl.ds(slot_smem[0, t], 1), :]

    to_slots(0)
    mine = pad_lanes(slot_ref[...].astype(F32)) + ((s * nplane + p) * F).astype(F32)
    gid[0] = jnp.broadcast_to(mine, (8, W))

    def send_pieces(it):
        for i in far[:7]:
            to = plane_at(i)
            pltpu.make_async_remote_copy(
                src_ref=rsend.at[it, to], dst_ref=rrecv.at[it, p],
                send_sem=rsend_sem.at[it], recv_sem=rrecv_sem.at[it],
                device_id=(s, to), device_id_type=MESH,
            ).start()
        pltpu.make_async_copy(rsend.at[it, p], rrecv.at[it, p], rrecv_sem.at[it]).start()

    for n in range(3):
        loads[n].wait()
    for load in loads[3:]:
        load.start()

    def relayout(g, _):
        for n in range(3):
            first_lane = pl.multiple_of(g * SEG, W)
            tiles = [flat[n, :, pl.ds(first_lane + v * W, W)] for v in range(5)]
            for a in range(8):
                tile, at = a * B // W, a * B % W
                row = tiles[tile]
                if at > W - B:
                    row = jnp.where(lane < at, tiles[tile + 1], row)
                if at:
                    row = pltpu.roll(row, W - at, 1)
                tall[n, pl.ds(pl.multiple_of((g * 8 + a) * F, F), F), :] = row
        return 0

    lax.fori_loop(0, NGRP, relayout, 0)

    pl.semaphore_wait(barrier, 19)
    send_pieces(0)
    gid_copies = []
    for n, to in enumerate(((s, p_next), (s, p_prev), (s_next, p), (s_prev, p))):
        copy = pltpu.make_async_remote_copy(
            src_ref=gid.at[0], dst_ref=gid.at[n + 1],
            send_sem=gsend_sem.at[n], recv_sem=grecv_sem.at[n],
            device_id=to, device_id_type=MESH,
        )
        copy.start()
        gid_copies.append(copy)

    zeros48 = jnp.zeros((W - B, W), F32)

    def flip(m):
        return jnp.transpose(jnp.concatenate([m, zeros48], axis=0))[:B]

    def product(a, b):
        ah, al = split(a[:, :B])
        bh, bl = split(b)
        part = bdot(jnp.concatenate([ah, al], axis=0), jnp.concatenate([bh, bl], axis=1))
        return part[:B, :W] + (part[:B, W:] + part[B:, :W])

    def prepare(c, _):
        for n in range(8):
            row = 8 * c + n

            def matrix(which):
                return tall[which, pl.ds(row, B, stride=F), :]

            low, piv, upp = matrix(0), matrix(1), matrix(2)
            both = product(piv, upp)
            if n % 2 == 0:
                lm[row], pm[row], pum[row] = flip(low), piv, both
            else:
                lm[row], pm[row], pum[row] = low, flip(piv), flip(both)
        return 0

    lax.fori_loop(0, F // 8, prepare, 0)

    for it in range(ITERS):
        zsend[it, 0] = jnp.zeros((4, W), F32)
        zsend[it, nplane + 1] = jnp.zeros((4, W), F32)
    thi[...] = jnp.zeros_like(thi)
    tlo[...] = jnp.zeros_like(tlo)

    def carried():
        def step(i, cs, ds, odd):
            new_c, new_d = [], []
            for m in range(2):
                low = tall[0, pl.ds(m * 16 + 8 + i, B, stride=F), :]
                c = -product(low, cs[m])
                upp = pum[m * 16 + 7 - i]
                d = -product(upp if odd else flip(upp), ds[m])
                cm[m * 8 + i] = c if odd else flip(c)
                dm[m * 8 + 7 - i] = d if odd else flip(d)
                new_c.append(c)
                new_d.append(d)
            return new_c, new_d

        def two(n, carry):
            cs, ds = step(2 * n + 1, *carry, True)
            return step(2 * n + 2, cs, ds, False)

        cs = [-tall[0, pl.ds(m * 16 + 8, B, stride=F), :] for m in range(2)]
        ds = [-flip(pum[m * 16 + 7]) for m in range(2)]
        cs, ds = lax.fori_loop(0, 3, two, (cs, ds))
        step(7, cs, ds, True)

    def set_up():
        for copy in gid_copies:
            copy.wait()
        below = jnp.where(p == 0, -1.0, gid[1])
        above = jnp.where(p == nplane - 1, -1.0, gid[2])
        rows = [below[0:1], gid[0][0:1], above[0:1], gid[3][0:1], gid[4][0:1]]
        stacked = jnp.concatenate(rows + [jnp.zeros((W - 5, W), F32)], axis=0)
        by_slot = jnp.transpose(stacked)[:F]
        n_at = iota((1, 2 * W), 1)
        blk_at = n_at // 4
        span_part = n_at >= 96
        dir_at = jnp.where(span_part, 3 + (blk_at - 24) // 8, blk_at % 3)
        slot_at = jnp.where(span_part, (n_at - 96) % F, (blk_at // 3) * 4 + n_at % 4)
        want = iota((F, 2 * W), 0) == slot_at
        numbers = jnp.zeros((F, 2 * W), F32)
        for d in range(5):
            numbers = numbers + jnp.where(want & (dir_at == d), by_slot[:, d : d + 1], 0.0)
        numbers = jnp.sum(numbers, axis=0, keepdims=True)
        numbers = jnp.where(iota((1, 2 * W), 1) < 160, numbers, -2.0)
        small[3].wait()
        cols = jnp.transpose(
            jnp.concatenate(
                [pad_lanes(columns_ref[...].astype(F32)), jnp.zeros((W - NBLK, W), F32)], axis=0
            )
        )[:F]
        for n, k in enumerate(EARLY):
            early_hot[pl.ds(n * F, F), :] = (cols[:, k : k + 1] == numbers[:, :W]).astype(BF16)
        for n, k in enumerate(LATE):
            late_hot[pl.ds(n * F, F), :] = (cols[:, k : k + 1] == numbers).astype(BF16)
        for n in range(4):
            loads[3 + n].wait()
        start = iota((SEG, W), 1) * B - iota((SEG, W), 0)

        def ones(n, _):
            ahead = start - n * SEG
            sfull[pl.ds(pl.multiple_of(n * SEG, SEG), SEG), :] = jnp.where(
                (ahead <= 0) & (ahead > -B), 1.0, 0.0
            ).astype(BF16)
            return 0

        lax.fori_loop(0, NGRP, ones, 0)

    def widen(it, start, count):
        got = trecv[it, pl.ds(start, count)].reshape(4 * count, W)[:, :B]
        hi, lo = split(jnp.concatenate([got] * 8, axis=1))
        thi[pl.ds(4 * start, 4 * count), :] = hi
        tlo[pl.ds(4 * start, 4 * count), :] = lo

    def weigh(row, half, which, picked, total):
        at = pl.ds(row, 8)
        for n, k in enumerate(which):
            term = blk[at, pl.ds(k * 6400 + half * 3200, 3200)] * jnp.concatenate(
                [picked[pl.ds(n * F + row, 8), :]] * 5, axis=1
            )
            total = term if total is None else total + term
        return total

    def one(it, _):
        pltpu.make_async_copy(rrecv.at[it], rrecv.at[it], rrecv_sem.at[it]).wait()
        diag = iota((B, W), 0) == iota((B, W), 1)

        def to_lanes(column):
            return add_rows(jnp.where(diag, column, 0.0))

        @pl.when(it == 0)
        def plain():
            ys = [[], []]
            for j in range(16):
                for m in range(2):
                    row = m * 16 + j
                    if j == 0:
                        ys[m].append(rrecv[it, 0, pl.ds(2 * m, 1), :])
                    elif j % 2:
                        base = jnp.where(diag, rrecv[it, j // 2, pl.ds(2 * m + 1, 1), :], 0.0)
                        ys[m].append(
                            add_lanes(base - lm[row] * ys[m][j - 1])
                        )
                    else:
                        r = rrecv[it, j // 2, pl.ds(2 * m, 1), :]
                        ys[m].append(r - add_rows(lm[row] * ys[m][j - 1]))
            zs = [None, None]
            for j in reversed(range(16)):
                for m in range(2):
                    row = m * 16 + j
                    term = pm[row] * ys[m][j]
                    if j < 15:
                        term = term - pum[row] * zs[m]
                    zs[m] = add_lanes(term) if j % 2 == 0 else add_rows(term)
                    if j % 2:
                        zsend[it, j // 2 + 1, pl.ds(2 * m + 1, 1), :] = zs[m]
                    else:
                        zsend[it, j // 2 + 1, pl.ds(2 * m, 1), :] = to_lanes(zs[m])

        @pl.when(it > 0)
        def halves():
            ys = [[None] * 16 for _ in range(2)]
            for i in range(8):
                for j in (i, 8 + i):
                    for m in range(2):
                        row = m * 16 + j
                        if j % 2:
                            base = jnp.where(diag, rrecv[it, j // 2, pl.ds(2 * m + 1, 1), :], 0.0)
                            ys[m][j] = add_lanes(base - lm[row] * ys[m][j - 1])
                        else:
                            ys[m][j] = rrecv[it, j // 2, pl.ds(2 * m, 1), :]
                            if i:
                                ys[m][j] = ys[m][j] - add_rows(lm[row] * ys[m][j - 1])
            for m in range(2):
                column = ys[m][7]
                across = to_lanes(column)
                ys[m][8] = ys[m][8] - add_rows(lm[m * 16 + 8] * column)
                for i in range(1, 8):
                    if i % 2:
                        more = add_lanes(cm[m * 8 + i] * across)
                    else:
                        more = add_rows(cm[m * 8 + i] * column)
                    ys[m][8 + i] = ys[m][8 + i] + more
            zs = [[None] * 16 for _ in range(2)]
            for i in range(8):
                for j in (15 - i, 7 - i):
                    for m in range(2):
                        term = pm[m * 16 + j] * ys[m][j]
                        if i:
                            term = term - pum[m * 16 + j] * zs[m][j + 1]
                        zs[m][j] = add_lanes(term) if j % 2 == 0 else add_rows(term)
            for m in range(2):
                column = zs[m][8]
                across = to_lanes(column)
                for j in range(8):
                    if j == 7:
                        more = -add_rows(pum[m * 16 + 7] * column)
                    elif j % 2:
                        more = add_rows(dm[m * 8 + j] * column)
                    else:
                        more = add_lanes(dm[m * 8 + j] * across)
                    zs[m][j] = zs[m][j] + more
                for j in range(16):
                    if j % 2:
                        zsend[it, j // 2 + 1, pl.ds(2 * m + 1, 1), :] = zs[m][j]
                    else:
                        zsend[it, j // 2 + 1, pl.ds(2 * m, 1), :] = to_lanes(zs[m][j])

        for i in far:
            to = plane_at(i)
            for n, there in enumerate((s_next, s_prev)):
                pltpu.make_async_remote_copy(
                    src_ref=zsend.at[it, to + 1], dst_ref=trecv.at[it, 24 + 8 * n + p],
                    send_sem=zsend_sem.at[it], recv_sem=tspan_sem.at[it],
                    device_id=(there, to), device_id_type=MESH,
                ).start()
        for i in far[:7]:
            to = plane_at(i)
            pltpu.make_async_remote_copy(
                src_ref=zsend.at[it, pl.ds(to, 3)], dst_ref=trecv.at[it, pl.ds(3 * p, 3)],
                send_sem=zsend_sem.at[it], recv_sem=tplane_sem.at[it],
                device_id=(s, to), device_id_type=MESH,
            ).start()
        pltpu.make_async_copy(
            zsend.at[it, pl.ds(p, 3)], trecv.at[it, pl.ds(3 * p, 3)], tplane_sem.at[it]
        ).start()

        @pl.when(it == 0)
        def _():
            set_up()
            carried()

        part = trecv.at[it, pl.ds(0, 24)]
        pltpu.make_async_copy(part, part, tplane_sem.at[it]).wait()
        widen(it, 0, 24)
        hot = early_hot[...]
        xe[...] = bdot(hot, thi[pl.ds(0, W), :]) + bdot(hot, tlo[pl.ds(0, W), :])
        zf[it] = xe[pl.ds(0, F), pl.ds(0, W)]

        for row in range(0, F, 8):
            for half in range(2):
                acc[pl.ds(row, 8), pl.ds(half * 3200, 3200)] = weigh(row, half, EARLY, xe, None)

        part = trecv.at[it, pl.ds(24, 16)]
        pltpu.make_async_copy(part, part, tspan_sem.at[it]).wait()
        widen(it, 24, 16)
        hot = late_hot[...]
        xl[...] = bdot(hot, thi[...]) + bdot(hot, tlo[...])

        out = None
        for half in range(2):
            lanes = pl.ds(half * 3200, 3200)
            for row in range(0, F, 16):
                total = jnp.concatenate(
                    [weigh(n, half, LATE, xl, acc[pl.ds(n, 8), lanes]) for n in (row, row + 8)],
                    axis=0,
                )
                hi, lo = split(total)
                acc2[pl.ds(row, 16), lanes] = hi
                acc2[pl.ds(F + row, 16), lanes] = lo
            part = bdot(acc2[:, lanes], sfull[lanes, :])
            out = part if out is None else out + part
        kf[it + 1] = out[:F] + out[F:]

        @pl.when(it < ITERS - 1)
        def _():
            for t in range(F):
                rsend[it + 1, t // 4, pl.ds(t % 4, 1), :] = kf[
                    it + 1, pl.ds(slot_smem[0, t], 1), :
                ]
            send_pieces(it + 1)

        return 0

    lax.fori_loop(0, ITERS, one, 0)

    ks = [kf[i] for i in range(4)]
    tile = jnp.concatenate(
        [jnp.sum(ks[i] * ks[j], axis=0, keepdims=True) for i, j in PAIRS]
        + [jnp.zeros((6, W), F32)],
        axis=0,
    )
    tile = jnp.sum(tile, axis=1, keepdims=True)
    tile = jnp.where(iota((16, W), 0) == iota((16, W), 1), tile, 0.0)
    ga[0] = jnp.sum(tile, axis=0, keepdims=True)
    for i, to in enumerate(first):
        pltpu.make_async_remote_copy(
            src_ref=ga.at[0], dst_ref=ga.at[i + 1],
            send_sem=gas_sem.at[0], recv_sem=gar_sem.at[0],
            device_id=to, device_id_type=MESH,
        ).start()
    arrived = ga.at[pl.ds(1, 31)]
    pltpu.make_async_copy(arrived, arrived, gar_sem.at[0]).wait()
    gb[0] = jnp.sum(ga[...], axis=0)
    for i, to in enumerate(second):
        pltpu.make_async_remote_copy(
            src_ref=gb.at[0], dst_ref=gb.at[i + 1],
            send_sem=gbs_sem.at[0], recv_sem=gbr_sem.at[0],
            device_id=to, device_id_type=MESH,
        ).start()
    arrived_b = gb.at[pl.ds(1, 7)]
    pltpu.make_async_copy(arrived_b, arrived_b, gbr_sem.at[0]).wait()
    whole = jnp.sum(gb[...], axis=0)
    gram = {
        pair: jnp.broadcast_to(whole[:, n : n + 1], (1, W)) for n, pair in enumerate(PAIRS)
    }
    coef = coefficients(gram)
    solved = sum(coef[i] * zf[i] for i in range(ITERS))
    left = ks[0] - sum(coef[i] * ks[i + 1] for i in range(ITERS))
    both_ref[0] = solved[:, :B]
    both_ref[1] = left[:, :B]

    pltpu.make_async_copy(arrived, arrived, gas_sem.at[0]).wait()
    pltpu.make_async_copy(arrived_b, arrived_b, gbs_sem.at[0]).wait()
    for it in range(ITERS):
        out = rsend.at[it, pl.ds(0, 7)]
        pltpu.make_async_copy(out, out, rsend_sem.at[it]).wait()
        out = trecv.at[it, pl.ds(0, 37)]
        pltpu.make_async_copy(out, out, zsend_sem.at[it]).wait()


def on_device(rhs, blocks, columns, line_slot, line_lower, line_upper, pivot_inv):
    vmem = pl.BlockSpec(memory_space=pltpu.VMEM)
    hbm = pl.BlockSpec(memory_space=pltpu.HBM)
    out = jax.ShapeDtypeStruct((F, B), F32)
    dma = pltpu.SemaphoreType.DMA
    both = pl.pallas_call(
        kernel,
        out_shape=jax.ShapeDtypeStruct((2, F, B), F32),
        in_specs=[hbm] * 7,
        out_specs=vmem,
        scratch_shapes=[
            pltpu.VMEM((F, B), F32),
            pltpu.VMEM((NBLK, F), jnp.int32),
            pltpu.VMEM((1, F), jnp.int32),
            pltpu.SMEM((1, F), jnp.int32),
            pltpu.VMEM((F, NBLK * B * B), F32),
            pltpu.VMEM((3, F, B * B), F32),
            pltpu.VMEM((3, B * F, W), F32),
            pltpu.VMEM((F, B, W), F32),
            pltpu.VMEM((F, B, W), F32),
            pltpu.VMEM((F, B, W), F32),
            pltpu.VMEM((ITERS + 1, F, W), F32),
            pltpu.VMEM((ITERS, F, W), F32),
            pltpu.VMEM((ITERS, 8, 4, W), F32),
            pltpu.VMEM((ITERS, 8, 4, W), F32),
            pltpu.VMEM((ITERS, 10, 4, W), F32),
            pltpu.VMEM((ITERS, 40, 4, W), F32),
            pltpu.VMEM((5, 8, W), F32),
            pltpu.VMEM((3 * F, W), BF16),
            pltpu.VMEM((8 * F, 2 * W), BF16),
            pltpu.VMEM((3 * F, SEG), F32),
            pltpu.VMEM((8 * F, SEG), F32),
            pltpu.VMEM((F, B * B), F32),
            pltpu.VMEM((2 * F, B * B), BF16),
            pltpu.VMEM((B * B, W), BF16),
            pltpu.VMEM((2 * W, SEG), BF16),
            pltpu.VMEM((2 * W, SEG), BF16),
            pltpu.VMEM((SEG, W), BF16),
            pltpu.VMEM((16, B, W), F32),
            pltpu.VMEM((16, B, W), F32),
            pltpu.VMEM((32, 1, W), F32),
            pltpu.VMEM((8, 1, W), F32),
            dma((11,)),
            dma((ITERS,)),
            dma((ITERS,)),
            dma((ITERS,)),
            dma((ITERS,)),
            dma((ITERS,)),
            dma((4,)),
            dma((4,)),
            dma((1,)),
            dma((1,)),
            dma((1,)),
            dma((1,)),
        ],
        compiler_params=pltpu.CompilerParams(
            collective_id=0, has_side_effects=True, vmem_limit_bytes=48 * 1024 * 1024
        ),
    )(
        *(
            pltpu.with_memory_space_constraint(given, pltpu.HBM)
            for given in (rhs.T, blocks, columns, line_slot, line_lower, line_upper, pivot_inv)
        )
    )
    return both[0].T, both[1].T


def solution(mesh):
    return jax.shard_map(
        on_device,
        mesh=mesh,
        in_specs=(
            P(None, ("span", "plane")),
            P(("span", "plane"), None),
            P(None, ("span", "plane")),
            P(("span", "plane"), None),
            P(("span", "plane"), None),
            P(("span", "plane"), None),
            P(("span", "plane"), None),
        ),
        out_specs=(P(None, ("span", "plane")), P(None, ("span", "plane"))),
        check_vma=False,
    )
```

```python
import functools

import jax
import jax.numpy as jnp
from jax import lax
from jax.experimental import pallas as pl
from jax.experimental.pallas import tpu as pltpu
from jax.sharding import PartitionSpec as P

MESH = pl.DeviceIdType.MESH
F32 = jnp.float32
BF16 = jnp.bfloat16

B = 80
NBLK = 11
ITERS = 3
F = 32
W = 128
SEG = 640
NGRP = 10
EARLY = (0, 3, 4)
LATE = (1, 2, 5, 6, 7, 8, 9, 10)
PAIRS = [(i, j) for i in range(4) for j in range(i, 4)]


def iota(shape, axis):
    return lax.broadcasted_iota(jnp.int32, shape, axis)


def split(x):
    hi = x.astype(BF16)
    lo = (x - hi.astype(F32)).astype(BF16)
    return hi, lo


def bdot(a, b):
    return jnp.dot(a, b, preferred_element_type=F32)


def pad_lanes(x):
    return jnp.concatenate([x, jnp.zeros((x.shape[0], W - x.shape[1]), x.dtype)], axis=1)


def add_rows(x):
    x = x[:40] + x[40:]
    last = x[32:]
    x = x[:16] + x[16:32]
    return jnp.sum((x[:8] + x[8:]) + last, axis=0, keepdims=True)


def add_lanes(x):
    return jnp.sum(x, axis=1, keepdims=True)


def small_solve(factor, target):
    extent = len(target)
    forward_vals = []
    for row in range(extent):
        running = target[row]
        for inner in range(row):
            running = running - factor[row][inner] * forward_vals[inner]
        forward_vals.append(running * factor[row][row])
    backward_vals = [None] * extent
    for row in reversed(range(extent)):
        running = forward_vals[row]
        for inner in range(row + 1, extent):
            running = running - factor[inner][row] * backward_vals[inner]
        backward_vals[row] = running * factor[row][row]
    return backward_vals


def coefficients(gram):
    def inner(c, d):
        out = None
        for i in range(len(c)):
            for j in range(len(d)):
                term = c[i] * d[j] * gram[min(i, j), max(i, j)]
                out = term if out is None else out + term
        return out

    square = gram[0, 0] + 1e-6
    scale = lax.rsqrt(square)
    beta = square * scale
    zero = jnp.zeros_like(beta)
    basis = [[scale]]
    h = [[zero] * ITERS for _ in range(ITERS + 1)]
    for step in range(ITERS):
        w = [zero] + basis[step]
        for i in range(step + 1):
            h[i][step] = inner(basis[i], w)
        for i in range(step + 1):
            for n, c in enumerate(basis[i]):
                w[n] = w[n] - h[i][step] * c
        square = jnp.maximum(inner(w, w), 0.0) + 1e-6
        scale = lax.rsqrt(square)
        h[step + 1][step] = square * scale
        basis.append([c * scale for c in w])
    normal = [
        [sum(h[n][i] * h[n][j] for n in range(min(i, j) + 2)) for j in range(ITERS)]
        for i in range(ITERS)
    ]
    target = [beta * h[0][j] for j in range(ITERS)]
    factor = [[None] * ITERS for _ in range(ITERS)]
    for j in range(ITERS):
        diag = normal[j][j]
        for n in range(j):
            diag = diag - factor[j][n] * factor[j][n]
        factor[j][j] = lax.rsqrt(diag)
        for i in range(j + 1, ITERS):
            below = normal[i][j]
            for n in range(j):
                below = below - factor[i][n] * factor[j][n]
            factor[i][j] = below * factor[j][j]
    y = small_solve(factor, target)
    out = []
    for n in range(ITERS):
        out.append(sum(y[j] * basis[j][n] for j in range(n, ITERS)))
    return out


def kernel(
    rhs_hbm, blocks_hbm, columns_hbm, slot_hbm, low_hbm, upp_hbm, piv_hbm,
    both_ref,
    rhs_ref, columns_ref, slot_ref, slot_smem, blk, flat, tall, lm, pm, pum, kf, zf, rsend, rrecv, zsend, trecv, gid, early_hot, late_hot, xe, xl, acc, acc2, sfull,
    thi, tlo, smat, cm, dm, ga, gb,
    load_sem, rsend_sem, rrecv_sem, zsend_sem, tplane_sem, tspan_sem, gsend_sem, grecv_sem,
    gas_sem, gar_sem, gbs_sem, gbr_sem,
):
    nspan, nplane = 32, 8
    s = lax.axis_index("span")
    p = lax.axis_index("plane")
    x, z = s // 8, s % 8
    s_next, s_prev = lax.rem(s + 1, nspan), lax.rem(s + nspan - 1, nspan)
    p_next, p_prev = lax.rem(p + 1, nplane), lax.rem(p + nplane - 1, nplane)

    peers = [lax.rem(p + i, nplane) for i in range(nplane)]

    def plane_at(i):
        return peers[i]

    small = []
    for n, (src, dst) in enumerate(
        (
            (rhs_hbm, rhs_ref), (slot_hbm, slot_smem), (slot_hbm, slot_ref),
            (columns_hbm, columns_ref),
        )
    ):
        small.append(pltpu.make_async_copy(src, dst, load_sem.at[7 + n]))
        small[-1].start()
    loads = []
    for n, src in enumerate((low_hbm, piv_hbm, upp_hbm)):
        loads.append(pltpu.make_async_copy(src, flat.at[n], load_sem.at[n]))
    for n in range(4):
        loads.append(
            pltpu.make_async_copy(
                blocks_hbm.at[pl.ds(8 * n, 8)], blk.at[pl.ds(8 * n, 8)], load_sem.at[3 + n]
            )
        )
    for load in loads[:3]:
        load.start()

    barrier = pltpu.get_barrier_semaphore()

    def near(dx, dz):
        return lax.rem(x + dx, 4) * 8 + lax.rem(z + dz, 8)

    def greet(device):
        pl.semaphore_signal(barrier, inc=1, device_id=device, device_id_type=MESH)

    far = (4, 3, 5, 2, 6, 1, 7, 0)
    first = [(near(i, 0), plane_at(n)) for i in (2, 1, 3, 0) for n in far if i or n]
    second = [(near(0, i), p) for i in far[:7]]
    for device in first[24:] + first[7:24:8] + second + [(s_next, p), (s_prev, p)]:
        greet(device)

    for n in range(3):
        small[n].wait()
    k0 = pad_lanes(rhs_ref[...])
    kf[0] = k0

    lane = iota((1, W), 1)
    def to_slots(it):
        for t in range(F):
            rsend[it, t // 4, pl.ds(t % 4, 1), :] = kf[it, pl.ds(slot_smem[0, t], 1), :]

    to_slots(0)
    mine = pad_lanes(slot_ref[...].astype(F32)) + ((s * nplane + p) * F).astype(F32)
    gid[0] = jnp.broadcast_to(mine, (8, W))

    def send_pieces(it):
        for i in far[:7]:
            to = plane_at(i)
            pltpu.make_async_remote_copy(
                src_ref=rsend.at[it, to], dst_ref=rrecv.at[it, p],
                send_sem=rsend_sem.at[it], recv_sem=rrecv_sem.at[it],
                device_id=(s, to), device_id_type=MESH,
            ).start()
        pltpu.make_async_copy(rsend.at[it, p], rrecv.at[it, p], rrecv_sem.at[it]).start()

    for n in range(3):
        loads[n].wait()
    for load in loads[3:]:
        load.start()

    def relayout(g, _):
        for n in range(3):
            first_lane = pl.multiple_of(g * SEG, W)
            tiles = [flat[n, :, pl.ds(first_lane + v * W, W)] for v in range(5)]
            for a in range(8):
                tile, at = a * B // W, a * B % W
                row = tiles[tile]
                if at > W - B:
                    row = jnp.where(lane < at, tiles[tile + 1], row)
                if at:
                    row = pltpu.roll(row, W - at, 1)
                tall[n, pl.ds(pl.multiple_of((g * 8 + a) * F, F), F), :] = row
        return 0

    lax.fori_loop(0, NGRP, relayout, 0)

    pl.semaphore_wait(barrier, 19)
    send_pieces(0)
    gid_copies = []
    for n, to in enumerate(((s, p_next), (s, p_prev), (s_next, p), (s_prev, p))):
        copy = pltpu.make_async_remote_copy(
            src_ref=gid.at[0], dst_ref=gid.at[n + 1],
            send_sem=gsend_sem.at[n], recv_sem=grecv_sem.at[n],
            device_id=to, device_id_type=MESH,
        )
        copy.start()
        gid_copies.append(copy)

    zeros48 = jnp.zeros((W - B, W), F32)

    def flip(m):
        return jnp.transpose(jnp.concatenate([m, zeros48], axis=0))[:B]

    def product(a, b):
        ah, al = split(a[:, :B])
        bh, bl = split(b)
        part = bdot(jnp.concatenate([ah, al], axis=0), jnp.concatenate([bh, bl], axis=1))
        return part[:B, :W] + (part[:B, W:] + part[B:, :W])

    def prepare(c, _):
        for n in range(8):
            row = 8 * c + n

            def matrix(which):
                return tall[which, pl.ds(row, B, stride=F), :]

            low, piv, upp = matrix(0), matrix(1), matrix(2)
            both = product(piv, upp)
            if n % 2 == 0:
                lm[row], pm[row], pum[row] = flip(low), piv, both
            else:
                lm[row], pm[row], pum[row] = low, flip(piv), flip(both)
        return 0

    lax.fori_loop(0, F // 8, prepare, 0)

    for it in range(ITERS):
        zsend[it, 0] = jnp.zeros((4, W), F32)
        zsend[it, nplane + 1] = jnp.zeros((4, W), F32)
    thi[...] = jnp.zeros_like(thi)
    tlo[...] = jnp.zeros_like(tlo)

    def carried():
        def step(i, cs, ds, odd):
            new_c, new_d = [], []
            for m in range(2):
                low = tall[0, pl.ds(m * 16 + 8 + i, B, stride=F), :]
                c = -product(low, cs[m])
                upp = pum[m * 16 + 7 - i]
                d = -product(upp if odd else flip(upp), ds[m])
                cm[m * 8 + i] = c if odd else flip(c)
                dm[m * 8 + 7 - i] = d if odd else flip(d)
                new_c.append(c)
                new_d.append(d)
            return new_c, new_d

        def two(n, carry):
            cs, ds = step(2 * n + 1, *carry, True)
            return step(2 * n + 2, cs, ds, False)

        cs = [-tall[0, pl.ds(m * 16 + 8, B, stride=F), :] for m in range(2)]
        ds = [-flip(pum[m * 16 + 7]) for m in range(2)]
        cs, ds = lax.fori_loop(0, 3, two, (cs, ds))
        step(7, cs, ds, True)

    def set_up():
        for copy in gid_copies:
            copy.wait()
        below = jnp.where(p == 0, -1.0, gid[1])
        above = jnp.where(p == nplane - 1, -1.0, gid[2])
        rows = [below[0:1], gid[0][0:1], above[0:1], gid[3][0:1], gid[4][0:1]]
        stacked = jnp.concatenate(rows + [jnp.zeros((W - 5, W), F32)], axis=0)
        by_slot = jnp.transpose(stacked)[:F]
        n_at = iota((1, 2 * W), 1)
        blk_at = n_at // 4
        span_part = n_at >= 96
        dir_at = jnp.where(span_part, 3 + (blk_at - 24) // 8, blk_at % 3)
        slot_at = jnp.where(span_part, (n_at - 96) % F, (blk_at // 3) * 4 + n_at % 4)
        want = iota((F, 2 * W), 0) == slot_at
        numbers = jnp.zeros((F, 2 * W), F32)
        for d in range(5):
            numbers = numbers + jnp.where(want & (dir_at == d), by_slot[:, d : d + 1], 0.0)
        numbers = jnp.sum(numbers, axis=0, keepdims=True)
        numbers = jnp.where(iota((1, 2 * W), 1) < 160, numbers, -2.0)
        small[3].wait()
        cols = jnp.transpose(
            jnp.concatenate(
                [pad_lanes(columns_ref[...].astype(F32)), jnp.zeros((W - NBLK, W), F32)], axis=0
            )
        )[:F]
        for n, k in enumerate(EARLY):
            early_hot[pl.ds(n * F, F), :] = (cols[:, k : k + 1] == numbers[:, :W]).astype(BF16)
        for n, k in enumerate(LATE):
            late_hot[pl.ds(n * F, F), :] = (cols[:, k : k + 1] == numbers).astype(BF16)
        for n in range(4):
            loads[3 + n].wait()
        start = iota((SEG, W), 1) * B - iota((SEG, W), 0)

        def ones(n, _):
            ahead = start - n * SEG
            sfull[pl.ds(pl.multiple_of(n * SEG, SEG), SEG), :] = jnp.where(
                (ahead <= 0) & (ahead > -B), 1.0, 0.0
            ).astype(BF16)
            return 0

        lax.fori_loop(0, NGRP, ones, 0)

    def widen(it, start, count):
        got = trecv[it, pl.ds(start, count)].reshape(4 * count, W)[:, :B]
        hi, lo = split(jnp.concatenate([got] * 8, axis=1))
        thi[pl.ds(4 * start, 4 * count), :] = hi
        tlo[pl.ds(4 * start, 4 * count), :] = lo

    def weigh(row, half, which, picked, total):
        at = pl.ds(row, 8)
        for n, k in enumerate(which):
            term = blk[at, pl.ds(k * 6400 + half * 3200, 3200)] * jnp.concatenate(
                [picked[pl.ds(n * F + row, 8), :]] * 5, axis=1
            )
            total = term if total is None else total + term
        return total

    def one(it, _):
        pltpu.make_async_copy(rrecv.at[it], rrecv.at[it], rrecv_sem.at[it]).wait()
        diag = iota((B, W), 0) == iota((B, W), 1)

        def to_lanes(column):
            return add_rows(jnp.where(diag, column, 0.0))

        @pl.when(it == 0)
        def plain():
            ys = [[], []]
            for j in range(16):
                for m in range(2):
                    row = m * 16 + j
                    if j == 0:
                        ys[m].append(rrecv[it, 0, pl.ds(2 * m, 1), :])
                    elif j % 2:
                        base = jnp.where(diag, rrecv[it, j // 2, pl.ds(2 * m + 1, 1), :], 0.0)
                        ys[m].append(
                            add_lanes(base - lm[row] * ys[m][j - 1])
                        )
                    else:
                        r = rrecv[it, j // 2, pl.ds(2 * m, 1), :]
                        ys[m].append(r - add_rows(lm[row] * ys[m][j - 1]))
            zs = [None, None]
            for j in reversed(range(16)):
                for m in range(2):
                    row = m * 16 + j
                    term = pm[row] * ys[m][j]
                    if j < 15:
                        term = term - pum[row] * zs[m]
                    zs[m] = add_lanes(term) if j % 2 == 0 else add_rows(term)
                    if j % 2:
                        zsend[it, j // 2 + 1, pl.ds(2 * m + 1, 1), :] = zs[m]
                    else:
                        zsend[it, j // 2 + 1, pl.ds(2 * m, 1), :] = to_lanes(zs[m])

        @pl.when(it > 0)
        def halves():
            ys = [[None] * 16 for _ in range(2)]
            for i in range(8):
                for j in (i, 8 + i):
                    for m in range(2):
                        row = m * 16 + j
                        if j % 2:
                            base = jnp.where(diag, rrecv[it, j // 2, pl.ds(2 * m + 1, 1), :], 0.0)
                            ys[m][j] = add_lanes(base - lm[row] * ys[m][j - 1])
                        else:
                            ys[m][j] = rrecv[it, j // 2, pl.ds(2 * m, 1), :]
                            if i:
                                ys[m][j] = ys[m][j] - add_rows(lm[row] * ys[m][j - 1])
            for m in range(2):
                column = ys[m][7]
                across = to_lanes(column)
                ys[m][8] = ys[m][8] - add_rows(lm[m * 16 + 8] * column)
                for i in range(1, 8):
                    if i % 2:
                        more = add_lanes(cm[m * 8 + i] * across)
                    else:
                        more = add_rows(cm[m * 8 + i] * column)
                    ys[m][8 + i] = ys[m][8 + i] + more
            zs = [[None] * 16 for _ in range(2)]
            for i in range(8):
                for j in (15 - i, 7 - i):
                    for m in range(2):
                        term = pm[m * 16 + j] * ys[m][j]
                        if i:
                            term = term - pum[m * 16 + j] * zs[m][j + 1]
                        zs[m][j] = add_lanes(term) if j % 2 == 0 else add_rows(term)
            for m in range(2):
                column = zs[m][8]
                across = to_lanes(column)
                for j in range(8):
                    if j == 7:
                        more = -add_rows(pum[m * 16 + 7] * column)
                    elif j % 2:
                        more = add_rows(dm[m * 8 + j] * column)
                    else:
                        more = add_lanes(dm[m * 8 + j] * across)
                    zs[m][j] = zs[m][j] + more
                for j in range(16):
                    if j % 2:
                        zsend[it, j // 2 + 1, pl.ds(2 * m + 1, 1), :] = zs[m][j]
                    else:
                        zsend[it, j // 2 + 1, pl.ds(2 * m, 1), :] = to_lanes(zs[m][j])

        for i in far:
            to = plane_at(i)
            for n, there in enumerate((s_next, s_prev)):
                pltpu.make_async_remote_copy(
                    src_ref=zsend.at[it, to + 1], dst_ref=trecv.at[it, 24 + 8 * n + p],
                    send_sem=zsend_sem.at[it], recv_sem=tspan_sem.at[it],
                    device_id=(there, to), device_id_type=MESH,
                ).start()
        for i in far[:7]:
            to = plane_at(i)
            pltpu.make_async_remote_copy(
                src_ref=zsend.at[it, pl.ds(to, 3)], dst_ref=trecv.at[it, pl.ds(3 * p, 3)],
                send_sem=zsend_sem.at[it], recv_sem=tplane_sem.at[it],
                device_id=(s, to), device_id_type=MESH,
            ).start()
        pltpu.make_async_copy(
            zsend.at[it, pl.ds(p, 3)], trecv.at[it, pl.ds(3 * p, 3)], tplane_sem.at[it]
        ).start()

        @pl.when(it == 0)
        def _():
            set_up()
            carried()

        part = trecv.at[it, pl.ds(0, 24)]
        pltpu.make_async_copy(part, part, tplane_sem.at[it]).wait()
        widen(it, 0, 24)
        hot = early_hot[...]
        xe[...] = bdot(hot, thi[pl.ds(0, W), :]) + bdot(hot, tlo[pl.ds(0, W), :])
        zf[it] = xe[pl.ds(0, F), pl.ds(0, W)]

        for row in range(0, F, 8):
            for half in range(2):
                acc[pl.ds(row, 8), pl.ds(half * 3200, 3200)] = weigh(row, half, EARLY, xe, None)

        part = trecv.at[it, pl.ds(24, 16)]
        pltpu.make_async_copy(part, part, tspan_sem.at[it]).wait()
        widen(it, 24, 16)
        hot = late_hot[...]
        for n in range(0, SEG, 2 * W):
            w = min(2 * W, SEG - n)
            xl[:, n : n + w] = bdot(hot, thi[:, n : n + w]) + bdot(hot, tlo[:, n : n + w])

        out = None
        for half in range(2):
            lanes = pl.ds(half * 3200, 3200)
            for row in range(0, F, 16):
                total = jnp.concatenate(
                    [weigh(n, half, LATE, xl, acc[pl.ds(n, 8), lanes]) for n in (row, row + 8)],
                    axis=0,
                )
                hi, lo = split(total)
                acc2[pl.ds(row, 16), lanes] = hi
                acc2[pl.ds(F + row, 16), lanes] = lo
            part = bdot(acc2[:, lanes], sfull[lanes, :])
            out = part if out is None else out + part
        kf[it + 1] = out[:F] + out[F:]

        @pl.when(it < ITERS - 1)
        def _():
            for t in range(F):
                rsend[it + 1, t // 4, pl.ds(t % 4, 1), :] = kf[
                    it + 1, pl.ds(slot_smem[0, t], 1), :
                ]
            send_pieces(it + 1)

        return 0

    lax.fori_loop(0, ITERS, one, 0)

    ks = [kf[i] for i in range(4)]
    tile = jnp.concatenate(
        [jnp.sum(ks[i] * ks[j], axis=0, keepdims=True) for i, j in PAIRS]
        + [jnp.zeros((6, W), F32)],
        axis=0,
    )
    tile = jnp.sum(tile, axis=1, keepdims=True)
    tile = jnp.where(iota((16, W), 0) == iota((16, W), 1), tile, 0.0)
    ga[0] = jnp.sum(tile, axis=0, keepdims=True)
    for i, to in enumerate(first):
        pltpu.make_async_remote_copy(
            src_ref=ga.at[0], dst_ref=ga.at[i + 1],
            send_sem=gas_sem.at[0], recv_sem=gar_sem.at[0],
            device_id=to, device_id_type=MESH,
        ).start()
    arrived = ga.at[pl.ds(1, 31)]
    pltpu.make_async_copy(arrived, arrived, gar_sem.at[0]).wait()
    gb[0] = jnp.sum(ga[...], axis=0)
    for i, to in enumerate(second):
        pltpu.make_async_remote_copy(
            src_ref=gb.at[0], dst_ref=gb.at[i + 1],
            send_sem=gbs_sem.at[0], recv_sem=gbr_sem.at[0],
            device_id=to, device_id_type=MESH,
        ).start()
    arrived_b = gb.at[pl.ds(1, 7)]
    pltpu.make_async_copy(arrived_b, arrived_b, gbr_sem.at[0]).wait()
    whole = jnp.sum(gb[...], axis=0)
    gram = {
        pair: jnp.broadcast_to(whole[:, n : n + 1], (1, W)) for n, pair in enumerate(PAIRS)
    }
    coef = coefficients(gram)
    solved = sum(coef[i] * zf[i] for i in range(ITERS))
    left = ks[0] - sum(coef[i] * ks[i + 1] for i in range(ITERS))
    both_ref[0] = solved[:, :B]
    both_ref[1] = left[:, :B]

    pltpu.make_async_copy(arrived, arrived, gas_sem.at[0]).wait()
    pltpu.make_async_copy(arrived_b, arrived_b, gbs_sem.at[0]).wait()
    for it in range(ITERS):
        out = rsend.at[it, pl.ds(0, 7)]
        pltpu.make_async_copy(out, out, rsend_sem.at[it]).wait()
        out = trecv.at[it, pl.ds(0, 37)]
        pltpu.make_async_copy(out, out, zsend_sem.at[it]).wait()


def on_device(rhs, blocks, columns, line_slot, line_lower, line_upper, pivot_inv):
    vmem = pl.BlockSpec(memory_space=pltpu.VMEM)
    hbm = pl.BlockSpec(memory_space=pltpu.HBM)
    out = jax.ShapeDtypeStruct((F, B), F32)
    dma = pltpu.SemaphoreType.DMA
    both = pl.pallas_call(
        kernel,
        out_shape=jax.ShapeDtypeStruct((2, F, B), F32),
        in_specs=[hbm] * 7,
        out_specs=vmem,
        scratch_shapes=[
            pltpu.VMEM((F, B), F32),
            pltpu.VMEM((NBLK, F), jnp.int32),
            pltpu.VMEM((1, F), jnp.int32),
            pltpu.SMEM((1, F), jnp.int32),
            pltpu.VMEM((F, NBLK * B * B), F32),
            pltpu.VMEM((3, F, B * B), F32),
            pltpu.VMEM((3, B * F + F, W), F32),
            pltpu.VMEM((F, B, W), F32),
            pltpu.VMEM((F, B, W), F32),
            pltpu.VMEM((F, B, W), F32),
            pltpu.VMEM((ITERS + 1, F, W), F32),
            pltpu.VMEM((ITERS, F, W), F32),
            pltpu.VMEM((ITERS, 8, 4, W), F32),
            pltpu.VMEM((ITERS, 8, 4, W), F32),
            pltpu.VMEM((ITERS, 10, 4, W), F32),
            pltpu.VMEM((ITERS, 40, 4, W), F32),
            pltpu.VMEM((5, 8, W), F32),
            pltpu.VMEM((3 * F, W), BF16),
            pltpu.VMEM((8 * F, 2 * W), BF16),
            pltpu.VMEM((3 * F, SEG), F32),
            pltpu.VMEM((8 * F, SEG), F32),
            pltpu.VMEM((F, B * B), F32),
            pltpu.VMEM((2 * F, B * B), BF16),
            pltpu.VMEM((B * B, W), BF16),
            pltpu.VMEM((2 * W, SEG), BF16),
            pltpu.VMEM((2 * W, SEG), BF16),
            pltpu.VMEM((SEG, W), BF16),
            pltpu.VMEM((16, B, W), F32),
            pltpu.VMEM((16, B, W), F32),
            pltpu.VMEM((32, 1, W), F32),
            pltpu.VMEM((8, 1, W), F32),
            dma((11,)),
            dma((ITERS,)),
            dma((ITERS,)),
            dma((ITERS,)),
            dma((ITERS,)),
            dma((ITERS,)),
            dma((4,)),
            dma((4,)),
            dma((1,)),
            dma((1,)),
            dma((1,)),
            dma((1,)),
        ],
        compiler_params=pltpu.CompilerParams(
            collective_id=0, has_side_effects=True, vmem_limit_bytes=48 * 1024 * 1024
        ),
    )(
        *(
            pltpu.with_memory_space_constraint(given, pltpu.HBM)
            for given in (rhs.T, blocks, columns, line_slot, line_lower, line_upper, pivot_inv)
        )
    )
    return both[0].T, both[1].T


def solution(mesh):
    return jax.shard_map(
        on_device,
        mesh=mesh,
        in_specs=(
            P(None, ("span", "plane")),
            P(("span", "plane"), None),
            P(None, ("span", "plane")),
            P(("span", "plane"), None),
            P(("span", "plane"), None),
            P(("span", "plane"), None),
            P(("span", "plane"), None),
        ),
        out_specs=(P(None, ("span", "plane")), P(None, ("span", "plane"))),
        check_vma=False,
    )
```
